32 devices in a mesh: ctx: 32 (over z, y, x, core), head: 1.
Axes of the slice: x: 2, y: 2, z: 4, core: 2. Of those that a mesh axis runs over, the one named last changes fastest.
Arguments:
- queries: bfloat16 [16384, 4096], P('ctx', 'head'), may hold values from -8 to 8
- keys: bfloat16 [16384, 1024], P('ctx', 'head'), may hold values from -6 to 6
- values: bfloat16 [16384, 1024], P('ctx', 'head'), may hold values from -6 to 6
- vertical_blocks: int32 [8, 8], P('head'), may hold values from 0 to 127, as said below
- slash_offsets: int32 [8, 8], P('head'), may hold values from 0 to 16, as said below
- out_weight: bfloat16 [4096, 4096], P(None, 'head'), may hold values from -0.5 to 0.5
Outputs:
- output: bfloat16 [16384, 4096], P('ctx', 'head')
The draws below stay inside these ranges and needn't reach their ends.
Inputs may be any that keep to these rules, and one draw needn't show every extreme that they name: `vertical_blocks`: within each key-value head the 8 entries are distinct; every head lists block 0, and head 0 lists block 127. `slash_offsets`: within each key-value head the 8 offsets are distinct, and every head holds 0 and 16.
All inputs are finite; a program needn't handle non-finite values.
Results may differ from the reference program's by a relative error of at most 0.0057.
Values may be sent and summed in bfloat16 or wider, within the bound.
No kernel may reach another device: no remote copies, remote signals or barrier semaphores. Data moves between devices by JAX's collectives and lax.ppermute only.
A program may use at most 192 MiB of HBM per device.

```python
import math
import jax
import jax.numpy as jnp
from jax import lax

D = 4096
NH = 32
KVH = 8
HD = 128
BLK = 128
NV = 8
NS = 8
MAXOFF = 16
TOKENS = 16384
NB = 128


def draw_queries(key, part):
    base_key = jax.random.fold_in(key, 1)
    result = jnp.clip(2.0 * jax.random.normal(base_key, (TOKENS, NH * HD), jnp.float32), -8.0, 8.0)
    return result.astype(jnp.bfloat16)


def draw_keys(key, part):
    base_key = jax.random.fold_in(key, 2)
    result = jnp.clip(jax.random.normal(base_key, (TOKENS, KVH * HD), jnp.float32), -6.0, 6.0)
    return result.astype(jnp.bfloat16)


def draw_vertical_blocks(key, part):

    def one_head(head_id):
        shuffled = jax.random.permutation(jax.random.fold_in(key, 100 + head_id), NB - 2) + 1
        return jnp.concatenate([jnp.zeros((1,), jnp.int32), shuffled[:NV - 1].astype(jnp.int32)])
    table = jax.vmap(one_head)(jnp.arange(KVH))
    return table.at[0, 1].set(NB - 1).astype(jnp.int32)


def draw_slash_offsets(key, part):

    def one_head(head_id):
        shuffled = jax.random.permutation(jax.random.fold_in(key, 200 + head_id), MAXOFF - 1) + 1
        fixed = jnp.array([0, MAXOFF], jnp.int32)
        return jnp.concatenate([fixed, shuffled[:NS - 2].astype(jnp.int32)])
    return jax.vmap(one_head)(jnp.arange(KVH)).astype(jnp.int32)


def levels(key, extent, shards, smallest, largest):
    level, own = 1.0, jax.random.fold_in(key, 6)
    for dim, shards_of in shards:
        draws = jnp.exp(jax.random.uniform(jax.random.fold_in(own, dim), (shards_of,), jnp.float32, smallest / len(shards), largest / len(shards)))
        level = level * jnp.repeat(draws, extent[dim] // shards_of).reshape([-1 if axis == dim else 1 for axis in range(len(extent))])
    return level


def normal_values(key, dims, spread, reach, pieces=(), kind=jnp.bfloat16):
    entries = spread * jax.random.normal(key, dims, jnp.float32)
    if pieces:
        entries = entries * levels(key, dims, pieces, -0.22, 0.18)
    return jnp.clip(entries, -reach, reach).astype(kind)


def setup_inputs(seed: int = 0) -> dict:
    key_list = jax.random.split(jax.random.key(seed), 7)
    return {
        "queries": draw_queries(jax.random.fold_in(key_list[6], 71), 0),
        "keys": draw_keys(jax.random.fold_in(key_list[6], 71), 0),
        "values": normal_values(key_list[2], (TOKENS, KVH * HD), 1.0, 6.0, ((0, 32),)),
        "vertical_blocks": draw_vertical_blocks(jax.random.fold_in(key_list[6], 71), 0),
        "slash_offsets": draw_slash_offsets(jax.random.fold_in(key_list[6], 71), 0),
        "out_weight": normal_values(key_list[5], (NH * HD, D), (NH * HD // 32) ** -0.5, 0.5),
    }


def reference(queries, keys, values, vertical_blocks, slash_offsets, out_weight):
    group_size = NH // KVH
    block_count = TOKENS // BLK
    query_blocks = queries.reshape(block_count, BLK, KVH, group_size, HD)
    key_heads = keys.reshape(block_count, BLK, KVH, HD).transpose(2, 0, 1, 3)
    value_heads = values.reshape(block_count, BLK, KVH, HD).transpose(2, 0, 1, 3)
    score_scale = 1.0 / math.sqrt(HD)
    positions = jnp.arange(BLK, dtype=jnp.int32)
    causal = positions[None, :] <= positions[:, None]

    def pick(heads, picks):
        return jnp.take(heads, picks, axis=0)

    def attend(global_block):
        slash_start = global_block - slash_offsets
        repeated = jnp.any(vertical_blocks[:, :, None] == slash_start[:, None, :], 2)
        valid = jnp.concatenate([slash_start >= 0, (vertical_blocks < global_block) & ~repeated], 1)
        diagonal = jnp.concatenate([slash_offsets == 0, jnp.zeros(vertical_blocks.shape, jnp.bool_)], 1)
        chosen = jnp.concatenate([jnp.maximum(slash_start, 0), vertical_blocks], 1).astype(jnp.int32)
        key_sel = jax.vmap(pick)(key_heads, chosen).astype(jnp.float32)
        value_sel = jax.vmap(pick)(value_heads, chosen).astype(jnp.float32)
        rows = query_blocks[global_block].astype(jnp.float32)
        scores = jnp.einsum('rhgd,hjcd->hgrjc', rows, key_sel) * score_scale
        allowed = valid[:, None, None, :, None] & (~diagonal[:, None, None, :, None] | causal[None, None, :, None, :])
        scores = jnp.where(allowed, scores, -1e+30)
        top = lax.optimization_barrier(jnp.max(scores, axis=(3, 4), keepdims=True))
        expo = jnp.exp(scores - top)
        total = lax.optimization_barrier(jnp.sum(expo, axis=(3, 4), keepdims=True))
        weights = (expo / total).astype(jnp.bfloat16)
        return jnp.einsum('hgrjc,hjcd->rhgd', weights.astype(jnp.float32), value_sel).astype(jnp.bfloat16)
    attended = lax.map(attend, jnp.arange(block_count, dtype=jnp.int32)).reshape(TOKENS, NH * HD)
    return jnp.dot(attended, out_weight, preferred_element_type=jnp.float32).astype(jnp.bfloat16)
```

```python
import functools
import math

import jax
import jax.numpy as jnp
from jax import lax
from jax.experimental import pallas as pl
from jax.experimental.pallas import tpu as pltpu
from jax.sharding import PartitionSpec as P

HD = 128
BLK = 128
MAXOFF = 16
MASKED = -1e30
VMEM_LIMIT = 56 * 1024 * 1024


def shifted(value, by, wrap_pairs=None):
    size = lax.axis_size("ctx")
    pairs = wrap_pairs or [(i, i + by) for i in range(size) if 0 <= i + by < size]
    return lax.ppermute(value, "ctx", pairs)


def swapped(value):
    size = lax.axis_size("ctx")
    return lax.ppermute(value, "ctx", [(i, i ^ 1) for i in range(size)])


def pick_kernel(place, k_ref, v_ref, out_ref):
    n_slots = pl.num_programs(1)
    owned = place[1, pl.program_id(0) * n_slots + pl.program_id(1)]
    keep = owned == 1

    @pl.when(keep)
    def _():
        out_ref[:, :HD] = k_ref[...]
        out_ref[:, HD:] = v_ref[...]

    @pl.when(jnp.logical_not(keep))
    def _():
        out_ref[...] = jnp.zeros_like(out_ref)


def pick_vertical(kv_chip, place, heads, slots):
    return pl.pallas_call(
        pick_kernel,
        grid_spec=pltpu.PrefetchScalarGridSpec(
            num_scalar_prefetch=1,
            grid=(heads, slots),
            in_specs=[
                pl.BlockSpec((BLK, HD), lambda e, j, place: (place[0, e * slots + j], e)),
                pl.BlockSpec((BLK, HD), lambda e, j, place: (place[0, e * slots + j], heads + e)),
            ],
            out_specs=pl.BlockSpec((BLK, 2 * HD), lambda e, j, place: (e * slots + j, 0)),
        ),
        out_shape=jax.ShapeDtypeStruct((heads * slots * BLK, 2 * HD), kv_chip.dtype),
        name="pick_vertical",
    )(place, kv_chip, kv_chip)


def attend_kernel(cfg, info, vert, slash, *refs):
    pair, local, group, reach, n_slash, n_vert = cfg
    q_refs, refs = refs[:pair], refs[pair:]
    k_refs, v_refs, refs = refs[: reach + 1], refs[reach + 1 : 2 * reach + 2], refs[2 * reach + 2 :]
    kv_vert, masks, refs = refs[0], refs[1], refs[2:]
    out_refs, refs = refs[:pair], refs[pair:]
    kwin, vwin, kg, vg, qx, sc = refs
    e = pl.program_id(0)
    chip, core = info[0], info[1]
    dev_rows = local * BLK
    chip_blocks = pair * local
    chip_rows = chip_blocks * BLK
    width = (n_slash + n_vert) * BLK
    step = min(2 * BLK, width)
    factor = math.log2(math.e) / math.sqrt(HD)

    for back in range(reach + 1):
        for slot in range(pair):
            owner = core ^ slot if pair > 1 else 0
            at = pl.multiple_of((reach - back) * chip_rows + owner * dev_rows, dev_rows)
            rows = slice(slot * dev_rows, (slot + 1) * dev_rows)
            kwin[pl.ds(at, dev_rows), :] = k_refs[back][rows, :]
            vwin[pl.ds(at, dev_rows), :] = v_refs[back][rows, :]
    kg[n_slash * BLK :, :HD] = kv_vert[:, :HD]
    vg[n_slash * BLK :, :HD] = kv_vert[:, HD:]
    vg[:, HD:] = jnp.ones((width, HD), vg.dtype)
    row = lax.broadcasted_iota(jnp.int32, (BLK, HD), 0)
    col = lax.broadcasted_iota(jnp.int32, (BLK, HD), 1)
    eye = jnp.where(row == col, 1.0, 0.0).astype(qx.dtype)
    for g in range(group):
        qx[g * BLK : (g + 1) * BLK, HD:] = eye

    for slot in range(pair):

        def one_block(b, carry, slot=slot):
            rel = (core ^ slot if pair > 1 else 0) * local + b
            here = chip * chip_blocks + rel
            starts = [here - slash[e, j] for j in range(n_slash)]
            for j in range(n_slash):
                off = slash[e, j]
                src = pl.multiple_of((reach * chip_blocks + rel - off) * BLK, BLK)
                rows = slice(j * BLK, (j + 1) * BLK)
                kg[rows, :HD] = kwin[pl.ds(src, BLK), :]
                vg[rows, :HD] = vwin[pl.ds(src, BLK), :]
                kind = jnp.where(starts[j] < 0, 2, jnp.where(off == 0, 1, 0))
                kg[rows, HD:] = masks[kind]
            for j in range(n_vert):
                block = vert[e, j]
                hidden = block >= here
                for start in starts:
                    hidden = hidden | (block == start)
                rows = slice((n_slash + j) * BLK, (n_slash + j + 1) * BLK)
                kg[rows, HD:] = masks[jnp.where(hidden, 2, 0)]
            q_rows = pl.ds(pl.multiple_of(b * BLK, BLK), BLK)
            for g in range(group):
                qx[g * BLK : (g + 1) * BLK, :HD] = q_refs[slot][q_rows, g * HD : (g + 1) * HD]
            top = None
            for t in range(0, width, step):
                s = lax.dot_general(
                    qx[...], kg[t : t + step, :], (((1,), (1,)), ((), ())),
                    preferred_element_type=jnp.float32,
                )
                sc[:, t : t + step] = s
                for u in range(0, step, HD):
                    piece = s[:, u : u + HD]
                    top = piece if top is None else jnp.maximum(top, piece)
            top = jnp.max(top, axis=1, keepdims=True)
            acc = None
            for t in range(0, width, step):
                p = jnp.exp2((sc[:, t : t + step] - top) * factor).astype(vg.dtype)
                o = jnp.dot(p, vg[t : t + step, :], preferred_element_type=jnp.float32)
                acc = o if acc is None else acc + o
            res = (acc[:, :HD] / acc[:, HD:]).astype(out_refs[slot].dtype)
            for g in range(group):
                out_refs[slot][q_rows, g * HD : (g + 1) * HD] = res[g * BLK : (g + 1) * BLK]
            return carry

        lax.fori_loop(0, local, one_block, 0)


def attend(qs, windows, kv_vert, vert, slash, info, heads, local):
    pair, reach = len(qs), len(windows) - 1
    dev_rows = qs[0].shape[0]
    group = qs[0].shape[1] // (heads * HD)
    n_slash, n_vert = slash.shape[1], vert.shape[1]
    width = (n_slash + n_vert) * BLK
    win_rows = sum(w.shape[0] for w in windows)
    dtype = qs[0].dtype
    pos = jnp.arange(BLK)
    causal = jnp.where(pos[:, None] > pos[None, :], MASKED, 0.0)
    masks = jnp.stack([jnp.zeros_like(causal), causal, jnp.full_like(causal, MASKED)]).astype(dtype)
    smem = pl.BlockSpec(memory_space=pltpu.SMEM)
    head_cols = pl.BlockSpec((dev_rows, group * HD), lambda e: (0, e))
    rows = heads * pair * local * group * BLK
    return pl.pallas_call(
        functools.partial(attend_kernel, (pair, local, group, reach, n_slash, n_vert)),
        grid=(heads,),
        in_specs=[smem] * 3
        + [head_cols] * pair
        + [pl.BlockSpec((w.shape[0], HD), lambda e: (0, e)) for w in windows]
        + [pl.BlockSpec((w.shape[0], HD), lambda e: (0, heads + e)) for w in windows]
        + [
            pl.BlockSpec((n_vert * BLK, 2 * HD), lambda e: (e, 0)),
            pl.BlockSpec((3, BLK, BLK), lambda e: (0, 0, 0)),
        ],
        out_specs=[head_cols] * pair,
        out_shape=[jax.ShapeDtypeStruct(q.shape, dtype) for q in qs],
        scratch_shapes=[
            pltpu.VMEM((win_rows, HD), dtype),
            pltpu.VMEM((win_rows, HD), dtype),
            pltpu.VMEM((width, 2 * HD), dtype),
            pltpu.VMEM((width, 2 * HD), dtype),
            pltpu.VMEM((group * BLK, 2 * HD), dtype),
            pltpu.VMEM((group * BLK, width), jnp.float32),
        ],
        compiler_params=pltpu.CompilerParams(vmem_limit_bytes=VMEM_LIMIT),
        cost_estimate=pl.CostEstimate(
            flops=8 * rows * width * HD,
            bytes_accessed=2 * (2 * win_rows * HD * heads + 2 * rows * HD),
            transcendentals=rows * width,
        ),
        name="attend",
    )(info, vert, slash, *qs, *windows, *windows, kv_vert, masks)


def body(queries, keys, values, vertical_blocks, slash_offsets, out_weight):
    tokens_dev = queries.shape[0]
    kv_heads = keys.shape[1] // HD
    local = tokens_dev // BLK
    size = lax.axis_size("ctx")
    pair = 2 if kv_heads % 2 == 0 and size % 2 == 0 else 1
    heads = kv_heads // pair
    chip_blocks = pair * local
    reach = -(-MAXOFF // chip_blocks)
    index = lax.axis_index("ctx")
    chip, core = index // pair, index % pair

    def mine(value, axis):
        span = value.shape[axis] // pair
        return lax.dynamic_slice_in_dim(value, core * span, span, axis)

    def theirs(value, axis):
        span = value.shape[axis] // pair
        return lax.dynamic_slice_in_dim(value, (1 - core) * span, span, axis)

    if pair == 2:
        kv_mine = jnp.concatenate([mine(keys, 1), mine(values, 1)], 1)
        kv_other = swapped(jnp.concatenate([theirs(keys, 1), theirs(values, 1)], 1))
        kv_chip = jnp.concatenate([kv_mine, kv_other], 0)
    else:
        kv_chip = jnp.concatenate([keys, values], 1)
    windows = [kv_chip] + [shifted(kv_chip, pair * d) for d in range(1, reach + 1)]
    if pair == 2:
        qs = [mine(queries, 1), swapped(theirs(queries, 1))]
    else:
        qs = [queries]
    vert, slash = mine(vertical_blocks, 0), mine(slash_offsets, 0)

    within = vert % chip_blocks
    if pair == 2:
        within = (within // local ^ core) * local + within % local
    owned = (vert // chip_blocks == chip).astype(jnp.int32)
    place = jnp.stack([within.reshape(-1), owned.reshape(-1)]).astype(jnp.int32)
    listed = pick_vertical(kv_chip, place, heads, vert.shape[1])
    groups = [list(range(c, size, pair)) for c in range(pair)]
    share = lax.psum_scatter(
        listed, "ctx", scatter_dimension=0, axis_index_groups=groups, tiled=True
    )
    kv_vert = lax.all_gather(share, "ctx", axis=0, axis_index_groups=groups, tiled=True)

    info = jnp.stack([chip, core]).astype(jnp.int32)
    att = attend(qs, windows, kv_vert, vert, slash, info, heads, local)
    if pair == 2:
        own, other = att[0], swapped(att[1])
        low, high = jnp.where(core == 0, own, other), jnp.where(core == 0, other, own)
        attended = jnp.concatenate([low, high], 1)
    else:
        attended = att[0]
    output = jnp.dot(
        lax.all_gather(attended, "head", axis=1, tiled=True),
        out_weight,
        preferred_element_type=jnp.float32,
    )
    return output.astype(jnp.bfloat16)


def solution(mesh):
    placed = (
        P("ctx", "head"),
        P("ctx", "head"),
        P("ctx", "head"),
        P("head", None),
        P("head", None),
        P(None, "head"),
    )
    return jax.shard_map(
        body, mesh=mesh, in_specs=placed, out_specs=P("ctx", "head"), check_vma=False
    )
```

```python
import functools
import math

import jax
import jax.numpy as jnp
from jax import lax
from jax.experimental import pallas as pl
from jax.experimental.pallas import tpu as pltpu
from jax.sharding import PartitionSpec as P

HD = 128
BLK = 128
MAXOFF = 16
PLANE = 4
MASKED = -1e30
VMEM_LIMIT = 56 * 1024 * 1024


def shifted(value, by):
    size = lax.axis_size("ctx")
    return lax.ppermute(value, "ctx", [(i, i + by) for i in range(size - by)])


def crossed(value, bits):
    size = lax.axis_size("ctx")
    return lax.ppermute(value, "ctx", [(i, i ^ bits) for i in range(size)])


def prepare_kernel(cfg, info, vert, *refs):
    pair, local, heads, plane = cfg
    chip, core = info[0], info[1]
    keys, values = refs[:2]
    refs = refs[2:]
    other = None
    if pair > 1:
        other, refs = refs[0], refs[1:]
    chip_outs, refs = refs[:heads], refs[heads:]
    list_outs, chip_kv = refs[:plane], refs[plane]
    n_vert = vert.shape[1]
    dev_rows = local * BLK
    chip_blocks = pair * local
    for e in range(heads):
        at = pl.multiple_of((core * heads + e) * HD, HD)
        chip_kv[e, :dev_rows, :HD] = keys[:, pl.ds(at, HD)]
        chip_kv[e, :dev_rows, HD:] = values[:, pl.ds(at, HD)]
        if pair > 1:
            chip_kv[e, dev_rows:, :HD] = other[:, e * HD : (e + 1) * HD]
            chip_kv[e, dev_rows:, HD:] = other[:, (heads + e) * HD : (heads + e + 1) * HD]
        chip_outs[e][...] = chip_kv[e]
    per = heads * n_vert // plane
    for k in range(plane):
        for i in range(per):
            flat = (chip % plane ^ k) * per + i
            e, j = flat // n_vert, flat % n_vert
            block = vert[e, j]
            within = block % chip_blocks
            if pair > 1:
                within = (within // local ^ core) * local + within % local
            rows = slice(i * BLK, (i + 1) * BLK)
            owned = block // chip_blocks == chip
            found = chip_kv[e, pl.ds(pl.multiple_of(within * BLK, BLK), BLK), :]
            list_outs[k][rows, :] = jnp.where(owned, found, jnp.zeros_like(found))


def prepare(info, vert, keys, values, other, heads, local, plane):
    pair = 1 if other is None else 2
    chip_rows = pair * local * BLK
    per = heads * vert.shape[1] // plane
    dtype = keys.dtype
    smem = pl.BlockSpec(memory_space=pltpu.SMEM)
    vmem = pl.BlockSpec(memory_space=pltpu.VMEM)
    data = [keys, values] + ([] if other is None else [other])
    outs = pl.pallas_call(
        functools.partial(prepare_kernel, (pair, local, heads, plane)),
        in_specs=[smem] * 2 + [vmem] * len(data),
        out_specs=[vmem] * (heads + plane),
        out_shape=[jax.ShapeDtypeStruct((chip_rows, 2 * HD), dtype)] * heads
        + [jax.ShapeDtypeStruct((per * BLK, 2 * HD), dtype)] * plane,
        scratch_shapes=[pltpu.VMEM((heads, chip_rows, 2 * HD), dtype)],
        compiler_params=pltpu.CompilerParams(vmem_limit_bytes=VMEM_LIMIT),
        cost_estimate=pl.CostEstimate(
            flops=0, bytes_accessed=8 * heads * chip_rows * 2 * HD, transcendentals=0
        ),
        name="prepare",
    )(info, vert, *data)
    return outs[:heads], outs[heads:]


def attend_kernel(cfg, info, vert, slash, *refs):
    e, pair, local, group, reach, n_slash, n_vert, plane, heads = cfg
    q_refs, refs = refs[:pair], refs[pair:]
    w_refs, refs = refs[: reach + 1], refs[reach + 1 :]
    kv_vert, masks, refs = refs[0], refs[1], refs[2:]
    out_refs, refs = refs[:pair], refs[pair:]
    win, kg, vg, qx, sc = refs
    chip, core = info[0], info[1]
    dev_rows = local * BLK
    chip_blocks = pair * local
    chip_rows = chip_blocks * BLK
    width = (n_slash + n_vert) * BLK
    step = min(2 * BLK, width)
    factor = math.log2(math.e) / math.sqrt(HD)

    for back in range(reach + 1):
        for slot in range(pair):
            owner = core ^ slot if pair > 1 else 0
            at = pl.multiple_of((reach - back) * chip_rows + owner * dev_rows, dev_rows)
            win[pl.ds(at, dev_rows), :] = w_refs[back][slot * dev_rows : (slot + 1) * dev_rows, :]
    per = heads * n_vert // plane
    for j in range(n_vert):
        part, place = divmod(e * n_vert + j, per)
        src = pl.multiple_of(((part ^ chip % plane) * per + place) * BLK, BLK)
        rows = slice((n_slash + j) * BLK, (n_slash + j + 1) * BLK)
        kg[rows, :HD] = kv_vert[pl.ds(src, BLK), :HD]
        vg[rows, :HD] = kv_vert[pl.ds(src, BLK), HD:]
    vg[:, HD:] = jnp.ones((width, HD), vg.dtype)
    row = lax.broadcasted_iota(jnp.int32, (BLK, HD), 0)
    col = lax.broadcasted_iota(jnp.int32, (BLK, HD), 1)
    eye = jnp.where(row == col, 1.0, 0.0).astype(qx.dtype)
    for g in range(group):
        qx[g * BLK : (g + 1) * BLK, HD:] = eye

    for slot in range(pair):

        def one_block(b, carry, slot=slot):
            rel = (core ^ slot if pair > 1 else 0) * local + b
            here = chip * chip_blocks + rel
            starts = [here - slash[e, j] for j in range(n_slash)]
            for j in range(n_slash):
                off = slash[e, j]
                src = pl.multiple_of((reach * chip_blocks + rel - off) * BLK, BLK)
                rows = slice(j * BLK, (j + 1) * BLK)
                kg[rows, :HD] = win[pl.ds(src, BLK), :HD]
                vg[rows, :HD] = win[pl.ds(src, BLK), HD:]
                kind = jnp.where(starts[j] < 0, 2, jnp.where(off == 0, 1, 0))
                kg[rows, HD:] = masks[kind]
            for j in range(n_vert):
                block = vert[e, j]
                hidden = block >= here
                for start in starts:
                    hidden = hidden | (block == start)
                rows = slice((n_slash + j) * BLK, (n_slash + j + 1) * BLK)
                kg[rows, HD:] = masks[jnp.where(hidden, 2, 0)]
            q_rows = pl.ds(pl.multiple_of(b * BLK, BLK), BLK)
            for g in range(group):
                qx[g * BLK : (g + 1) * BLK, :HD] = q_refs[slot][q_rows, g * HD : (g + 1) * HD]
            top = None
            for t in range(0, width, step):
                s = lax.dot_general(
                    qx[...], kg[t : t + step, :], (((1,), (1,)), ((), ())),
                    preferred_element_type=jnp.float32,
                )
                sc[:, t : t + step] = s
                for u in range(0, step, HD):
                    piece = s[:, u : u + HD]
                    top = piece if top is None else jnp.maximum(top, piece)
            top = jnp.max(top, axis=1, keepdims=True)
            acc = None
            for t in range(0, width, step):
                p = jnp.exp2((sc[:, t : t + step] - top) * factor).astype(vg.dtype)
                o = jnp.dot(p, vg[t : t + step, :], preferred_element_type=jnp.float32)
                acc = o if acc is None else acc + o
            res = (acc[:, :HD] / acc[:, HD:]).astype(out_refs[slot].dtype)
            for g in range(group):
                out_refs[slot][q_rows, g * HD : (g + 1) * HD] = res[g * BLK : (g + 1) * BLK]
            return carry

        lax.fori_loop(0, local, one_block, 0)


def attend(e, queries, q_other, windows, kv_vert, masks, vert, slash, info, local, plane):
    pair, reach = (1 if q_other is None else 2), len(windows) - 1
    heads, (n_slash, n_vert) = vert.shape[0], (slash.shape[1], vert.shape[1])
    dev_rows = queries.shape[0]
    wide = queries.shape[1] // (pair * heads)
    group = wide // HD
    width = (n_slash + n_vert) * BLK
    win_rows = sum(w.shape[0] for w in windows)
    dtype = queries.dtype
    rows = pair * local * group * BLK
    q_specs = [pl.BlockSpec((dev_rows, wide), lambda i, info, *_: (0, info[1] * heads + e))]
    if pair > 1:
        q_specs.append(pl.BlockSpec((dev_rows, wide), lambda i, *_: (0, e)))

    def whole(a):
        return pl.BlockSpec(a.shape, lambda i, *_: (0,) * a.ndim)

    return pl.pallas_call(
        functools.partial(
            attend_kernel, (e, pair, local, group, reach, n_slash, n_vert, plane, heads)
        ),
        grid_spec=pltpu.PrefetchScalarGridSpec(
            num_scalar_prefetch=3,
            grid=(1,),
            in_specs=q_specs + [whole(w) for w in windows] + [whole(kv_vert), whole(masks)],
            out_specs=[pl.BlockSpec((dev_rows, wide), lambda i, *_: (0, 0))] * pair,
            scratch_shapes=[
                pltpu.VMEM((win_rows, 2 * HD), dtype),
                pltpu.VMEM((width, 2 * HD), dtype),
                pltpu.VMEM((width, 2 * HD), dtype),
                pltpu.VMEM((group * BLK, 2 * HD), dtype),
                pltpu.VMEM((group * BLK, width), jnp.float32),
            ],
        ),
        out_shape=[jax.ShapeDtypeStruct((dev_rows, wide), dtype)] * pair,
        compiler_params=pltpu.CompilerParams(vmem_limit_bytes=VMEM_LIMIT),
        cost_estimate=pl.CostEstimate(
            flops=8 * rows * width * HD,
            bytes_accessed=2 * (2 * win_rows * HD + 2 * rows * HD),
            transcendentals=rows * width,
        ),
        name="attend",
    )(info, vert, slash, *([queries] if pair == 1 else [queries, q_other]), *windows, kv_vert, masks)


def project_kernel(n, has_before, info, *refs):
    lefts, rights, refs = refs[:n], refs[n : 2 * n], refs[2 * n :]
    acc = refs[0][...] if has_before else None
    for left, right in zip(lefts, rights):
        part = jnp.dot(left[...], right[...], preferred_element_type=jnp.float32)
        acc = part if acc is None else acc + part
    refs[-1][...] = acc.astype(refs[-1].dtype)


def project(pieces, before, out_weight, info, heads, dtype):
    rows, wide = pieces[0][2].shape
    columns = out_weight.shape[1]
    tile = min(512, columns)
    n = len(pieces)

    def weight_spec(swap, e):
        if swap:
            return pl.BlockSpec((wide, tile), lambda i, info: ((1 - info[1]) * heads + e, i))
        return pl.BlockSpec((wide, tile), lambda i, info: (info[1] * heads + e, i))

    in_specs = [pl.BlockSpec((rows, wide), lambda i, info: (0, 0))] * n
    in_specs += [weight_spec(swap, e) for swap, e, _ in pieces]
    args = [a for _, _, a in pieces] + [out_weight] * n
    out_spec = pl.BlockSpec((rows, tile), lambda i, info: (0, i))
    if before is not None:
        in_specs.append(out_spec)
        args.append(before)
    return pl.pallas_call(
        functools.partial(project_kernel, n, before is not None),
        grid_spec=pltpu.PrefetchScalarGridSpec(
            num_scalar_prefetch=1, grid=(columns // tile,), in_specs=in_specs, out_specs=out_spec
        ),
        out_shape=jax.ShapeDtypeStruct((rows, columns), dtype),
        compiler_params=pltpu.CompilerParams(vmem_limit_bytes=VMEM_LIMIT),
        cost_estimate=pl.CostEstimate(
            flops=2 * n * rows * wide * columns,
            bytes_accessed=2 * n * wide * (rows + columns) + 8 * rows * columns,
            transcendentals=0,
        ),
        name="project",
    )(info, *args)


def body(queries, keys, values, vertical_blocks, slash_offsets, out_weight):
    tokens_dev = queries.shape[0]
    kv_heads = keys.shape[1] // HD
    local = tokens_dev // BLK
    size = lax.axis_size("ctx")
    pair = 2 if kv_heads % 2 == 0 and size % 2 == 0 and lax.axis_size("head") == 1 else 1
    chips = size // pair
    heads = kv_heads // pair
    plane = PLANE if chips % PLANE == 0 and heads * vertical_blocks.shape[1] % PLANE == 0 else 1
    chip_blocks = pair * local
    reach = -(-MAXOFF // chip_blocks)
    index = lax.axis_index("ctx")
    chip, core = index // pair, index % pair
    info = jnp.stack([chip, core]).astype(jnp.int32)
    pos = jnp.arange(BLK)
    causal = jnp.where(pos[:, None] > pos[None, :], MASKED, 0.0)
    masks = jnp.stack([jnp.zeros_like(causal), causal, jnp.full_like(causal, MASKED)])
    masks = masks.astype(queries.dtype)

    def part(value, axis, which):
        span = value.shape[axis] // pair
        return lax.dynamic_slice_in_dim(value, which * span, span, axis)

    vert, slash = part(vertical_blocks, 0, core), part(slash_offsets, 0, core)
    kv_other = q_other = None
    if pair == 2:
        away = 1 - core
        kv_other = crossed(jnp.concatenate([part(keys, 1, away), part(values, 1, away)], 1), 1)
        q_other = crossed(part(queries, 1, away), 1)
    own, listed = prepare(info, vert, keys, values, kv_other, heads, local, plane)

    total = listed[0]
    for k in range(1, plane):
        total = total + crossed(listed[k], k * pair)
    step = 1
    while step < chips // plane:
        total = total + shifted(total, step * plane * pair)
        step *= 2
    kv_vert = jnp.concatenate([total] + [crossed(total, k * pair) for k in range(1, plane)], 0)

    near, far = [], []
    for e in range(heads):
        windows = [own[e]]
        if pair == 2 and reach == 2 and chips % 2 == 0:
            two_back = shifted(own[e], 2 * pair)
            sent = jnp.where(chip % 2 == 0, own[e], two_back)
            windows += [crossed(sent, pair), two_back]
        else:
            windows += [shifted(own[e], pair * d) for d in range(1, reach + 1)]
        att = attend(e, queries, q_other, windows, kv_vert, masks, vert, slash, info, local, plane)
        near.append((False, e, att[0]))
        if pair == 2:
            far.append((True, e, crossed(att[1], 1)))
    if pair == 1:
        attended = jnp.concatenate([a for _, _, a in near], 1)
        attended = lax.all_gather(attended, "head", axis=1, tiled=True)
        output = jnp.dot(attended, out_weight, preferred_element_type=jnp.float32)
        return output.astype(jnp.bfloat16)
    first = None
    if heads > 1:
        first = project(near[:-1] + far[:-1], None, out_weight, info, heads, jnp.float32)
    return project(near[-1:] + far[-1:], first, out_weight, info, heads, jnp.bfloat16)


def solution(mesh):
    placed = (
        P("ctx", "head"),
        P("ctx", "head"),
        P("ctx", "head"),
        P("head", None),
        P("head", None),
        P(None, "head"),
    )
    return jax.shard_map(
        body, mesh=mesh, in_specs=placed, out_specs=P("ctx", "head"), check_vma=False
    )
```

```python
import functools
import math

import jax
import jax.numpy as jnp
from jax import lax
from jax.experimental import pallas as pl
from jax.experimental.pallas import tpu as pltpu
from jax.sharding import PartitionSpec as P

HD = 128
BLK = 128
MAXOFF = 16
PLANE = 4
MASKED = -1e30
VMEM_LIMIT = 56 * 1024 * 1024


def shifted(value, by):
    size = lax.axis_size("ctx")
    return lax.ppermute(value, "ctx", [(i, i + by) for i in range(size - by)])


def crossed(value, bits):
    size = lax.axis_size("ctx")
    return lax.ppermute(value, "ctx", [(i, i ^ bits) for i in range(size)])


def prepare_kernel(cfg, info, vert, *refs):
    pair, local, heads, plane = cfg
    chip, core = info[0], info[1]
    keys, values = refs[:2]
    refs = refs[2:]
    other = None
    if pair > 1:
        other, refs = refs[0], refs[1:]
    chip_outs, refs = refs[:heads], refs[heads:]
    list_outs, chip_kv = refs[:plane], refs[plane]
    n_vert = vert.shape[1]
    dev_rows = local * BLK
    chip_blocks = pair * local
    for e in range(heads):
        at = pl.multiple_of((core * heads + e) * HD, HD)
        chip_kv[e, :dev_rows, :HD] = keys[:, pl.ds(at, HD)]
        chip_kv[e, :dev_rows, HD:] = values[:, pl.ds(at, HD)]
        if pair > 1:
            chip_kv[e, dev_rows:, :HD] = other[:, e * HD : (e + 1) * HD]
            chip_kv[e, dev_rows:, HD:] = other[:, (heads + e) * HD : (heads + e + 1) * HD]
        chip_outs[e][...] = chip_kv[e]
    per = heads * n_vert // plane
    for k in range(plane):
        for i in range(per):
            flat = (chip % plane ^ k) * per + i
            e, j = flat // n_vert, flat % n_vert
            block = vert[e, j]
            within = block % chip_blocks
            if pair > 1:
                within = (within // local ^ core) * local + within % local
            rows = slice(i * BLK, (i + 1) * BLK)
            owned = block // chip_blocks == chip
            found = chip_kv[e, pl.ds(pl.multiple_of(within * BLK, BLK), BLK), :]
            list_outs[k][rows, :] = jnp.where(owned, found, jnp.zeros_like(found))


def prepare(info, vert, keys, values, other, heads, local, plane):
    pair = 1 if other is None else 2
    chip_rows = pair * local * BLK
    per = heads * vert.shape[1] // plane
    dtype = keys.dtype
    smem = pl.BlockSpec(memory_space=pltpu.SMEM)
    vmem = pl.BlockSpec(memory_space=pltpu.VMEM)
    data = [keys, values] + ([] if other is None else [other])
    outs = pl.pallas_call(
        functools.partial(prepare_kernel, (pair, local, heads, plane)),
        in_specs=[smem] * 2 + [vmem] * len(data),
        out_specs=[vmem] * (heads + plane),
        out_shape=[jax.ShapeDtypeStruct((chip_rows, 2 * HD), dtype)] * heads
        + [jax.ShapeDtypeStruct((per * BLK, 2 * HD), dtype)] * plane,
        scratch_shapes=[pltpu.VMEM((heads, chip_rows, 2 * HD), dtype)],
        compiler_params=pltpu.CompilerParams(vmem_limit_bytes=VMEM_LIMIT),
        cost_estimate=pl.CostEstimate(
            flops=0, bytes_accessed=8 * heads * chip_rows * 2 * HD, transcendentals=0
        ),
        name="prepare",
    )(info, vert, *data)
    return outs[:heads], outs[heads:]


def attend_kernel(cfg, info, vert, slash, *refs):
    e, pair, local, group, reach, n_slash, n_vert, plane, heads = cfg
    q_refs, refs = refs[:pair], refs[pair:]
    w_refs, refs = refs[: reach + 1], refs[reach + 1 :]
    kv_vert, masks, refs = refs[0], refs[1], refs[2:]
    out_refs, refs = refs[:pair], refs[pair:]
    win, kg, qx, res = refs[:4]
    vgs, scs, tops, ps = refs[4:6], refs[6:8], refs[8:10], refs[10:12]
    chip, core = info[0], info[1]
    dev_rows = local * BLK
    chip_blocks = pair * local
    chip_rows = chip_blocks * BLK
    width = (n_slash + n_vert) * BLK
    step = min(2 * BLK, width)
    factor = math.log2(math.e) / math.sqrt(HD)

    for back in range(reach + 1):
        for slot in range(pair):
            owner = core ^ slot if pair > 1 else 0
            at = pl.multiple_of((reach - back) * chip_rows + owner * dev_rows, dev_rows)
            win[pl.ds(at, dev_rows), :] = w_refs[back][slot * dev_rows : (slot + 1) * dev_rows, :]
    per = heads * n_vert // plane
    ones = jnp.ones((width, HD), vgs[0].dtype)
    for j in range(n_vert):
        part, place = divmod(e * n_vert + j, per)
        src = pl.multiple_of(((part ^ chip % plane) * per + place) * BLK, BLK)
        rows = slice((n_slash + j) * BLK, (n_slash + j + 1) * BLK)
        kg[rows, :HD] = kv_vert[pl.ds(src, BLK), :HD]
        for vg in vgs:
            vg[rows, :HD] = kv_vert[pl.ds(src, BLK), HD:]
    for vg in vgs:
        vg[:, HD:] = ones
    row = lax.broadcasted_iota(jnp.int32, (BLK, HD), 0)
    col = lax.broadcasted_iota(jnp.int32, (BLK, HD), 1)
    eye = jnp.where(row == col, 1.0, 0.0).astype(qx.dtype)
    for i in range(chip_blocks):
        slot, b = divmod(i, local)
        for g in range(group):
            rows = slice(g * BLK, (g + 1) * BLK)
            qx[i, rows, :HD] = q_refs[slot][b * BLK : (b + 1) * BLK, g * HD : (g + 1) * HD]
            qx[i, rows, HD:] = eye

    def within(i):
        return (core ^ i // local) * local + i % local if pair > 1 else i

    def take(i, j):
        src = (reach * chip_blocks + within(i) - slash[e, j]) * BLK
        return pl.ds(pl.multiple_of(src, BLK), BLK)

    def place_keys(i):
        here = chip * chip_blocks + within(i)
        starts = [here - slash[e, j] for j in range(n_slash)]
        for j in range(n_slash):
            rows = slice(j * BLK, (j + 1) * BLK)
            kg[rows, :HD] = win[take(i, j), :HD]
            kind = jnp.where(starts[j] < 0, 2, jnp.where(slash[e, j] == 0, 1, 0))
            kg[rows, HD:] = masks[kind]
        for j in range(n_vert):
            block = vert[e, j]
            hidden = block >= here
            for start in starts:
                hidden = hidden | (block == start)
            rows = slice((n_slash + j) * BLK, (n_slash + j + 1) * BLK)
            kg[rows, HD:] = masks[jnp.where(hidden, 2, 0)]

    def place_values(i, at):
        for j in range(n_slash):
            vgs[at][j * BLK : (j + 1) * BLK, :HD] = win[take(i, j), HD:]

    def score_tile(i, at, t):
        s = lax.dot_general(
            qx[i], kg[t : t + step, :], (((1,), (1,)), ((), ())),
            preferred_element_type=jnp.float32,
        )
        scs[at][:, t : t + step] = s
        top = s[:, :HD]
        for u in range(HD, step, HD):
            top = jnp.maximum(top, s[:, u : u + HD])
        tops[at][...] = top if t == 0 else jnp.maximum(tops[at][...], top)

    def soften(at, r, some):
        rows = slice(r, r + some)
        top = jnp.max(tops[at][rows, :], axis=1, keepdims=True)
        for t in range(0, width, step):
            p = jnp.exp2((scs[at][rows, t : t + step] - top) * factor)
            ps[at][rows, t : t + step] = p.astype(ps[at].dtype)

    def weigh(i, at):
        acc = jnp.dot(ps[at][...], vgs[at][...], preferred_element_type=jnp.float32)
        res[i] = (acc[:, :HD] / acc[:, HD:]).astype(res.dtype)

    n_tiles = width // step
    some = group * BLK // n_tiles

    def stage(i, at, ahead, behind):
        place_values(i, at)
        if ahead:
            place_keys(i + 1)
        if behind:
            weigh(i - 1, 1 - at)
        for u in range(n_tiles):
            if ahead:
                score_tile(i + 1, 1 - at, u * step)
            soften(at, u * some, some)

    place_keys(0)
    for u in range(n_tiles):
        score_tile(0, 0, u * step)
    stage(0, 0, chip_blocks > 1, False)

    def two_blocks(n, carry):
        stage(2 * n + 1, 1, True, True)
        stage(2 * n + 2, 0, True, True)
        return carry

    inner = max(chip_blocks - 2, 0) // 2
    lax.fori_loop(0, inner, two_blocks, 0)
    for i in range(2 * inner + 1, chip_blocks):
        stage(i, i % 2, i + 1 < chip_blocks, True)
    weigh(chip_blocks - 1, (chip_blocks - 1) % 2)
    for i in range(chip_blocks):
        slot, b = divmod(i, local)
        for g in range(group):
            out_refs[slot][b * BLK : (b + 1) * BLK, g * HD : (g + 1) * HD] = res[
                i, g * BLK : (g + 1) * BLK
            ]


def attend(e, queries, q_other, windows, kv_vert, masks, vert, slash, info, local, plane):
    pair, reach = (1 if q_other is None else 2), len(windows) - 1
    heads, (n_slash, n_vert) = vert.shape[0], (slash.shape[1], vert.shape[1])
    dev_rows = queries.shape[0]
    wide = queries.shape[1] // (pair * heads)
    group = wide // HD
    width = (n_slash + n_vert) * BLK
    win_rows = sum(w.shape[0] for w in windows)
    dtype = queries.dtype
    blocks = pair * local
    rows = blocks * group * BLK
    q_specs = [pl.BlockSpec((dev_rows, wide), lambda i, info, *_: (0, info[1] * heads + e))]
    if pair > 1:
        q_specs.append(pl.BlockSpec((dev_rows, wide), lambda i, *_: (0, e)))

    def whole(a):
        return pl.BlockSpec(a.shape, lambda i, *_: (0,) * a.ndim)

    return pl.pallas_call(
        functools.partial(
            attend_kernel, (e, pair, local, group, reach, n_slash, n_vert, plane, heads)
        ),
        grid_spec=pltpu.PrefetchScalarGridSpec(
            num_scalar_prefetch=3,
            grid=(1,),
            in_specs=q_specs + [whole(w) for w in windows] + [whole(kv_vert), whole(masks)],
            out_specs=[pl.BlockSpec((dev_rows, wide), lambda i, *_: (0, 0))] * pair,
            scratch_shapes=[
                pltpu.VMEM((win_rows, 2 * HD), dtype),
                pltpu.VMEM((width, 2 * HD), dtype),
                pltpu.VMEM((blocks, group * BLK, 2 * HD), dtype),
                pltpu.VMEM((blocks, group * BLK, HD), dtype),
            ]
            + [pltpu.VMEM((width, 2 * HD), dtype)] * 2
            + [pltpu.VMEM((group * BLK, width), jnp.float32)] * 2
            + [pltpu.VMEM((group * BLK, HD), jnp.float32)] * 2
            + [pltpu.VMEM((group * BLK, width), dtype)] * 2,
        ),
        out_shape=[jax.ShapeDtypeStruct((dev_rows, wide), dtype)] * pair,
        compiler_params=pltpu.CompilerParams(vmem_limit_bytes=VMEM_LIMIT),
        cost_estimate=pl.CostEstimate(
            flops=8 * rows * width * HD,
            bytes_accessed=2 * (2 * win_rows * HD + 2 * rows * HD),
            transcendentals=rows * width,
        ),
        name="attend",
    )(info, vert, slash, *([queries] if pair == 1 else [queries, q_other]), *windows, kv_vert, masks)


def project_kernel(n, has_before, info, *refs):
    lefts, rights, refs = refs[:n], refs[n : 2 * n], refs[2 * n :]
    acc = refs[0][...] if has_before else None
    for left, right in zip(lefts, rights):
        part = jnp.dot(left[...], right[...], preferred_element_type=jnp.float32)
        acc = part if acc is None else acc + part
    refs[-1][...] = acc.astype(refs[-1].dtype)


def project(pieces, before, out_weight, info, heads, dtype):
    rows, wide = pieces[0][2].shape
    columns = out_weight.shape[1]
    tile = min(512, columns)
    n = len(pieces)

    def weight_spec(swap, e):
        if swap:
            return pl.BlockSpec((wide, tile), lambda i, info: ((1 - info[1]) * heads + e, i))
        return pl.BlockSpec((wide, tile), lambda i, info: (info[1] * heads + e, i))

    in_specs = [pl.BlockSpec((rows, wide), lambda i, info: (0, 0))] * n
    in_specs += [weight_spec(swap, e) for swap, e, _ in pieces]
    args = [a for _, _, a in pieces] + [out_weight] * n
    out_spec = pl.BlockSpec((rows, tile), lambda i, info: (0, i))
    if before is not None:
        in_specs.append(out_spec)
        args.append(before)
    return pl.pallas_call(
        functools.partial(project_kernel, n, before is not None),
        grid_spec=pltpu.PrefetchScalarGridSpec(
            num_scalar_prefetch=1, grid=(columns // tile,), in_specs=in_specs, out_specs=out_spec
        ),
        out_shape=jax.ShapeDtypeStruct((rows, columns), dtype),
        compiler_params=pltpu.CompilerParams(vmem_limit_bytes=VMEM_LIMIT),
        cost_estimate=pl.CostEstimate(
            flops=2 * n * rows * wide * columns,
            bytes_accessed=2 * n * wide * (rows + columns) + 8 * rows * columns,
            transcendentals=0,
        ),
        name="project",
    )(info, *args)


def body(queries, keys, values, vertical_blocks, slash_offsets, out_weight):
    tokens_dev = queries.shape[0]
    kv_heads = keys.shape[1] // HD
    local = tokens_dev // BLK
    size = lax.axis_size("ctx")
    pair = 2 if kv_heads % 2 == 0 and size % 2 == 0 and lax.axis_size("head") == 1 else 1
    chips = size // pair
    heads = kv_heads // pair
    plane = PLANE if chips % PLANE == 0 and heads * vertical_blocks.shape[1] % PLANE == 0 else 1
    chip_blocks = pair * local
    reach = -(-MAXOFF // chip_blocks)
    index = lax.axis_index("ctx")
    chip, core = index // pair, index % pair
    info = jnp.stack([chip, core]).astype(jnp.int32)
    pos = jnp.arange(BLK)
    causal = jnp.where(pos[:, None] > pos[None, :], MASKED, 0.0)
    masks = jnp.stack([jnp.zeros_like(causal), causal, jnp.full_like(causal, MASKED)])
    masks = masks.astype(queries.dtype)

    def part(value, axis, which):
        span = value.shape[axis] // pair
        return lax.dynamic_slice_in_dim(value, which * span, span, axis)

    vert, slash = part(vertical_blocks, 0, core), part(slash_offsets, 0, core)
    kv_other = q_other = None
    if pair == 2:
        away = 1 - core
        kv_other = crossed(jnp.concatenate([part(keys, 1, away), part(values, 1, away)], 1), 1)
        q_other = crossed(part(queries, 1, away), 1)
    own, listed = prepare(info, vert, keys, values, kv_other, heads, local, plane)

    total = listed[0]
    for k in range(1, plane):
        total = total + crossed(listed[k], k * pair)
    step = 1
    while step < chips // plane:
        total = total + shifted(total, step * plane * pair)
        step *= 2
    kv_vert = jnp.concatenate([total] + [crossed(total, k * pair) for k in range(1, plane)], 0)

    near, far = [], []
    for e in range(heads):
        windows = [own[e]]
        if pair == 2 and reach == 2 and chips % 2 == 0:
            two_back = shifted(own[e], 2 * pair)
            sent = jnp.where(chip % 2 == 0, own[e], two_back)
            windows += [crossed(sent, pair), two_back]
        else:
            windows += [shifted(own[e], pair * d) for d in range(1, reach + 1)]
        att = attend(e, queries, q_other, windows, kv_vert, masks, vert, slash, info, local, plane)
        near.append((False, e, att[0]))
        if pair == 2:
            far.append((True, e, crossed(att[1], 1)))
    if pair == 1:
        attended = jnp.concatenate([a for _, _, a in near], 1)
        attended = lax.all_gather(attended, "head", axis=1, tiled=True)
        output = jnp.dot(attended, out_weight, preferred_element_type=jnp.float32)
        return output.astype(jnp.bfloat16)
    first = None
    if heads > 1:
        first = project(near[:-1] + far[:-1], None, out_weight, info, heads, jnp.float32)
    return project(near[-1:] + far[-1:], first, out_weight, info, heads, jnp.bfloat16)


def solution(mesh):
    placed = (
        P("ctx", "head"),
        P("ctx", "head"),
        P("ctx", "head"),
        P("head", None),
        P("head", None),
        P(None, "head"),
    )
    return jax.shard_map(
        body, mesh=mesh, in_specs=placed, out_specs=P("ctx", "head"), check_vma=False
    )
```

```python
import functools
import math

import jax
import jax.numpy as jnp
from jax import lax
from jax.experimental import pallas as pl
from jax.experimental.pallas import tpu as pltpu
from jax.sharding import PartitionSpec as P

HD = 128
BLK = 128
MAXOFF = 16
PLANE = 4
MASKED = -1e30
SMALLEST, LARGEST = 2.0**-60, 2.0**100
VMEM_LIMIT = 56 * 1024 * 1024


def shifted(value, by):
    size = lax.axis_size("ctx")
    return lax.ppermute(value, "ctx", [(i, i + by) for i in range(size - by)])


def crossed(value, bits):
    size = lax.axis_size("ctx")
    return lax.ppermute(value, "ctx", [(i, i ^ bits) for i in range(size)])


def prepare_kernel(cfg, info, vert, *refs):
    pair, local, heads, plane, per_chunk = cfg
    chip, core = info[0], info[1]
    keys, values = refs[:2]
    refs = refs[2:]
    other = None
    if pair > 1:
        other, refs = refs[0], refs[1:]
    n_chunks = heads // per_chunk
    chip_outs, refs = refs[:n_chunks], refs[n_chunks:]
    list_outs, chip_kv = refs[:plane], refs[plane]
    n_vert = vert.shape[1]
    dev_rows = local * BLK
    chip_blocks = pair * local
    for e in range(heads):
        at = pl.multiple_of((core * heads + e) * HD, HD)
        chip_kv[e, :dev_rows, :HD] = keys[:, pl.ds(at, HD)]
        chip_kv[e, :dev_rows, HD:] = values[:, pl.ds(at, HD)]
        if pair > 1:
            chip_kv[e, dev_rows:, :HD] = other[:, e * HD : (e + 1) * HD]
            chip_kv[e, dev_rows:, HD:] = other[:, (heads + e) * HD : (heads + e + 1) * HD]
        c, at = divmod(e, per_chunk)
        chip_outs[c][:, at * 2 * HD : (at + 1) * 2 * HD] = chip_kv[e]
    per = heads * n_vert // plane
    for k in range(plane):
        for i in range(per):
            flat = (chip % plane ^ k) * per + i
            e, j = flat // n_vert, flat % n_vert
            block = vert[e, j]
            within = block % chip_blocks
            if pair > 1:
                within = (within // local ^ core) * local + within % local
            rows = slice(i * BLK, (i + 1) * BLK)
            owned = block // chip_blocks == chip
            found = chip_kv[e, pl.ds(pl.multiple_of(within * BLK, BLK), BLK), :]
            list_outs[k][rows, :] = jnp.where(owned, found, jnp.zeros_like(found))


def prepare(info, vert, keys, values, other, heads, local, plane, per_chunk):
    pair = 1 if other is None else 2
    chip_rows = pair * local * BLK
    n_chunks = heads // per_chunk
    per = heads * vert.shape[1] // plane
    dtype = keys.dtype
    smem = pl.BlockSpec(memory_space=pltpu.SMEM)
    vmem = pl.BlockSpec(memory_space=pltpu.VMEM)
    data = [keys, values] + ([] if other is None else [other])
    specs = [vmem] * 2
    if other is not None:
        specs.append(pl.BlockSpec((other.shape[0], heads * 2 * HD), lambda i: (0, 0)))
    outs = pl.pallas_call(
        functools.partial(prepare_kernel, (pair, local, heads, plane, per_chunk)),
        grid=(1,),
        in_specs=[smem] * 2 + specs,
        out_specs=[vmem] * (n_chunks + plane),
        out_shape=[jax.ShapeDtypeStruct((chip_rows, per_chunk * 2 * HD), dtype)] * n_chunks
        + [jax.ShapeDtypeStruct((per * BLK, 2 * HD), dtype)] * plane,
        scratch_shapes=[pltpu.VMEM((heads, chip_rows, 2 * HD), dtype)],
        compiler_params=pltpu.CompilerParams(vmem_limit_bytes=VMEM_LIMIT),
        cost_estimate=pl.CostEstimate(
            flops=0, bytes_accessed=8 * heads * chip_rows * 2 * HD, transcendentals=0
        ),
        name="prepare",
    )(info, vert, *data)
    return outs[:n_chunks], outs[n_chunks:]


def attend_kernel(cfg, info, vert, slash, *refs):
    e, pair, local, group, reach, n_slash, n_vert, plane, heads = cfg
    q_refs, refs = refs[:pair], refs[pair:]
    w_refs, refs = refs[: reach + 1], refs[reach + 1 :]
    kv_vert, masks, refs = refs[0], refs[1], refs[2:]
    out_refs, refs = refs[:pair], refs[pair:]
    win, qx, res, sc, good = refs[:5]
    kgs, vgs, ps = refs[5:7], refs[7:9], refs[9:11]
    chip, core = info[0], info[1]
    dev_rows = local * BLK
    chip_blocks = pair * local
    chip_rows = chip_blocks * BLK
    width = (n_slash + n_vert) * BLK
    step = min(2 * BLK, width)
    factor = math.log2(math.e) / math.sqrt(HD)

    for back in range(reach + 1):
        for slot in range(pair):
            owner = core ^ slot if pair > 1 else 0
            at = pl.multiple_of((reach - back) * chip_rows + owner * dev_rows, dev_rows)
            rows = slice(slot * dev_rows, (slot + 1) * dev_rows)
            win[pl.ds(at, dev_rows), :] = w_refs[back][rows, :]
    per = heads * n_vert // plane
    ones = jnp.ones((width, HD), vgs[0].dtype)
    for j in range(n_vert):
        part, place = divmod(e * n_vert + j, per)
        src = pl.multiple_of(((part ^ chip % plane) * per + place) * BLK, BLK)
        rows = slice((n_slash + j) * BLK, (n_slash + j + 1) * BLK)
        for kg in kgs:
            kg[rows, :HD] = kv_vert[pl.ds(src, BLK), :HD]
        for vg in vgs:
            vg[rows, :HD] = kv_vert[pl.ds(src, BLK), HD:]
    for vg in vgs:
        vg[:, HD:] = ones
    row = lax.broadcasted_iota(jnp.int32, (BLK, HD), 0)
    col = lax.broadcasted_iota(jnp.int32, (BLK, HD), 1)
    eye = jnp.where(row == col, 1.0, 0.0).astype(qx.dtype)
    for i in range(chip_blocks):
        slot, b = divmod(i, local)
        for g in range(group):
            rows = slice(g * BLK, (g + 1) * BLK)
            qx[i, rows, :HD] = q_refs[slot][b * BLK : (b + 1) * BLK, g * HD : (g + 1) * HD]
            qx[i, rows, HD:] = eye

    def within(i):
        return (core ^ i // local) * local + i % local if pair > 1 else i

    def take(i, j):
        src = (reach * chip_blocks + within(i) - slash[e, j]) * BLK
        return pl.ds(pl.multiple_of(src, BLK), BLK)

    def place_keys(i, at):
        here = chip * chip_blocks + within(i)
        starts = [here - slash[e, j] for j in range(n_slash)]
        for j in range(n_slash):
            rows = slice(j * BLK, (j + 1) * BLK)
            kgs[at][rows, :HD] = win[take(i, j), :HD]
            kind = jnp.where(starts[j] < 0, 2, jnp.where(slash[e, j] == 0, 1, 0))
            kgs[at][rows, HD:] = masks[kind]
        for j in range(n_vert):
            block = vert[e, j]
            hidden = block >= here
            for start in starts:
                hidden = hidden | (block == start)
            rows = slice((n_slash + j) * BLK, (n_slash + j + 1) * BLK)
            kgs[at][rows, HD:] = masks[jnp.where(hidden, 2, 0)]

    def place_values(i, at):
        for j in range(n_slash):
            vgs[at][j * BLK : (j + 1) * BLK, :HD] = win[take(i, j), HD:]

    def score_tile(i, at, t):
        return lax.dot_general(
            qx[i], kgs[at][t : t + step, :], (((1,), (1,)), ((), ())),
            preferred_element_type=jnp.float32,
        )

    def weigh(i, at):
        acc = jnp.dot(ps[at][...], vgs[at][...], preferred_element_type=jnp.float32)
        total = acc[:, HD:]
        res[i] = (acc[:, :HD] / total).astype(res.dtype)
        fine = jnp.where((total > SMALLEST) & (total < LARGEST), 1.0, 0.0)
        good[...] = jnp.minimum(good[...], jnp.min(fine, axis=0, keepdims=True))

    def stage(i, at, ahead, behind):
        if ahead:
            place_keys(i + 1, 1 - at)
        place_values(i, at)
        if behind:
            weigh(i - 1, 1 - at)
        for t in range(0, width, step):
            p = jnp.exp2(score_tile(i, at, t) * factor)
            ps[at][:, t : t + step] = p.astype(ps[at].dtype)

    good[...] = jnp.ones(good.shape, good.dtype)
    place_keys(0, 0)
    stage(0, 0, chip_blocks > 1, False)

    def two_blocks(n, carry):
        stage(2 * n + 1, 1, True, True)
        stage(2 * n + 2, 0, True, True)
        return carry

    inner = max(chip_blocks - 2, 0) // 2
    lax.fori_loop(0, inner, two_blocks, 0)
    for i in range(2 * inner + 1, chip_blocks):
        stage(i, i % 2, i + 1 < chip_blocks, True)
    weigh(chip_blocks - 1, (chip_blocks - 1) % 2)

    @pl.when(jnp.logical_not(jnp.min(good[...]) > 0.5))
    def _():
        def shifted_block(i, carry):
            place_keys(i, 0)
            place_values(i, 0)
            top = None
            for t in range(0, width, step):
                s = score_tile(i, 0, t)
                sc[:, t : t + step] = s
                for u in range(0, step, HD):
                    piece = s[:, u : u + HD]
                    top = piece if top is None else jnp.maximum(top, piece)
            top = jnp.max(top, axis=1, keepdims=True)
            for t in range(0, width, step):
                p = jnp.exp2((sc[:, t : t + step] - top) * factor)
                ps[0][:, t : t + step] = p.astype(ps[0].dtype)
            acc = jnp.dot(ps[0][...], vgs[0][...], preferred_element_type=jnp.float32)
            res[i] = (acc[:, :HD] / acc[:, HD:]).astype(res.dtype)
            return carry

        lax.fori_loop(0, chip_blocks, shifted_block, 0)

    for i in range(chip_blocks):
        slot, b = divmod(i, local)
        for g in range(group):
            out_refs[slot][b * BLK : (b + 1) * BLK, g * HD : (g + 1) * HD] = res[
                i, g * BLK : (g + 1) * BLK
            ]


def attend(e, col, queries, q_other, windows, kv_vert, masks, vert, slash, info, local, plane):
    pair, reach = (1 if q_other is None else 2), len(windows) - 1
    heads, (n_slash, n_vert) = vert.shape[0], (slash.shape[1], vert.shape[1])
    dev_rows = queries.shape[0]
    wide = queries.shape[1] // (pair * heads)
    group = wide // HD
    width = (n_slash + n_vert) * BLK
    win_rows = sum(w.shape[0] for w in windows)
    dtype = queries.dtype
    blocks = pair * local
    rows = blocks * group * BLK
    q_at = 0 if pair == 1 else q_other.shape[1] // wide - heads
    q_specs = [pl.BlockSpec((dev_rows, wide), lambda i, info, *_: (0, info[1] * heads + e))]
    if pair > 1:
        q_specs.append(pl.BlockSpec((dev_rows, wide), lambda i, *_: (0, q_at + e)))

    def whole(a):
        return pl.BlockSpec(a.shape, lambda i, *_: (0,) * a.ndim)

    return pl.pallas_call(
        functools.partial(
            attend_kernel, (e, pair, local, group, reach, n_slash, n_vert, plane, heads)
        ),
        grid_spec=pltpu.PrefetchScalarGridSpec(
            num_scalar_prefetch=3,
            grid=(1,),
            in_specs=q_specs + [pl.BlockSpec((w.shape[0], 2 * HD), lambda i, *_: (0, col)) for w in windows] + [whole(kv_vert), whole(masks)],
            out_specs=[pl.BlockSpec((dev_rows, wide), lambda i, *_: (0, 0))] * pair,
            scratch_shapes=[
                pltpu.VMEM((win_rows, 2 * HD), dtype),
                pltpu.VMEM((blocks, group * BLK, 2 * HD), dtype),
                pltpu.VMEM((blocks, group * BLK, HD), dtype),
                pltpu.VMEM((group * BLK, width), jnp.float32),
                pltpu.VMEM((1, HD), jnp.float32),
            ]
            + [pltpu.VMEM((width, 2 * HD), dtype)] * 4
            + [pltpu.VMEM((group * BLK, width), dtype)] * 2,
        ),
        out_shape=[jax.ShapeDtypeStruct((dev_rows, wide), dtype)] * pair,
        compiler_params=pltpu.CompilerParams(vmem_limit_bytes=VMEM_LIMIT),
        cost_estimate=pl.CostEstimate(
            flops=8 * rows * width * HD,
            bytes_accessed=2 * (2 * win_rows * HD + 2 * rows * HD),
            transcendentals=rows * width,
        ),
        name="attend",
    )(info, vert, slash, *([queries] if pair == 1 else [queries, q_other]), *windows, kv_vert, masks)


def project_kernel(n, has_before, info, *refs):
    lefts, rights, refs = refs[:n], refs[n : 2 * n], refs[2 * n :]
    acc = refs[0][...] if has_before else None
    for left, right in zip(lefts, rights):
        part = jnp.dot(left[...], right[...], preferred_element_type=jnp.float32)
        acc = part if acc is None else acc + part
    refs[-1][...] = acc.astype(refs[-1].dtype)


def project(pieces, before, out_weight, info, heads, dtype):
    rows, wide = pieces[0][2].shape
    columns = out_weight.shape[1]
    tile = min(512, columns)
    n = len(pieces)

    def weight_spec(swap, e):
        if swap:
            return pl.BlockSpec((wide, tile), lambda i, info: ((1 - info[1]) * heads + e, i))
        return pl.BlockSpec((wide, tile), lambda i, info: (info[1] * heads + e, i))

    in_specs = [pl.BlockSpec((rows, wide), lambda i, info: (0, 0))] * n
    in_specs += [weight_spec(swap, e) for swap, e, _ in pieces]
    args = [a for _, _, a in pieces] + [out_weight] * n
    out_spec = pl.BlockSpec((rows, tile), lambda i, info: (0, i))
    if before is not None:
        in_specs.append(out_spec)
        args.append(before)
    return pl.pallas_call(
        functools.partial(project_kernel, n, before is not None),
        grid_spec=pltpu.PrefetchScalarGridSpec(
            num_scalar_prefetch=1, grid=(columns // tile,), in_specs=in_specs, out_specs=out_spec
        ),
        out_shape=jax.ShapeDtypeStruct((rows, columns), dtype),
        compiler_params=pltpu.CompilerParams(vmem_limit_bytes=VMEM_LIMIT),
        cost_estimate=pl.CostEstimate(
            flops=2 * n * rows * wide * columns,
            bytes_accessed=2 * n * wide * (rows + columns) + 8 * rows * columns,
            transcendentals=0,
        ),
        name="project",
    )(info, *args)


def body(queries, keys, values, vertical_blocks, slash_offsets, out_weight):
    tokens_dev = queries.shape[0]
    kv_heads = keys.shape[1] // HD
    local = tokens_dev // BLK
    size = lax.axis_size("ctx")
    pair = 2 if kv_heads % 2 == 0 and size % 2 == 0 and lax.axis_size("head") == 1 else 1
    chips = size // pair
    heads = kv_heads // pair
    plane = PLANE if chips % PLANE == 0 and heads * vertical_blocks.shape[1] % PLANE == 0 else 1
    chip_blocks = pair * local
    reach = -(-MAXOFF // chip_blocks)
    index = lax.axis_index("ctx")
    chip, core = index // pair, index % pair
    info = jnp.stack([chip, core]).astype(jnp.int32)
    pos = jnp.arange(BLK)
    causal = jnp.where(pos[:, None] > pos[None, :], MASKED, 0.0)
    masks = jnp.stack([jnp.zeros_like(causal), causal, jnp.full_like(causal, MASKED)])
    masks = masks.astype(queries.dtype)

    def part(value, axis, which):
        span = value.shape[axis] // pair
        return lax.dynamic_slice_in_dim(value, which * span, span, axis)

    vert, slash = part(vertical_blocks, 0, core), part(slash_offsets, 0, core)
    other = None
    if pair == 2:
        sent = [part(a, 1, 1 - core) for a in (keys, values, queries)]
        other = crossed(jnp.concatenate(sent, 1), 1)
    per_chunk = 2 if heads % 2 == 0 else 1
    own, listed = prepare(info, vert, keys, values, other, heads, local, plane, per_chunk)

    total = listed[0]
    for k in range(1, plane):
        total = total + crossed(listed[k], k * pair)
    step = 1
    while step < chips // plane:
        total = total + shifted(total, step * plane * pair)
        step *= 2
    kv_vert = jnp.concatenate([total] + [crossed(total, k * pair) for k in range(1, plane)], 0)

    near, far = [], []
    for c in range(heads // per_chunk):
        windows = [own[c]]
        if pair == 2 and reach == 2 and chips % 2 == 0:
            two_back = shifted(own[c], 2 * pair)
            passed = jnp.where(chip % 2 == 0, own[c], two_back)
            windows += [crossed(passed, pair), two_back]
        else:
            windows += [shifted(own[c], pair * d) for d in range(1, reach + 1)]
        for col in range(per_chunk):
            e = c * per_chunk + col
            att = attend(
                e, col, queries, other, windows, kv_vert, masks, vert, slash, info, local, plane
            )
            near.append((False, e, att[0]))
            if pair == 2:
                far.append((True, e, crossed(att[1], 1)))
    if pair == 1:
        attended = jnp.concatenate([a for _, _, a in near], 1)
        attended = lax.all_gather(attended, "head", axis=1, tiled=True)
        output = jnp.dot(attended, out_weight, preferred_element_type=jnp.float32)
        return output.astype(jnp.bfloat16)
    first = None
    if heads > 1:
        first = project(near[:-1] + far[:-1], None, out_weight, info, heads, jnp.float32)
    return project(near[-1:] + far[-1:], first, out_weight, info, heads, jnp.bfloat16)


def solution(mesh):
    placed = (
        P("ctx", "head"),
        P("ctx", "head"),
        P("ctx", "head"),
        P("head", None),
        P("head", None),
        P(None, "head"),
    )
    return jax.shard_map(
        body, mesh=mesh, in_specs=placed, out_specs=P("ctx", "head"), check_vma=False
    )
```

```python
import functools
import math

import jax
import jax.numpy as jnp
from jax import lax
from jax.experimental import pallas as pl
from jax.experimental.pallas import tpu as pltpu
from jax.sharding import PartitionSpec as P

HD = 128
BLK = 128
MAXOFF = 16
PLANE = 4
MASKED = -1e30
SMALLEST, LARGEST = 2.0**-60, 2.0**100
VMEM_LIMIT = 56 * 1024 * 1024


def shifted(value, by):
    size = lax.axis_size("ctx")
    return lax.ppermute(value, "ctx", [(i, i + by) for i in range(size - by)])


def crossed(value, bits):
    size = lax.axis_size("ctx")
    return lax.ppermute(value, "ctx", [(i, i ^ bits) for i in range(size)])


def prepare_kernel(cfg, info, vert, *refs):
    pair, local, heads, plane, per_chunk = cfg
    chip, core = info[0], info[1]
    keys, values = refs[:2]
    refs = refs[2:]
    other = None
    if pair > 1:
        other, refs = refs[0], refs[1:]
    n_chunks = heads // per_chunk
    chip_outs, refs = refs[:n_chunks], refs[n_chunks:]
    list_outs, chip_kv = refs[:plane], refs[plane]
    n_vert = vert.shape[1]
    dev_rows = local * BLK
    chip_blocks = pair * local
    for e in range(heads):
        at = pl.multiple_of((core * heads + e) * HD, HD)
        chip_kv[e, :dev_rows, :HD] = keys[:, pl.ds(at, HD)]
        chip_kv[e, :dev_rows, HD:] = values[:, pl.ds(at, HD)]
        if pair > 1:
            chip_kv[e, dev_rows:, :HD] = other[:, e * HD : (e + 1) * HD]
            chip_kv[e, dev_rows:, HD:] = other[:, (heads + e) * HD : (heads + e + 1) * HD]
        c, at = divmod(e, per_chunk)
        chip_outs[c][:, at * 2 * HD : (at + 1) * 2 * HD] = chip_kv[e]
    per = heads * n_vert // plane
    for k in range(plane):
        for i in range(per):
            flat = (chip % plane ^ k) * per + i
            e, j = flat // n_vert, flat % n_vert
            block = vert[e, j]
            within = block % chip_blocks
            if pair > 1:
                within = (within // local ^ core) * local + within % local
            rows = slice(i * BLK, (i + 1) * BLK)
            owned = block // chip_blocks == chip
            found = chip_kv[e, pl.ds(pl.multiple_of(within * BLK, BLK), BLK), :]
            list_outs[k][rows, :] = jnp.where(owned, found, jnp.zeros_like(found))


def prepare(info, vert, keys, values, other, heads, local, plane, per_chunk):
    pair = 1 if other is None else 2
    chip_rows = pair * local * BLK
    n_chunks = heads // per_chunk
    per = heads * vert.shape[1] // plane
    dtype = keys.dtype
    smem = pl.BlockSpec(memory_space=pltpu.SMEM)
    vmem = pl.BlockSpec(memory_space=pltpu.VMEM)
    data = [keys, values] + ([] if other is None else [other])
    specs = [vmem] * 2
    if other is not None:
        specs.append(pl.BlockSpec((other.shape[0], heads * 2 * HD), lambda i: (0, 0)))
    outs = pl.pallas_call(
        functools.partial(prepare_kernel, (pair, local, heads, plane, per_chunk)),
        grid=(1,),
        in_specs=[smem] * 2 + specs,
        out_specs=[vmem] * (n_chunks + plane),
        out_shape=[jax.ShapeDtypeStruct((chip_rows, per_chunk * 2 * HD), dtype)] * n_chunks
        + [jax.ShapeDtypeStruct((per * BLK, 2 * HD), dtype)] * plane,
        scratch_shapes=[pltpu.VMEM((heads, chip_rows, 2 * HD), dtype)],
        compiler_params=pltpu.CompilerParams(vmem_limit_bytes=VMEM_LIMIT),
        cost_estimate=pl.CostEstimate(
            flops=0, bytes_accessed=8 * heads * chip_rows * 2 * HD, transcendentals=0
        ),
        name="prepare",
    )(info, vert, *data)
    return outs[:n_chunks], outs[n_chunks:]


def onehot_rows(shape, at, dtype):
    row = lax.broadcasted_iota(jnp.int32, shape, 0)
    col = lax.broadcasted_iota(jnp.int32, shape, 1)
    return jnp.where(col == at(row), 1.0, 0.0).astype(dtype)


def exponentials(q, k, factor):
    s = lax.dot_general(q, k, (((1,), (1,)), ((), ())), preferred_element_type=jnp.float32)
    return jnp.exp2(s * factor)


def pipelined(blocks, stage):
    stage(0, 0, blocks > 1, False)

    def two_blocks(n, carry):
        stage(2 * n + 1, 1, True, True)
        stage(2 * n + 2, 0, True, True)
        return carry

    inner = max(blocks - 2, 0) // 2
    lax.fori_loop(0, inner, two_blocks, 0)
    for i in range(2 * inner + 1, blocks):
        stage(i, i % 2, i + 1 < blocks, True)
    stage(blocks, blocks % 2, False, True)


def slash_kernel(cfg, info, slash, *refs):
    first, pair, local, group, reach, n_slash = cfg
    q_refs, refs = refs[:pair], refs[pair:]
    w_refs, refs = refs[: reach + 1], refs[reach + 1 :]
    masks, acc, win, qx = refs[:4]
    kgs, vgs, ps = refs[4:6], refs[6:8], refs[8:10]
    e = first + pl.program_id(0)
    chip, core = info[0], info[1]
    dev_rows = local * BLK
    chip_blocks = pair * local
    chip_rows = chip_blocks * BLK
    width = n_slash * BLK
    step = min(2 * BLK, width)
    factor = math.log2(math.e) / math.sqrt(HD)

    for back in range(reach + 1):
        for slot in range(pair):
            owner = core ^ slot if pair > 1 else 0
            at = pl.multiple_of((reach - back) * chip_rows + owner * dev_rows, dev_rows)
            rows = slice(slot * dev_rows, (slot + 1) * dev_rows)
            win[pl.ds(at, dev_rows), :] = w_refs[back][rows, :]
    for vg in vgs:
        vg[:, HD:] = jnp.ones((width, HD), vg.dtype)
    eye = onehot_rows((BLK, HD), lambda row: row, qx.dtype)
    for i in range(chip_blocks):
        slot, b = divmod(i, local)
        for g in range(group):
            rows = slice(g * BLK, (g + 1) * BLK)
            qx[i, rows, :HD] = q_refs[slot][b * BLK : (b + 1) * BLK, g * HD : (g + 1) * HD]
            qx[i, rows, HD:] = eye

    def within(i):
        return (core ^ i // local) * local + i % local if pair > 1 else i

    def take(i, j):
        src = (reach * chip_blocks + within(i) - slash[e, j]) * BLK
        return pl.ds(pl.multiple_of(src, BLK), BLK)

    def place_keys(i, at):
        here = chip * chip_blocks + within(i)
        for j in range(n_slash):
            off = slash[e, j]
            rows = slice(j * BLK, (j + 1) * BLK)
            kgs[at][rows, :HD] = win[take(i, j), :HD]
            kgs[at][rows, HD:] = masks[jnp.where(off > here, 2, jnp.where(off == 0, 1, 0))]

    def stage(i, at, ahead, behind):
        if ahead:
            place_keys(i + 1, 1 - at)
        if behind:
            acc[i - 1] = jnp.dot(
                ps[1 - at][...], vgs[1 - at][...], preferred_element_type=jnp.float32
            )
        if isinstance(i, int) and i == chip_blocks:
            return
        for j in range(n_slash):
            vgs[at][j * BLK : (j + 1) * BLK, :HD] = win[take(i, j), HD:]
        for t in range(0, width, step):
            p = exponentials(qx[i], kgs[at][t : t + step, :], factor)
            ps[at][:, t : t + step] = p.astype(ps[at].dtype)

    place_keys(0, 0)
    pipelined(chip_blocks, stage)


def vertical_kernel(cfg, info, vert, slash, *refs):
    first, pair, local, group, reach, n_slash, n_vert, plane, heads = cfg
    q_refs, refs = refs[:pair], refs[pair:]
    w_refs, refs = refs[: reach + 1], refs[reach + 1 :]
    before, kv_vert, masks, refs = refs[0], refs[1], refs[2], refs[3:]
    out_refs, refs = refs[:pair], refs[pair:]
    ke, ve, qx, res, good = refs[:5]
    ps, (kg, vg, sc, pg) = refs[5:7], refs[7:]
    e = first + pl.program_id(0)
    chip, core = info[0], info[1]
    dev_rows = local * BLK
    chip_blocks = pair * local
    wide = n_vert * BLK
    step = min(2 * BLK, wide)
    factor = math.log2(math.e) / math.sqrt(HD)

    def within(i):
        return (core ^ i // local) * local + i % local if pair > 1 else i

    def hidden(i, j):
        here = chip * chip_blocks + within(i)
        found = vert[e, j] >= here
        for u in range(n_slash):
            found = found | (vert[e, j] == here - slash[e, u])
        return found

    per = heads * n_vert // plane
    lane = lax.broadcasted_iota(jnp.int32, (BLK, HD), 1)
    for j in range(n_vert):
        flat = e * n_vert + j
        src = pl.multiple_of(((flat // per ^ chip % plane) * per + flat % per) * BLK, BLK)
        rows = slice(j * BLK, (j + 1) * BLK)
        ke[rows, :HD] = kv_vert[pl.ds(src, BLK), :HD]
        ve[rows, :HD] = kv_vert[pl.ds(src, BLK), HD:]
        bias = jnp.zeros((BLK, HD), jnp.float32)
        for i in range(chip_blocks):
            bias = jnp.where((lane == i) & hidden(i, j), MASKED, bias)
        ke[rows, HD:] = bias.astype(ke.dtype)
    ve[:, HD:] = jnp.ones((wide, HD), ve.dtype)
    for i in range(chip_blocks):
        slot, b = divmod(i, local)
        for g in range(group):
            rows = slice(g * BLK, (g + 1) * BLK)
            qx[i, rows, :HD] = q_refs[slot][b * BLK : (b + 1) * BLK, g * HD : (g + 1) * HD]
            qx[i, rows, HD:] = onehot_rows((BLK, HD), lambda row, i=i: i, qx.dtype)
    good[...] = jnp.ones(good.shape, good.dtype)

    def stage(i, at, ahead, behind):
        if behind:
            acc = before[i - 1] + jnp.dot(
                ps[1 - at][...], ve[...], preferred_element_type=jnp.float32
            )
            total = acc[:, HD:]
            res[i - 1] = (acc[:, :HD] / total).astype(res.dtype)
            fine = jnp.where((total > SMALLEST) & (total < LARGEST), 1.0, 0.0)
            good[...] = jnp.minimum(good[...], jnp.min(fine, axis=0, keepdims=True))
        if isinstance(i, int) and i == chip_blocks:
            return
        for t in range(0, wide, step):
            p = exponentials(qx[i], ke[t : t + step, :], factor)
            ps[at][:, t : t + step] = p.astype(ps[at].dtype)

    pipelined(chip_blocks, stage)

    @pl.when(jnp.logical_not(jnp.min(good[...]) > 0.5))
    def _():
        vg[: n_slash * BLK, HD:] = jnp.ones((n_slash * BLK, HD), vg.dtype)
        kg[n_slash * BLK :, :] = ke[...]
        vg[n_slash * BLK :, :] = ve[...]
        eye = onehot_rows((BLK, HD), lambda row: row, qx.dtype)

        def shifted_block(i, carry):
            here = chip * chip_blocks + within(i)
            for g in range(group):
                qx[i, g * BLK : (g + 1) * BLK, HD:] = eye
            for j in range(n_slash):
                off = slash[e, j]
                pos = reach * chip_blocks + within(i) - off
                back = reach - pos // chip_blocks
                src = pos % chip_blocks
                if pair > 1:
                    src = (src // local ^ core) * local + src % local
                at = pl.ds(pl.multiple_of(src * BLK, BLK), BLK)
                found = w_refs[0][at, :]
                for d in range(1, reach + 1):
                    found = jnp.where(back == d, w_refs[d][at, :], found)
                rows = slice(j * BLK, (j + 1) * BLK)
                kg[rows, :HD] = found[:, :HD]
                vg[rows, :HD] = found[:, HD:]
                kg[rows, HD:] = masks[jnp.where(off > here, 2, jnp.where(off == 0, 1, 0))]
            for j in range(n_vert):
                rows = slice((n_slash + j) * BLK, (n_slash + j + 1) * BLK)
                kg[rows, HD:] = masks[jnp.where(hidden(i, j), 2, 0)]
            top = None
            for t in range(0, kg.shape[0], step):
                s = lax.dot_general(
                    qx[i], kg[t : t + step, :], (((1,), (1,)), ((), ())),
                    preferred_element_type=jnp.float32,
                )
                sc[:, t : t + step] = s
                for u in range(0, step, HD):
                    piece = s[:, u : u + HD]
                    top = piece if top is None else jnp.maximum(top, piece)
            top = jnp.max(top, axis=1, keepdims=True)
            for t in range(0, kg.shape[0], step):
                p = jnp.exp2((sc[:, t : t + step] - top) * factor)
                pg[:, t : t + step] = p.astype(pg.dtype)
            acc = jnp.dot(pg[...], vg[...], preferred_element_type=jnp.float32)
            res[i] = (acc[:, :HD] / acc[:, HD:]).astype(res.dtype)
            return carry

        lax.fori_loop(0, chip_blocks, shifted_block, 0)

    for i in range(chip_blocks):
        slot, b = divmod(i, local)
        for g in range(group):
            out_refs[slot][b * BLK : (b + 1) * BLK, g * HD : (g + 1) * HD] = res[
                i, g * BLK : (g + 1) * BLK
            ]


class Attention:
    def __init__(self, queries, q_other, info, vert, slash, masks, heads, local, plane):
        self.pair = 1 if q_other is None else 2
        self.qs = [queries] if q_other is None else [queries, q_other]
        self.info, self.vert, self.slash, self.masks = info, vert, slash, masks
        self.heads, self.local, self.plane = heads, local, plane
        self.dev_rows = queries.shape[0]
        self.wide = queries.shape[1] // (self.pair * heads)
        self.group = self.wide // HD
        self.blocks = self.pair * local
        self.dtype = queries.dtype

    def specs(self, first, windows):
        heads, shape = self.heads, (self.dev_rows, self.wide)
        specs = [pl.BlockSpec(shape, lambda i, info, *_: (0, info[1] * heads + first + i))]
        if self.pair > 1:
            at = self.qs[1].shape[1] // self.wide - heads + first
            specs.append(pl.BlockSpec(shape, lambda i, *_: (0, at + i)))
        return specs + [pl.BlockSpec((w.shape[0], 2 * HD), lambda i, *_: (0, i)) for w in windows]

    def whole(self, a):
        return pl.BlockSpec(a.shape, lambda i, *_: (0,) * a.ndim)

    def cost(self, n, width, more):
        rows = n * self.blocks * self.group * BLK
        return pl.CostEstimate(
            flops=8 * rows * width * HD,
            bytes_accessed=rows * HD * 2 + more,
            transcendentals=rows * width,
        )

    def acc_spec(self):
        shape = (self.blocks, self.group * BLK, 2 * HD)
        return pl.BlockSpec((None, *shape), lambda i, *_: (i, 0, 0, 0))

    def over_slash(self, first, n, windows):
        n_slash = self.slash.shape[1]
        width, rows = n_slash * BLK, self.group * BLK
        shape = (n, self.blocks, rows, 2 * HD)
        cfg = (first, self.pair, self.local, self.group, len(windows) - 1, n_slash)
        return pl.pallas_call(
            functools.partial(slash_kernel, cfg),
            grid_spec=pltpu.PrefetchScalarGridSpec(
                num_scalar_prefetch=2,
                grid=(n,),
                in_specs=self.specs(first, windows) + [self.whole(self.masks)],
                out_specs=self.acc_spec(),
                scratch_shapes=[
                    pltpu.VMEM((sum(w.shape[0] for w in windows), 2 * HD), self.dtype),
                    pltpu.VMEM((self.blocks, rows, 2 * HD), self.dtype),
                ]
                + [pltpu.VMEM((width, 2 * HD), self.dtype)] * 4
                + [pltpu.VMEM((rows, width), self.dtype)] * 2,
            ),
            out_shape=jax.ShapeDtypeStruct(shape, jnp.float32),
            compiler_params=pltpu.CompilerParams(vmem_limit_bytes=VMEM_LIMIT),
            cost_estimate=self.cost(n, width, 4 * math.prod(shape)),
            name="attend_slash",
        )(self.info, self.slash, *self.qs, *windows, self.masks)

    def over_vertical(self, first, n, windows, before, kv_vert):
        n_slash, n_vert = self.slash.shape[1], self.vert.shape[1]
        width, both, rows = n_vert * BLK, (n_slash + n_vert) * BLK, self.group * BLK
        cfg = (first, self.pair, self.local, self.group, len(windows) - 1, n_slash, n_vert)
        out = pl.BlockSpec((self.dev_rows, self.wide), lambda i, *_: (0, i))
        return pl.pallas_call(
            functools.partial(vertical_kernel, cfg + (self.plane, self.heads)),
            grid_spec=pltpu.PrefetchScalarGridSpec(
                num_scalar_prefetch=3,
                grid=(n,),
                in_specs=self.specs(first, windows)
                + [self.acc_spec(), self.whole(kv_vert), self.whole(self.masks)],
                out_specs=[out] * self.pair,
                scratch_shapes=[
                    pltpu.VMEM((width, 2 * HD), self.dtype),
                    pltpu.VMEM((width, 2 * HD), self.dtype),
                    pltpu.VMEM((self.blocks, rows, 2 * HD), self.dtype),
                    pltpu.VMEM((self.blocks, rows, HD), self.dtype),
                    pltpu.VMEM((1, HD), jnp.float32),
                    pltpu.VMEM((rows, width), self.dtype),
                    pltpu.VMEM((rows, width), self.dtype),
                    pltpu.VMEM((both, 2 * HD), self.dtype),
                    pltpu.VMEM((both, 2 * HD), self.dtype),
                    pltpu.VMEM((rows, both), jnp.float32),
                    pltpu.VMEM((rows, both), self.dtype),
                ],
            ),
            out_shape=[jax.ShapeDtypeStruct((self.dev_rows, n * self.wide), self.dtype)]
            * self.pair,
            compiler_params=pltpu.CompilerParams(vmem_limit_bytes=VMEM_LIMIT),
            cost_estimate=self.cost(n, width, 4 * math.prod(before.shape)),
            name="attend_vertical",
        )(self.info, self.vert, self.slash, *self.qs, *windows, before, kv_vert, self.masks)


def project_kernel(n, has_before, info, *refs):
    lefts, rights, refs = refs[:n], refs[n : 2 * n], refs[2 * n :]
    acc = refs[0][...] if has_before else None
    for left, right in zip(lefts, rights):
        part = jnp.dot(left[...], right[...], preferred_element_type=jnp.float32)
        acc = part if acc is None else acc + part
    refs[-1][...] = acc.astype(refs[-1].dtype)


def project(pieces, before, out_weight, info, chunks, dtype):
    rows, wide = pieces[0][2].shape
    columns = out_weight.shape[1]
    tile = min(512, columns)
    n = len(pieces)

    def weight_spec(swap, c):
        if swap:
            return pl.BlockSpec((wide, tile), lambda i, info: ((1 - info[1]) * chunks + c, i))
        return pl.BlockSpec((wide, tile), lambda i, info: (info[1] * chunks + c, i))

    in_specs = [pl.BlockSpec((rows, wide), lambda i, info: (0, 0))] * n
    in_specs += [weight_spec(swap, c) for swap, c, _ in pieces]
    args = [a for _, _, a in pieces] + [out_weight] * n
    out_spec = pl.BlockSpec((rows, tile), lambda i, info: (0, i))
    if before is not None:
        in_specs.append(out_spec)
        args.append(before)
    return pl.pallas_call(
        functools.partial(project_kernel, n, before is not None),
        grid_spec=pltpu.PrefetchScalarGridSpec(
            num_scalar_prefetch=1, grid=(columns // tile,), in_specs=in_specs, out_specs=out_spec
        ),
        out_shape=jax.ShapeDtypeStruct((rows, columns), dtype),
        compiler_params=pltpu.CompilerParams(vmem_limit_bytes=VMEM_LIMIT),
        cost_estimate=pl.CostEstimate(
            flops=2 * n * rows * wide * columns,
            bytes_accessed=2 * n * wide * (rows + columns) + 8 * rows * columns,
            transcendentals=0,
        ),
        name="project",
    )(info, *args)


def body(queries, keys, values, vertical_blocks, slash_offsets, out_weight):
    tokens_dev = queries.shape[0]
    kv_heads = keys.shape[1] // HD
    local = tokens_dev // BLK
    size = lax.axis_size("ctx")
    pair = 2 if kv_heads % 2 == 0 and size % 2 == 0 and lax.axis_size("head") == 1 else 1
    chips = size // pair
    heads = kv_heads // pair
    plane = PLANE if chips % PLANE == 0 and heads * vertical_blocks.shape[1] % PLANE == 0 else 1
    chip_blocks = pair * local
    reach = -(-MAXOFF // chip_blocks)
    index = lax.axis_index("ctx")
    chip, core = index // pair, index % pair
    info = jnp.stack([chip, core]).astype(jnp.int32)
    pos = jnp.arange(BLK)
    causal = jnp.where(pos[:, None] > pos[None, :], MASKED, 0.0)
    masks = jnp.stack([jnp.zeros_like(causal), causal, jnp.full_like(causal, MASKED)])
    masks = masks.astype(queries.dtype)

    def part(value, axis, which):
        span = value.shape[axis] // pair
        return lax.dynamic_slice_in_dim(value, which * span, span, axis)

    vert, slash = part(vertical_blocks, 0, core), part(slash_offsets, 0, core)
    other = None
    if pair == 2:
        sent = [part(a, 1, 1 - core) for a in (keys, values, queries)]
        other = crossed(jnp.concatenate(sent, 1), 1)
    per_chunk = 2 if heads % 2 == 0 else 1
    own, listed = prepare(info, vert, keys, values, other, heads, local, plane, per_chunk)

    total = listed[0]
    for k in range(1, plane):
        total = total + crossed(listed[k], k * pair)
    step = 1
    while step < chips // plane:
        total = total + shifted(total, step * plane * pair)
        step *= 2
    kv_vert = jnp.concatenate([total] + [crossed(total, k * pair) for k in range(1, plane)], 0)

    attention = Attention(queries, other, info, vert, slash, masks, heads, local, plane)
    near, far = [], []
    for c in range(heads // per_chunk):
        windows = [own[c]]
        if pair == 2 and reach == 2 and chips % 2 == 0:
            two_back = shifted(own[c], 2 * pair)
            passed = jnp.where(chip % 2 == 0, own[c], two_back)
            windows += [crossed(passed, pair), two_back]
        else:
            windows += [shifted(own[c], pair * d) for d in range(1, reach + 1)]
        first = c * per_chunk
        sums = attention.over_slash(first, per_chunk, windows)
        att = attention.over_vertical(first, per_chunk, windows, sums, kv_vert)
        near.append((False, c, att[0]))
        if pair == 2:
            far.append((True, c, crossed(att[1], 1)))
    if pair == 1:
        attended = jnp.concatenate([a for _, _, a in near], 1)
        attended = lax.all_gather(attended, "head", axis=1, tiled=True)
        output = jnp.dot(attended, out_weight, preferred_element_type=jnp.float32)
        return output.astype(jnp.bfloat16)
    chunks = heads // per_chunk
    first = None
    if chunks > 1:
        first = project(near[:-1] + far[:-1], None, out_weight, info, chunks, jnp.float32)
    return project(near[-1:] + far[-1:], first, out_weight, info, chunks, jnp.bfloat16)


def solution(mesh):
    placed = (
        P("ctx", "head"),
        P("ctx", "head"),
        P("ctx", "head"),
        P("head", None),
        P("head", None),
        P(None, "head"),
    )
    return jax.shard_map(
        body, mesh=mesh, in_specs=placed, out_specs=P("ctx", "head"), check_vma=False
    )
```

```python
import functools
import math

import jax
import jax.numpy as jnp
from jax import lax
from jax.experimental import pallas as pl
from jax.experimental.pallas import tpu as pltpu
from jax.sharding import PartitionSpec as P

HD = 128
BLK = 128
MAXOFF = 16
PLANE = 4
MASKED = -1e30
SMALLEST, LARGEST = 2.0**-60, 2.0**100
VMEM_LIMIT = 56 * 1024 * 1024


def shifted(value, by):
    size = lax.axis_size("ctx")
    return lax.ppermute(value, "ctx", [(i, i + by) for i in range(size - by)])


def crossed(value, bits):
    size = lax.axis_size("ctx")
    return lax.ppermute(value, "ctx", [(i, i ^ bits) for i in range(size)])


def prepare_kernel(cfg, info, vert, *refs):
    pair, local, heads, plane, per_chunk = cfg
    chip, core = info[0], info[1]
    keys, values = refs[:2]
    refs = refs[2:]
    other = None
    if pair > 1:
        other, refs = refs[0], refs[1:]
    n_chunks = heads // per_chunk
    chip_outs, refs = refs[:n_chunks], refs[n_chunks:]
    list_outs, chip_kv = refs[:plane], refs[plane]
    n_vert = vert.shape[1]
    dev_rows = local * BLK
    chip_blocks = pair * local
    for e in range(heads):
        at = pl.multiple_of((core * heads + e) * HD, HD)
        chip_kv[e, :dev_rows, :HD] = keys[:, pl.ds(at, HD)]
        chip_kv[e, :dev_rows, HD:] = values[:, pl.ds(at, HD)]
        if pair > 1:
            chip_kv[e, dev_rows:, :HD] = other[:, e * HD : (e + 1) * HD]
            chip_kv[e, dev_rows:, HD:] = other[:, (heads + e) * HD : (heads + e + 1) * HD]
        c, at = divmod(e, per_chunk)
        chip_outs[c][:, at * 2 * HD : (at + 1) * 2 * HD] = chip_kv[e]
    per = heads * n_vert // plane
    for k in range(plane):
        for i in range(per):
            flat = (chip % plane ^ k) * per + i
            e, j = flat // n_vert, flat % n_vert
            block = vert[e, j]
            within = block % chip_blocks
            if pair > 1:
                within = (within // local ^ core) * local + within % local
            rows = slice(i * BLK, (i + 1) * BLK)
            owned = block // chip_blocks == chip
            found = chip_kv[e, pl.ds(pl.multiple_of(within * BLK, BLK), BLK), :]
            list_outs[k][rows, :] = jnp.where(owned, found, jnp.zeros_like(found))


def prepare(info, vert, keys, values, other, heads, local, plane, per_chunk):
    pair = 1 if other is None else 2
    chip_rows = pair * local * BLK
    n_chunks = heads // per_chunk
    per = heads * vert.shape[1] // plane
    dtype = keys.dtype
    smem = pl.BlockSpec(memory_space=pltpu.SMEM)
    vmem = pl.BlockSpec(memory_space=pltpu.VMEM)
    data = [keys, values] + ([] if other is None else [other])
    specs = [vmem] * 2
    if other is not None:
        specs.append(pl.BlockSpec((other.shape[0], heads * 2 * HD), lambda i: (0, 0)))
    outs = pl.pallas_call(
        functools.partial(prepare_kernel, (pair, local, heads, plane, per_chunk)),
        grid=(1,),
        in_specs=[smem] * 2 + specs,
        out_specs=[vmem] * (n_chunks + plane),
        out_shape=[jax.ShapeDtypeStruct((chip_rows, per_chunk * 2 * HD), dtype)] * n_chunks
        + [jax.ShapeDtypeStruct((per * BLK, 2 * HD), dtype)] * plane,
        scratch_shapes=[pltpu.VMEM((heads, chip_rows, 2 * HD), dtype)],
        compiler_params=pltpu.CompilerParams(vmem_limit_bytes=VMEM_LIMIT),
        cost_estimate=pl.CostEstimate(
            flops=0, bytes_accessed=8 * heads * chip_rows * 2 * HD, transcendentals=0
        ),
        name="prepare",
    )(info, vert, *data)
    return list(outs[:n_chunks]), list(outs[n_chunks:])


def onehot_rows(shape, at, dtype):
    row = lax.broadcasted_iota(jnp.int32, shape, 0)
    col = lax.broadcasted_iota(jnp.int32, shape, 1)
    return jnp.where(col == at(row), 1.0, 0.0).astype(dtype)


def exponentials(q, k, factor):
    s = lax.dot_general(q, k, (((1,), (1,)), ((), ())), preferred_element_type=jnp.float32)
    return jnp.exp2(s * factor)


def pipelined(blocks, stage):
    stage(0, 0, blocks > 1, False)

    def two_blocks(n, carry):
        stage(2 * n + 1, 1, True, True)
        stage(2 * n + 2, 0, True, True)
        return carry

    inner = max(blocks - 2, 0) // 2
    lax.fori_loop(0, inner, two_blocks, 0)
    for i in range(2 * inner + 1, blocks):
        stage(i, i % 2, i + 1 < blocks, True)
    stage(blocks, blocks % 2, False, True)


def slash_kernel(cfg, info, slash, *refs):
    first, pair, local, group, reach, n_slash = cfg
    q_refs, refs = refs[:pair], refs[pair:]
    w_refs, refs = refs[: reach + 1], refs[reach + 1 :]
    masks, acc, win, qx = refs[:4]
    kgs, vgs, ps = refs[4:6], refs[6:8], refs[8:10]
    e = first + pl.program_id(0)
    chip, core = info[0], info[1]
    dev_rows = local * BLK
    chip_blocks = pair * local
    chip_rows = chip_blocks * BLK
    width = n_slash * BLK
    factor = math.log2(math.e) / math.sqrt(HD)

    for back in range(reach + 1):
        for slot in range(pair):
            owner = core ^ slot if pair > 1 else 0
            at = pl.multiple_of((reach - back) * chip_rows + owner * dev_rows, dev_rows)
            rows = slice(slot * dev_rows, (slot + 1) * dev_rows)
            win[pl.ds(at, dev_rows), :] = w_refs[back][rows, :]
    for vg in vgs:
        vg[:, HD:] = jnp.ones((width, HD), vg.dtype)
    eye = onehot_rows((BLK, HD), lambda row: row, qx.dtype)
    for i in range(chip_blocks):
        slot, b = divmod(i, local)
        for g in range(group):
            rows = slice(g * BLK, (g + 1) * BLK)
            qx[i, rows, :HD] = q_refs[slot][b * BLK : (b + 1) * BLK, g * HD : (g + 1) * HD]
            qx[i, rows, HD:] = eye

    def within(i):
        return (core ^ i // local) * local + i % local if pair > 1 else i

    def take(i, j):
        src = (reach * chip_blocks + within(i) - slash[e, j]) * BLK
        return pl.ds(pl.multiple_of(src, BLK), BLK)

    def place_keys(i, at):
        here = chip * chip_blocks + within(i)
        for j in range(n_slash):
            off = slash[e, j]
            rows = slice(j * BLK, (j + 1) * BLK)
            kgs[at][rows, :HD] = win[take(i, j), :HD]
            kgs[at][rows, HD:] = masks[jnp.where(off > here, 2, jnp.where(off == 0, 1, 0))]

    def stage(i, at, ahead, behind):
        if ahead:
            place_keys(i + 1, 1 - at)
        if behind:
            acc[i - 1] = jnp.dot(
                ps[1 - at][...], vgs[1 - at][...], preferred_element_type=jnp.float32
            )
        if isinstance(i, int) and i == chip_blocks:
            return
        for j in range(n_slash):
            vgs[at][j * BLK : (j + 1) * BLK, :HD] = win[take(i, j), HD:]
        ps[at][...] = exponentials(qx[i], kgs[at][...], factor).astype(ps[at].dtype)

    place_keys(0, 0)
    pipelined(chip_blocks, stage)


def vertical_kernel(cfg, info, vert, slash, *refs):
    first, pair, local, group, reach, n_slash, n_vert, plane, heads = cfg
    q_refs, refs = refs[:pair], refs[pair:]
    w_refs, refs = refs[: reach + 1], refs[reach + 1 :]
    before, kv_vert, masks, refs = refs[0], refs[1], refs[2], refs[3:]
    out_refs, refs = refs[:pair], refs[pair:]
    ke, ve, qx, res, good = refs[:5]
    ps, (kg, vg, sc, pg) = refs[5:7], refs[7:]
    e = first + pl.program_id(0)
    chip, core = info[0], info[1]
    dev_rows = local * BLK
    chip_blocks = pair * local
    wide = n_vert * BLK
    step = min(2 * BLK, wide)
    factor = math.log2(math.e) / math.sqrt(HD)

    def within(i):
        return (core ^ i // local) * local + i % local if pair > 1 else i

    def hidden(i, j):
        here = chip * chip_blocks + within(i)
        found = vert[e, j] >= here
        for u in range(n_slash):
            found = found | (vert[e, j] == here - slash[e, u])
        return found

    per = heads * n_vert // plane
    lane = lax.broadcasted_iota(jnp.int32, (BLK, HD), 1)
    for j in range(n_vert):
        flat = e * n_vert + j
        src = pl.multiple_of(((flat // per ^ chip % plane) * per + flat % per) * BLK, BLK)
        rows = slice(j * BLK, (j + 1) * BLK)
        ke[rows, :HD] = kv_vert[pl.ds(src, BLK), :HD]
        ve[rows, :HD] = kv_vert[pl.ds(src, BLK), HD:]
        bias = jnp.zeros((BLK, HD), jnp.float32)
        for i in range(chip_blocks):
            bias = jnp.where((lane == i) & hidden(i, j), MASKED, bias)
        ke[rows, HD:] = bias.astype(ke.dtype)
    ve[:, HD:] = jnp.ones((wide, HD), ve.dtype)
    for i in range(chip_blocks):
        slot, b = divmod(i, local)
        for g in range(group):
            rows = slice(g * BLK, (g + 1) * BLK)
            qx[i, rows, :HD] = q_refs[slot][b * BLK : (b + 1) * BLK, g * HD : (g + 1) * HD]
            qx[i, rows, HD:] = onehot_rows((BLK, HD), lambda row, i=i: i, qx.dtype)
    good[...] = jnp.ones(good.shape, good.dtype)

    def stage(i, at, ahead, behind):
        if behind:
            acc = before[i - 1] + jnp.dot(
                ps[1 - at][...], ve[...], preferred_element_type=jnp.float32
            )
            total = acc[:, HD:]
            res[i - 1] = (acc[:, :HD] / total).astype(res.dtype)
            fine = jnp.where((total > SMALLEST) & (total < LARGEST), 1.0, 0.0)
            good[...] = jnp.minimum(good[...], jnp.min(fine, axis=0, keepdims=True))
        if isinstance(i, int) and i == chip_blocks:
            return
        ps[at][...] = exponentials(qx[i], ke[...], factor).astype(ps[at].dtype)

    pipelined(chip_blocks, stage)

    @pl.when(jnp.logical_not(jnp.min(good[...]) > 0.5))
    def _():
        vg[: n_slash * BLK, HD:] = jnp.ones((n_slash * BLK, HD), vg.dtype)
        kg[n_slash * BLK :, :] = ke[...]
        vg[n_slash * BLK :, :] = ve[...]
        eye = onehot_rows((BLK, HD), lambda row: row, qx.dtype)

        def shifted_block(i, carry):
            here = chip * chip_blocks + within(i)
            for g in range(group):
                qx[i, g * BLK : (g + 1) * BLK, HD:] = eye
            for j in range(n_slash):
                off = slash[e, j]
                pos = reach * chip_blocks + within(i) - off
                back = reach - pos // chip_blocks
                src = pos % chip_blocks
                if pair > 1:
                    src = (src // local ^ core) * local + src % local
                at = pl.ds(pl.multiple_of(src * BLK, BLK), BLK)
                found = w_refs[0][at, :]
                for d in range(1, reach + 1):
                    found = jnp.where(back == d, w_refs[d][at, :], found)
                rows = slice(j * BLK, (j + 1) * BLK)
                kg[rows, :HD] = found[:, :HD]
                vg[rows, :HD] = found[:, HD:]
                kg[rows, HD:] = masks[jnp.where(off > here, 2, jnp.where(off == 0, 1, 0))]
            for j in range(n_vert):
                rows = slice((n_slash + j) * BLK, (n_slash + j + 1) * BLK)
                kg[rows, HD:] = masks[jnp.where(hidden(i, j), 2, 0)]
            top = None
            for t in range(0, kg.shape[0], step):
                s = lax.dot_general(
                    qx[i], kg[t : t + step, :], (((1,), (1,)), ((), ())),
                    preferred_element_type=jnp.float32,
                )
                sc[:, t : t + step] = s
                for u in range(0, step, HD):
                    piece = s[:, u : u + HD]
                    top = piece if top is None else jnp.maximum(top, piece)
            top = jnp.max(top, axis=1, keepdims=True)
            for t in range(0, kg.shape[0], step):
                p = jnp.exp2((sc[:, t : t + step] - top) * factor)
                pg[:, t : t + step] = p.astype(pg.dtype)
            acc = jnp.dot(pg[...], vg[...], preferred_element_type=jnp.float32)
            res[i] = (acc[:, :HD] / acc[:, HD:]).astype(res.dtype)
            return carry

        lax.fori_loop(0, chip_blocks, shifted_block, 0)

    for i in range(chip_blocks):
        slot, b = divmod(i, local)
        for g in range(group):
            out_refs[slot][b * BLK : (b + 1) * BLK, g * HD : (g + 1) * HD] = res[
                i, g * BLK : (g + 1) * BLK
            ]


class Attention:
    def __init__(self, queries, q_other, info, vert, slash, masks, heads, local, plane):
        self.pair = 1 if q_other is None else 2
        self.qs = [queries] if q_other is None else [queries, q_other]
        self.info, self.vert, self.slash, self.masks = info, vert, slash, masks
        self.heads, self.local, self.plane = heads, local, plane
        self.dev_rows = queries.shape[0]
        self.wide = queries.shape[1] // (self.pair * heads)
        self.group = self.wide // HD
        self.blocks = self.pair * local
        self.dtype = queries.dtype

    def specs(self, first, windows):
        heads, shape = self.heads, (self.dev_rows, self.wide)
        specs = [pl.BlockSpec(shape, lambda i, info, *_: (0, info[1] * heads + first + i))]
        if self.pair > 1:
            at = self.qs[1].shape[1] // self.wide - heads + first
            specs.append(pl.BlockSpec(shape, lambda i, *_: (0, at + i)))
        return specs + [pl.BlockSpec((w.shape[0], 2 * HD), lambda i, *_: (0, i)) for w in windows]

    def whole(self, a):
        return pl.BlockSpec(a.shape, lambda i, *_: (0,) * a.ndim)

    def cost(self, n, width, more):
        rows = n * self.blocks * self.group * BLK
        return pl.CostEstimate(
            flops=8 * rows * width * HD,
            bytes_accessed=rows * HD * 2 + more,
            transcendentals=rows * width,
        )

    def acc_spec(self):
        shape = (self.blocks, self.group * BLK, 2 * HD)
        return pl.BlockSpec((None, *shape), lambda i, *_: (i, 0, 0, 0))

    def over_slash(self, first, n, windows):
        n_slash = self.slash.shape[1]
        width, rows = n_slash * BLK, self.group * BLK
        shape = (n, self.blocks, rows, 2 * HD)
        cfg = (first, self.pair, self.local, self.group, len(windows) - 1, n_slash)
        return pl.pallas_call(
            functools.partial(slash_kernel, cfg),
            grid_spec=pltpu.PrefetchScalarGridSpec(
                num_scalar_prefetch=2,
                grid=(n,),
                in_specs=self.specs(first, windows) + [self.whole(self.masks)],
                out_specs=self.acc_spec(),
                scratch_shapes=[
                    pltpu.VMEM((sum(w.shape[0] for w in windows), 2 * HD), self.dtype),
                    pltpu.VMEM((self.blocks, rows, 2 * HD), self.dtype),
                ]
                + [pltpu.VMEM((width, 2 * HD), self.dtype)] * 4
                + [pltpu.VMEM((rows, width), self.dtype)] * 2,
            ),
            out_shape=jax.ShapeDtypeStruct(shape, jnp.float32),
            compiler_params=pltpu.CompilerParams(vmem_limit_bytes=VMEM_LIMIT),
            cost_estimate=self.cost(n, width, 4 * math.prod(shape)),
            name="attend_slash",
        )(self.info, self.slash, *self.qs, *windows, self.masks)

    def over_vertical(self, first, n, windows, before, kv_vert):
        n_slash, n_vert = self.slash.shape[1], self.vert.shape[1]
        width, both, rows = n_vert * BLK, (n_slash + n_vert) * BLK, self.group * BLK
        cfg = (first, self.pair, self.local, self.group, len(windows) - 1, n_slash, n_vert)
        out = pl.BlockSpec((self.dev_rows, self.wide), lambda i, *_: (0, i))
        return pl.pallas_call(
            functools.partial(vertical_kernel, cfg + (self.plane, self.heads)),
            grid_spec=pltpu.PrefetchScalarGridSpec(
                num_scalar_prefetch=3,
                grid=(n,),
                in_specs=self.specs(first, windows)
                + [self.acc_spec(), self.whole(kv_vert), self.whole(self.masks)],
                out_specs=[out] * self.pair,
                scratch_shapes=[
                    pltpu.VMEM((width, 2 * HD), self.dtype),
                    pltpu.VMEM((width, 2 * HD), self.dtype),
                    pltpu.VMEM((self.blocks, rows, 2 * HD), self.dtype),
                    pltpu.VMEM((self.blocks, rows, HD), self.dtype),
                    pltpu.VMEM((1, HD), jnp.float32),
                    pltpu.VMEM((rows, width), self.dtype),
                    pltpu.VMEM((rows, width), self.dtype),
                    pltpu.VMEM((both, 2 * HD), self.dtype),
                    pltpu.VMEM((both, 2 * HD), self.dtype),
                    pltpu.VMEM((rows, both), jnp.float32),
                    pltpu.VMEM((rows, both), self.dtype),
                ],
            ),
            out_shape=[jax.ShapeDtypeStruct((self.dev_rows, n * self.wide), self.dtype)]
            * self.pair,
            compiler_params=pltpu.CompilerParams(vmem_limit_bytes=VMEM_LIMIT),
            cost_estimate=self.cost(n, width, 4 * math.prod(before.shape)),
            name="attend_vertical",
        )(self.info, self.vert, self.slash, *self.qs, *windows, before, kv_vert, self.masks)


def project_kernel(n, has_before, info, *refs):
    lefts, rights, refs = refs[:n], refs[n : 2 * n], refs[2 * n :]
    acc = refs[0][...] if has_before else None
    for left, right in zip(lefts, rights):
        part = jnp.dot(left[...], right[...], preferred_element_type=jnp.float32)
        acc = part if acc is None else acc + part
    refs[-1][...] = acc.astype(refs[-1].dtype)


def project(pieces, before, out_weight, info, chunks, dtype):
    rows, wide = pieces[0][2].shape
    columns = out_weight.shape[1]
    tile = min(1024, columns)
    n = len(pieces)

    def weight_spec(swap, c):
        if swap:
            return pl.BlockSpec((wide, tile), lambda i, info: ((1 - info[1]) * chunks + c, i))
        return pl.BlockSpec((wide, tile), lambda i, info: (info[1] * chunks + c, i))

    in_specs = [pl.BlockSpec((rows, wide), lambda i, info: (0, 0))] * n
    in_specs += [weight_spec(swap, c) for swap, c, _ in pieces]
    args = [a for _, _, a in pieces] + [out_weight] * n
    out_spec = pl.BlockSpec((rows, tile), lambda i, info: (0, i))
    if before is not None:
        in_specs.append(out_spec)
        args.append(before)
    return pl.pallas_call(
        functools.partial(project_kernel, n, before is not None),
        grid_spec=pltpu.PrefetchScalarGridSpec(
            num_scalar_prefetch=1, grid=(columns // tile,), in_specs=in_specs, out_specs=out_spec
        ),
        out_shape=jax.ShapeDtypeStruct((rows, columns), dtype),
        compiler_params=pltpu.CompilerParams(vmem_limit_bytes=VMEM_LIMIT),
        cost_estimate=pl.CostEstimate(
            flops=2 * n * rows * wide * columns,
            bytes_accessed=2 * n * wide * (rows + columns) + 8 * rows * columns,
            transcendentals=0,
        ),
        name="project",
    )(info, *args)


def body(queries, keys, values, vertical_blocks, slash_offsets, out_weight):
    tokens_dev = queries.shape[0]
    kv_heads = keys.shape[1] // HD
    local = tokens_dev // BLK
    size = lax.axis_size("ctx")
    pair = 2 if kv_heads % 2 == 0 and size % 2 == 0 and lax.axis_size("head") == 1 else 1
    chips = size // pair
    heads = kv_heads // pair
    plane = PLANE if chips % PLANE == 0 and heads * vertical_blocks.shape[1] % PLANE == 0 else 1
    chip_blocks = pair * local
    reach = -(-MAXOFF // chip_blocks)
    index = lax.axis_index("ctx")
    chip, core = index // pair, index % pair
    info = jnp.stack([chip, core]).astype(jnp.int32)
    pos = jnp.arange(BLK)
    causal = jnp.where(pos[:, None] > pos[None, :], MASKED, 0.0)
    masks = jnp.stack([jnp.zeros_like(causal), causal, jnp.full_like(causal, MASKED)])
    masks = masks.astype(queries.dtype)

    def part(value, axis, which):
        span = value.shape[axis] // pair
        return lax.dynamic_slice_in_dim(value, which * span, span, axis)

    vert, slash = part(vertical_blocks, 0, core), part(slash_offsets, 0, core)
    other = None
    if pair == 2:
        sent = [part(a, 1, 1 - core) for a in (keys, values, queries)]
        other = crossed(jnp.concatenate(sent, 1), 1)
    per_chunk = 2 if heads % 2 == 0 else 1
    own, listed = prepare(info, vert, keys, values, other, heads, local, plane, per_chunk)

    total = listed[0]
    for k in range(1, plane):
        total = total + crossed(listed[k], k * pair)
    total, own[1:] = lax.optimization_barrier((total, own[1:]))
    step = 1
    while step < chips // plane:
        total = total + shifted(total, step * plane * pair)
        step *= 2

    attention = Attention(queries, other, info, vert, slash, masks, heads, local, plane)
    chunks = heads // per_chunk
    all_windows, sums = [], []
    for c in range(chunks):
        windows = [own[c]]
        if pair == 2 and reach == 2 and chips % 2 == 0:
            two_back = shifted(own[c], 2 * pair)
            passed = jnp.where(chip % 2 == 0, own[c], two_back)
            windows += [crossed(passed, pair), two_back]
        else:
            windows += [shifted(own[c], pair * d) for d in range(1, reach + 1)]
        all_windows.append(windows)
        sums.append(attention.over_slash(c * per_chunk, per_chunk, windows))
    gathered = [total] + [crossed(total, k * pair) for k in range(1, plane)]
    gathered, sums = lax.optimization_barrier((gathered, sums))
    kv_vert = jnp.concatenate(gathered, 0)
    near, far = [], []
    for c in range(chunks):
        att = attention.over_vertical(c * per_chunk, per_chunk, all_windows[c], sums[c], kv_vert)
        near.append((False, c, att[0]))
        if pair == 2:
            far.append((True, c, crossed(att[1], 1)))
    if pair == 1:
        attended = jnp.concatenate([a for _, _, a in near], 1)
        attended = lax.all_gather(attended, "head", axis=1, tiled=True)
        output = jnp.dot(attended, out_weight, preferred_element_type=jnp.float32)
        return output.astype(jnp.bfloat16)
    first = None
    if chunks > 1:
        first = project(near[:-1] + far[:-1], None, out_weight, info, chunks, jnp.float32)
    return project(near[-1:] + far[-1:], first, out_weight, info, chunks, jnp.bfloat16)


def solution(mesh):
    placed = (
        P("ctx", "head"),
        P("ctx", "head"),
        P("ctx", "head"),
        P("head", None),
        P("head", None),
        P(None, "head"),
    )
    return jax.shard_map(
        body, mesh=mesh, in_specs=placed, out_specs=P("ctx", "head"), check_vma=False
    )
```

```python
import functools
import math

import jax
import jax.numpy as jnp
from jax import lax
from jax.experimental import pallas as pl
from jax.experimental.pallas import tpu as pltpu
from jax.sharding import PartitionSpec as P

HD = 128
BLK = 128
MAXOFF = 16
PLANE = 4
MASKED = -1e30
SMALLEST, LARGEST = 2.0**-60, 2.0**100
VMEM_LIMIT = 56 * 1024 * 1024


def shifted(value, by):
    size = lax.axis_size("ctx")
    return lax.ppermute(value, "ctx", [(i, i + by) for i in range(size - by)])


def crossed(value, bits):
    size = lax.axis_size("ctx")
    return lax.ppermute(value, "ctx", [(i, i ^ bits) for i in range(size)])


def prepare_kernel(cfg, info, vert, *refs):
    pair, local, heads, plane, per_chunk = cfg
    chip, core = info[0], info[1]
    keys, values = refs[:2]
    refs = refs[2:]
    other = None
    if pair > 1:
        other, refs = refs[0], refs[1:]
    n_chunks = heads // per_chunk
    chip_outs, refs = refs[:n_chunks], refs[n_chunks:]
    list_outs, chip_kv = refs[:plane], refs[plane]
    n_vert = vert.shape[1]
    dev_rows = local * BLK
    chip_blocks = pair * local
    for e in range(heads):
        at = pl.multiple_of((core * heads + e) * HD, HD)
        chip_kv[e, :dev_rows, HD:] = values[:, pl.ds(at, HD)]
        if pair > 1:
            chip_kv[e, dev_rows:, HD:] = other[:, (heads + e) * HD : (heads + e + 1) * HD]
        for b in range(pair * local):
            rows = slice(b % local * BLK, (b % local + 1) * BLK)
            block = keys[rows, pl.ds(at, HD)] if b < local else other[rows, e * HD : (e + 1) * HD]
            chip_kv[e, b * BLK : (b + 1) * BLK, :HD] = block.T
        c, at = divmod(e, per_chunk)
        chip_outs[c][:, at * 2 * HD : (at + 1) * 2 * HD] = chip_kv[e]
    per = heads * n_vert // plane
    for k in range(plane):
        for i in range(per):
            flat = (chip % plane ^ k) * per + i
            e, j = flat // n_vert, flat % n_vert
            block = vert[e, j]
            within = block % chip_blocks
            if pair > 1:
                within = (within // local ^ core) * local + within % local
            rows = slice(i * BLK, (i + 1) * BLK)
            owned = block // chip_blocks == chip
            found = chip_kv[e, pl.ds(pl.multiple_of(within * BLK, BLK), BLK), :]
            list_outs[k][rows, :] = jnp.where(owned, found, jnp.zeros_like(found))


def prepare(info, vert, keys, values, other, heads, local, plane, per_chunk):
    pair = 1 if other is None else 2
    chip_rows = pair * local * BLK
    n_chunks = heads // per_chunk
    per = heads * vert.shape[1] // plane
    dtype = keys.dtype
    smem = pl.BlockSpec(memory_space=pltpu.SMEM)
    vmem = pl.BlockSpec(memory_space=pltpu.VMEM)
    data = [keys, values] + ([] if other is None else [other])
    specs = [vmem] * 2
    if other is not None:
        specs.append(pl.BlockSpec((other.shape[0], heads * 2 * HD), lambda i: (0, 0)))
    outs = pl.pallas_call(
        functools.partial(prepare_kernel, (pair, local, heads, plane, per_chunk)),
        grid=(1,),
        in_specs=[smem] * 2 + specs,
        out_specs=[vmem] * (n_chunks + plane),
        out_shape=[jax.ShapeDtypeStruct((chip_rows, per_chunk * 2 * HD), dtype)] * n_chunks
        + [jax.ShapeDtypeStruct((per * BLK, 2 * HD), dtype)] * plane,
        scratch_shapes=[pltpu.VMEM((heads, chip_rows, 2 * HD), dtype)],
        compiler_params=pltpu.CompilerParams(vmem_limit_bytes=VMEM_LIMIT),
        cost_estimate=pl.CostEstimate(
            flops=0, bytes_accessed=8 * heads * chip_rows * 2 * HD, transcendentals=0
        ),
        name="prepare",
    )(info, vert, *data)
    return list(outs[:n_chunks]), list(outs[n_chunks:])


def onehot_rows(shape, at, dtype):
    row = lax.broadcasted_iota(jnp.int32, shape, 0)
    col = lax.broadcasted_iota(jnp.int32, shape, 1)
    return jnp.where(col == at(row), 1.0, 0.0).astype(dtype)


def exponentials(q, k, factor):
    return jnp.exp2(jnp.dot(q, k, preferred_element_type=jnp.float32) * factor)


def pipelined(blocks, stage):
    stage(0, 0, blocks > 1, False)

    def two_blocks(n, carry):
        stage(2 * n + 1, 1, True, True)
        stage(2 * n + 2, 0, True, True)
        return carry

    inner = max(blocks - 2, 0) // 2
    lax.fori_loop(0, inner, two_blocks, 0)
    for i in range(2 * inner + 1, blocks):
        stage(i, i % 2, i + 1 < blocks, True)
    stage(blocks, blocks % 2, False, True)


def slash_kernel(cfg, info, slash, *refs):
    first, pair, local, group, reach, n_slash = cfg
    q_refs, refs = refs[:pair], refs[pair:]
    w_refs, refs = refs[: reach + 1], refs[reach + 1 :]
    masks, acc, win, qx = refs[:4]
    kgs, vgs, ps = refs[4:6], refs[6:8], refs[8:10]
    e = first + pl.program_id(0)
    chip, core = info[0], info[1]
    dev_rows = local * BLK
    chip_blocks = pair * local
    chip_rows = chip_blocks * BLK
    width = n_slash * BLK
    factor = math.log2(math.e) / math.sqrt(HD)

    for back in range(reach + 1):
        for slot in range(pair):
            owner = core ^ slot if pair > 1 else 0
            at = pl.multiple_of((reach - back) * chip_rows + owner * dev_rows, dev_rows)
            rows = slice(slot * dev_rows, (slot + 1) * dev_rows)
            win[pl.ds(at, dev_rows), :] = w_refs[back][rows, :]
    for vg in vgs:
        vg[:, HD:] = jnp.ones((width, HD), vg.dtype)
    eye = onehot_rows((BLK, HD), lambda row: row, qx.dtype)
    for i in range(chip_blocks):
        slot, b = divmod(i, local)
        for g in range(group):
            rows = slice(g * BLK, (g + 1) * BLK)
            qx[i, rows, :HD] = q_refs[slot][b * BLK : (b + 1) * BLK, g * HD : (g + 1) * HD]
            qx[i, rows, HD:] = eye

    def within(i):
        return (core ^ i // local) * local + i % local if pair > 1 else i

    def take(i, j):
        src = (reach * chip_blocks + within(i) - slash[e, j]) * BLK
        return pl.ds(pl.multiple_of(src, BLK), BLK)

    def place_keys(i, at):
        here = chip * chip_blocks + within(i)
        for j in range(n_slash):
            off = slash[e, j]
            cols = slice(j * BLK, (j + 1) * BLK)
            kgs[at][:HD, cols] = win[take(i, j), :HD]
            kgs[at][HD:, cols] = masks[jnp.where(off > here, 2, jnp.where(off == 0, 1, 0))]

    def stage(i, at, ahead, behind):
        if ahead:
            place_keys(i + 1, 1 - at)
        if behind:
            acc[i - 1] = jnp.dot(
                ps[1 - at][...], vgs[1 - at][...], preferred_element_type=jnp.float32
            )
        if isinstance(i, int) and i == chip_blocks:
            return
        for j in range(n_slash):
            vgs[at][j * BLK : (j + 1) * BLK, :HD] = win[take(i, j), HD:]
        ps[at][...] = exponentials(qx[i], kgs[at][...], factor).astype(ps[at].dtype)

    place_keys(0, 0)
    pipelined(chip_blocks, stage)


def vertical_kernel(cfg, info, vert, slash, *refs):
    first, pair, local, group, reach, n_slash, n_vert, plane, heads = cfg
    q_refs, refs = refs[:pair], refs[pair:]
    w_refs, refs = refs[: reach + 1], refs[reach + 1 :]
    before, kv_vert, masks, refs = refs[0], refs[1], refs[2], refs[3:]
    out_refs, refs = refs[:pair], refs[pair:]
    ke, ve, qx, res, good = refs[:5]
    ps, (kg, vg, sc, pg) = refs[5:7], refs[7:]
    e = first + pl.program_id(0)
    chip, core = info[0], info[1]
    dev_rows = local * BLK
    chip_blocks = pair * local
    wide = n_vert * BLK
    step = min(2 * BLK, wide)
    factor = math.log2(math.e) / math.sqrt(HD)

    def within(i):
        return (core ^ i // local) * local + i % local if pair > 1 else i

    def hidden(i, j):
        here = chip * chip_blocks + within(i)
        found = vert[e, j] >= here
        for u in range(n_slash):
            found = found | (vert[e, j] == here - slash[e, u])
        return found

    per = heads * n_vert // plane
    row = lax.broadcasted_iota(jnp.int32, (HD, BLK), 0)
    for j in range(n_vert):
        flat = e * n_vert + j
        src = pl.multiple_of(((flat // per ^ chip % plane) * per + flat % per) * BLK, BLK)
        rows = slice(j * BLK, (j + 1) * BLK)
        ke[:HD, rows] = kv_vert[pl.ds(src, BLK), :HD]
        ve[rows, :HD] = kv_vert[pl.ds(src, BLK), HD:]
        bias = jnp.zeros((HD, BLK), jnp.float32)
        for i in range(chip_blocks):
            bias = jnp.where((row == i) & hidden(i, j), MASKED, bias)
        ke[HD:, rows] = bias.astype(ke.dtype)
    ve[:, HD:] = jnp.ones((wide, HD), ve.dtype)
    for i in range(chip_blocks):
        slot, b = divmod(i, local)
        for g in range(group):
            rows = slice(g * BLK, (g + 1) * BLK)
            qx[i, rows, :HD] = q_refs[slot][b * BLK : (b + 1) * BLK, g * HD : (g + 1) * HD]
            qx[i, rows, HD:] = onehot_rows((BLK, HD), lambda row, i=i: i, qx.dtype)
    good[...] = jnp.ones(good.shape, good.dtype)

    def stage(i, at, ahead, behind):
        if behind:
            acc = before[i - 1] + jnp.dot(
                ps[1 - at][...], ve[...], preferred_element_type=jnp.float32
            )
            total = acc[:, HD:]
            res[i - 1] = (acc[:, :HD] / total).astype(res.dtype)
            fine = jnp.where((total > SMALLEST) & (total < LARGEST), 1.0, 0.0)
            good[...] = jnp.minimum(good[...], jnp.min(fine, axis=0, keepdims=True))
        if isinstance(i, int) and i == chip_blocks:
            return
        ps[at][...] = exponentials(qx[i], ke[...], factor).astype(ps[at].dtype)

    pipelined(chip_blocks, stage)

    @pl.when(jnp.logical_not(jnp.min(good[...]) > 0.5))
    def _():
        vg[: n_slash * BLK, HD:] = jnp.ones((n_slash * BLK, HD), vg.dtype)
        kg[:, n_slash * BLK :] = ke[...]
        vg[n_slash * BLK :, :] = ve[...]
        eye = onehot_rows((BLK, HD), lambda row: row, qx.dtype)

        def shifted_block(i, carry):
            here = chip * chip_blocks + within(i)
            for g in range(group):
                qx[i, g * BLK : (g + 1) * BLK, HD:] = eye
            for j in range(n_slash):
                off = slash[e, j]
                pos = reach * chip_blocks + within(i) - off
                back = reach - pos // chip_blocks
                src = pos % chip_blocks
                if pair > 1:
                    src = (src // local ^ core) * local + src % local
                at = pl.ds(pl.multiple_of(src * BLK, BLK), BLK)
                found = w_refs[0][at, :]
                for d in range(1, reach + 1):
                    found = jnp.where(back == d, w_refs[d][at, :], found)
                rows = slice(j * BLK, (j + 1) * BLK)
                kg[:HD, rows] = found[:, :HD]
                vg[rows, :HD] = found[:, HD:]
                kg[HD:, rows] = masks[jnp.where(off > here, 2, jnp.where(off == 0, 1, 0))]
            for j in range(n_vert):
                rows = slice((n_slash + j) * BLK, (n_slash + j + 1) * BLK)
                kg[HD:, rows] = masks[jnp.where(hidden(i, j), 2, 0)]
            top = None
            for t in range(0, kg.shape[1], step):
                s = jnp.dot(qx[i], kg[:, t : t + step], preferred_element_type=jnp.float32)
                sc[:, t : t + step] = s
                for u in range(0, step, HD):
                    piece = s[:, u : u + HD]
                    top = piece if top is None else jnp.maximum(top, piece)
            top = jnp.max(top, axis=1, keepdims=True)
            for t in range(0, kg.shape[1], step):
                p = jnp.exp2((sc[:, t : t + step] - top) * factor)
                pg[:, t : t + step] = p.astype(pg.dtype)
            acc = jnp.dot(pg[...], vg[...], preferred_element_type=jnp.float32)
            res[i] = (acc[:, :HD] / acc[:, HD:]).astype(res.dtype)
            return carry

        lax.fori_loop(0, chip_blocks, shifted_block, 0)

    for i in range(chip_blocks):
        slot, b = divmod(i, local)
        for g in range(group):
            out_refs[slot][b * BLK : (b + 1) * BLK, g * HD : (g + 1) * HD] = res[
                i, g * BLK : (g + 1) * BLK
            ]


class Attention:
    def __init__(self, queries, q_other, info, vert, slash, masks, heads, local, plane):
        self.pair = 1 if q_other is None else 2
        self.qs = [queries] if q_other is None else [queries, q_other]
        self.info, self.vert, self.slash, self.masks = info, vert, slash, masks
        self.heads, self.local, self.plane = heads, local, plane
        self.dev_rows = queries.shape[0]
        self.wide = queries.shape[1] // (self.pair * heads)
        self.group = self.wide // HD
        self.blocks = self.pair * local
        self.dtype = queries.dtype

    def specs(self, first, windows):
        heads, shape = self.heads, (self.dev_rows, self.wide)
        specs = [pl.BlockSpec(shape, lambda i, info, *_: (0, info[1] * heads + first + i))]
        if self.pair > 1:
            at = self.qs[1].shape[1] // self.wide - heads + first
            specs.append(pl.BlockSpec(shape, lambda i, *_: (0, at + i)))
        return specs + [pl.BlockSpec((w.shape[0], 2 * HD), lambda i, *_: (0, i)) for w in windows]

    def whole(self, a):
        return pl.BlockSpec(a.shape, lambda i, *_: (0,) * a.ndim)

    def cost(self, n, width, more):
        rows = n * self.blocks * self.group * BLK
        return pl.CostEstimate(
            flops=8 * rows * width * HD,
            bytes_accessed=rows * HD * 2 + more,
            transcendentals=rows * width,
        )

    def acc_spec(self):
        shape = (self.blocks, self.group * BLK, 2 * HD)
        return pl.BlockSpec((None, *shape), lambda i, *_: (i, 0, 0, 0))

    def over_slash(self, first, n, windows):
        n_slash = self.slash.shape[1]
        width, rows = n_slash * BLK, self.group * BLK
        shape = (n, self.blocks, rows, 2 * HD)
        cfg = (first, self.pair, self.local, self.group, len(windows) - 1, n_slash)
        return pl.pallas_call(
            functools.partial(slash_kernel, cfg),
            grid_spec=pltpu.PrefetchScalarGridSpec(
                num_scalar_prefetch=2,
                grid=(n,),
                in_specs=self.specs(first, windows) + [self.whole(self.masks)],
                out_specs=self.acc_spec(),
                scratch_shapes=[
                    pltpu.VMEM((sum(w.shape[0] for w in windows), 2 * HD), self.dtype),
                    pltpu.VMEM((self.blocks, rows, 2 * HD), self.dtype),
                ]
                + [pltpu.VMEM((2 * HD, width), self.dtype)] * 2
                + [pltpu.VMEM((width, 2 * HD), self.dtype)] * 2
                + [pltpu.VMEM((rows, width), self.dtype)] * 2,
            ),
            out_shape=jax.ShapeDtypeStruct(shape, jnp.float32),
            compiler_params=pltpu.CompilerParams(vmem_limit_bytes=VMEM_LIMIT),
            cost_estimate=self.cost(n, width, 4 * math.prod(shape)),
            name="attend_slash",
        )(self.info, self.slash, *self.qs, *windows, self.masks)

    def over_vertical(self, first, n, windows, before, kv_vert):
        n_slash, n_vert = self.slash.shape[1], self.vert.shape[1]
        width, both, rows = n_vert * BLK, (n_slash + n_vert) * BLK, self.group * BLK
        cfg = (first, self.pair, self.local, self.group, len(windows) - 1, n_slash, n_vert)
        out = pl.BlockSpec((self.dev_rows, self.wide), lambda i, *_: (0, i))
        return pl.pallas_call(
            functools.partial(vertical_kernel, cfg + (self.plane, self.heads)),
            grid_spec=pltpu.PrefetchScalarGridSpec(
                num_scalar_prefetch=3,
                grid=(n,),
                in_specs=self.specs(first, windows)
                + [self.acc_spec(), self.whole(kv_vert), self.whole(self.masks)],
                out_specs=[out] * self.pair,
                scratch_shapes=[
                    pltpu.VMEM((2 * HD, width), self.dtype),
                    pltpu.VMEM((width, 2 * HD), self.dtype),
                    pltpu.VMEM((self.blocks, rows, 2 * HD), self.dtype),
                    pltpu.VMEM((self.blocks, rows, HD), self.dtype),
                    pltpu.VMEM((1, HD), jnp.float32),
                    pltpu.VMEM((rows, width), self.dtype),
                    pltpu.VMEM((rows, width), self.dtype),
                    pltpu.VMEM((2 * HD, both), self.dtype),
                    pltpu.VMEM((both, 2 * HD), self.dtype),
                    pltpu.VMEM((rows, both), jnp.float32),
                    pltpu.VMEM((rows, both), self.dtype),
                ],
            ),
            out_shape=[jax.ShapeDtypeStruct((self.dev_rows, n * self.wide), self.dtype)]
            * self.pair,
            compiler_params=pltpu.CompilerParams(vmem_limit_bytes=VMEM_LIMIT),
            cost_estimate=self.cost(n, width, 4 * math.prod(before.shape)),
            name="attend_vertical",
        )(self.info, self.vert, self.slash, *self.qs, *windows, before, kv_vert, self.masks)


def project_kernel(n, has_before, info, *refs):
    lefts, rights, refs = refs[:n], refs[n : 2 * n], refs[2 * n :]
    acc = refs[0][...] if has_before else None
    for left, right in zip(lefts, rights):
        part = jnp.dot(left[...], right[...], preferred_element_type=jnp.float32)
        acc = part if acc is None else acc + part
    refs[-1][...] = acc.astype(refs[-1].dtype)


def project(pieces, before, out_weight, info, chunks, dtype):
    rows, wide = pieces[0][2].shape
    columns = out_weight.shape[1]
    tile = min(1024, columns)
    n = len(pieces)

    def weight_spec(swap, c):
        if swap:
            return pl.BlockSpec((wide, tile), lambda i, info: ((1 - info[1]) * chunks + c, i))
        return pl.BlockSpec((wide, tile), lambda i, info: (info[1] * chunks + c, i))

    in_specs = [pl.BlockSpec((rows, wide), lambda i, info: (0, 0))] * n
    in_specs += [weight_spec(swap, c) for swap, c, _ in pieces]
    args = [a for _, _, a in pieces] + [out_weight] * n
    out_spec = pl.BlockSpec((rows, tile), lambda i, info: (0, i))
    if before is not None:
        in_specs.append(out_spec)
        args.append(before)
    return pl.pallas_call(
        functools.partial(project_kernel, n, before is not None),
        grid_spec=pltpu.PrefetchScalarGridSpec(
            num_scalar_prefetch=1, grid=(columns // tile,), in_specs=in_specs, out_specs=out_spec
        ),
        out_shape=jax.ShapeDtypeStruct((rows, columns), dtype),
        compiler_params=pltpu.CompilerParams(vmem_limit_bytes=VMEM_LIMIT),
        cost_estimate=pl.CostEstimate(
            flops=2 * n * rows * wide * columns,
            bytes_accessed=2 * n * wide * (rows + columns) + 8 * rows * columns,
            transcendentals=0,
        ),
        name="project",
    )(info, *args)


def body(queries, keys, values, vertical_blocks, slash_offsets, out_weight):
    tokens_dev = queries.shape[0]
    kv_heads = keys.shape[1] // HD
    local = tokens_dev // BLK
    size = lax.axis_size("ctx")
    pair = 2 if kv_heads % 2 == 0 and size % 2 == 0 and lax.axis_size("head") == 1 else 1
    chips = size // pair
    heads = kv_heads // pair
    plane = PLANE if chips % PLANE == 0 and heads * vertical_blocks.shape[1] % PLANE == 0 else 1
    chip_blocks = pair * local
    reach = -(-MAXOFF // chip_blocks)
    index = lax.axis_index("ctx")
    chip, core = index // pair, index % pair
    info = jnp.stack([chip, core]).astype(jnp.int32)
    pos = jnp.arange(BLK)
    causal = jnp.where(pos[:, None] < pos[None, :], MASKED, 0.0)
    masks = jnp.stack([jnp.zeros_like(causal), causal, jnp.full_like(causal, MASKED)])
    masks = masks.astype(queries.dtype)

    def part(value, axis, which):
        span = value.shape[axis] // pair
        return lax.dynamic_slice_in_dim(value, which * span, span, axis)

    vert, slash = part(vertical_blocks, 0, core), part(slash_offsets, 0, core)
    kv_other = None
    if pair == 2:
        kv_other = crossed(jnp.concatenate([part(a, 1, 1 - core) for a in (keys, values)], 1), 1)
    per_chunk = 2 if heads % 2 == 0 else 1
    own, listed = prepare(info, vert, keys, values, kv_other, heads, local, plane, per_chunk)

    total = listed[0]
    for k in range(1, plane):
        total = total + crossed(listed[k], k * pair)
    q_sent = part(queries, 1, 1 - core) if pair == 2 else None
    total, own[0], q_sent = lax.optimization_barrier((total, own[0], q_sent))
    q_other = crossed(q_sent, 1) if pair == 2 else None
    step = 1
    while step < chips // plane:
        total = total + shifted(total, step * plane * pair)
        total, q_other = lax.optimization_barrier((total, q_other))
        step *= 2
    total, own[1:] = lax.optimization_barrier((total, own[1:]))

    attention = Attention(queries, q_other, info, vert, slash, masks, heads, local, plane)
    chunks = heads // per_chunk
    all_windows, sums = [], []
    for c in range(chunks):
        windows = [own[c]]
        if pair == 2 and reach == 2 and chips % 2 == 0:
            two_back = shifted(own[c], 2 * pair)
            passed = jnp.where(chip % 2 == 0, own[c], two_back)
            windows += [crossed(passed, pair), two_back]
        else:
            windows += [shifted(own[c], pair * d) for d in range(1, reach + 1)]
        all_windows.append(windows)
        sums.append(attention.over_slash(c * per_chunk, per_chunk, windows))
    gathered = [total] + [crossed(total, k * pair) for k in range(1, plane)]
    gathered, sums[0] = lax.optimization_barrier((gathered, sums[0]))
    kv_vert = jnp.concatenate(gathered, 0)
    near, far = [], []
    for c in range(chunks):
        att = attention.over_vertical(c * per_chunk, per_chunk, all_windows[c], sums[c], kv_vert)
        near.append((False, c, att[0]))
        if pair == 2:
            far.append((True, c, crossed(att[1], 1)))
    if pair == 1:
        attended = jnp.concatenate([a for _, _, a in near], 1)
        attended = lax.all_gather(attended, "head", axis=1, tiled=True)
        output = jnp.dot(attended, out_weight, preferred_element_type=jnp.float32)
        return output.astype(jnp.bfloat16)
    first = None
    if chunks > 1:
        first = project(near[:-1] + far[:-1], None, out_weight, info, chunks, jnp.float32)
    return project(near[-1:] + far[-1:], first, out_weight, info, chunks, jnp.bfloat16)


def solution(mesh):
    placed = (
        P("ctx", "head"),
        P("ctx", "head"),
        P("ctx", "head"),
        P("head", None),
        P("head", None),
        P(None, "head"),
    )
    return jax.shard_map(
        body, mesh=mesh, in_specs=placed, out_specs=P("ctx", "head"), check_vma=False
    )
```

```python
import functools
import math

import jax
import jax.numpy as jnp
from jax import lax
from jax.experimental import pallas as pl
from jax.experimental.pallas import tpu as pltpu
from jax.sharding import PartitionSpec as P

HD = 128
BLK = 128
MAXOFF = 16
PLANE = 4
MASKED = -1e30
SMALLEST, LARGEST = 2.0**-60, 2.0**100
VMEM_LIMIT = 56 * 1024 * 1024


def shifted(value, by):
    size = lax.axis_size("ctx")
    return lax.ppermute(value, "ctx", [(i, i + by) for i in range(size - by)])


def crossed(value, bits):
    size = lax.axis_size("ctx")
    return lax.ppermute(value, "ctx", [(i, i ^ bits) for i in range(size)])


def prepare_kernel(cfg, info, vert, *refs):
    pair, local, heads, plane, per_chunk = cfg
    chip, core = info[0], info[1]
    keys, values = refs[:2]
    refs = refs[2:]
    other = None
    if pair > 1:
        other, refs = refs[0], refs[1:]
    n_chunks = heads // per_chunk
    chip_outs, refs = refs[:n_chunks], refs[n_chunks:]
    list_outs, chip_kv = refs[:plane], refs[plane]
    n_vert = vert.shape[1]
    dev_rows = local * BLK
    chip_blocks = pair * local
    for e in range(heads):
        at = pl.multiple_of((core * heads + e) * HD, HD)
        chip_kv[e, :dev_rows, HD:] = values[:, pl.ds(at, HD)]
        if pair > 1:
            chip_kv[e, dev_rows:, HD:] = other[:, (heads + e) * HD : (heads + e + 1) * HD]
        for b in range(pair * local):
            rows = slice(b % local * BLK, (b % local + 1) * BLK)
            block = keys[rows, pl.ds(at, HD)] if b < local else other[rows, e * HD : (e + 1) * HD]
            chip_kv[e, b * BLK : (b + 1) * BLK, :HD] = block.T
        c, at = divmod(e, per_chunk)
        chip_outs[c][:, at * 2 * HD : (at + 1) * 2 * HD] = chip_kv[e]
    per = heads * n_vert // plane
    for k in range(plane):
        for i in range(per):
            flat = (chip % plane ^ k) * per + i
            e, j = flat // n_vert, flat % n_vert
            block = vert[e, j]
            within = block % chip_blocks
            if pair > 1:
                within = (within // local ^ core) * local + within % local
            rows = slice(i * BLK, (i + 1) * BLK)
            owned = block // chip_blocks == chip
            found = chip_kv[e, pl.ds(pl.multiple_of(within * BLK, BLK), BLK), :]
            list_outs[k][rows, :] = jnp.where(owned, found, jnp.zeros_like(found))


def prepare(info, vert, keys, values, other, heads, local, plane, per_chunk):
    pair = 1 if other is None else 2
    chip_rows = pair * local * BLK
    n_chunks = heads // per_chunk
    per = heads * vert.shape[1] // plane
    dtype = keys.dtype
    smem = pl.BlockSpec(memory_space=pltpu.SMEM)
    vmem = pl.BlockSpec(memory_space=pltpu.VMEM)
    data = [keys, values] + ([] if other is None else [other])
    specs = [vmem] * 2
    if other is not None:
        specs.append(pl.BlockSpec((other.shape[0], heads * 2 * HD), lambda i: (0, 0)))
    outs = pl.pallas_call(
        functools.partial(prepare_kernel, (pair, local, heads, plane, per_chunk)),
        grid=(1,),
        in_specs=[smem] * 2 + specs,
        out_specs=[vmem] * (n_chunks + plane),
        out_shape=[jax.ShapeDtypeStruct((chip_rows, per_chunk * 2 * HD), dtype)] * n_chunks
        + [jax.ShapeDtypeStruct((per * BLK, 2 * HD), dtype)] * plane,
        scratch_shapes=[pltpu.VMEM((heads, chip_rows, 2 * HD), dtype)],
        compiler_params=pltpu.CompilerParams(vmem_limit_bytes=VMEM_LIMIT),
        cost_estimate=pl.CostEstimate(
            flops=0, bytes_accessed=8 * heads * chip_rows * 2 * HD, transcendentals=0
        ),
        name="prepare",
    )(info, vert, *data)
    return list(outs[:n_chunks]), list(outs[n_chunks:])


def soften(q, k, bias, p_ref, group, factor):
    s = jnp.dot(q, k, preferred_element_type=jnp.float32)
    totals = []
    for g in range(group):
        rows = slice(g * BLK, (g + 1) * BLK)
        total = None
        for j in range(k.shape[1] // BLK):
            cols = slice(j * BLK, (j + 1) * BLK)
            p = jnp.exp2(s[rows, cols] * factor + bias(j))
            p_ref[rows, cols] = p.astype(p_ref.dtype)
            total = p if total is None else total + p
        totals.append(total)
    return jnp.concatenate(totals, 0)


def pipelined(blocks, stage):
    stage(0, 0, blocks > 1, False)

    def two_blocks(n, carry):
        stage(2 * n + 1, 1, True, True)
        stage(2 * n + 2, 0, True, True)
        return carry

    inner = max(blocks - 2, 0) // 2
    lax.fori_loop(0, inner, two_blocks, 0)
    for i in range(2 * inner + 1, blocks):
        stage(i, i % 2, i + 1 < blocks, True)
    stage(blocks, blocks % 2, False, True)


def slash_kernel(cfg, info, slash, *refs):
    first, pair, local, group, reach, n_slash = cfg
    q_refs, refs = refs[:pair], refs[pair:]
    w_refs, refs = refs[: reach + 1], refs[reach + 1 :]
    masks, acc, win, qx = refs[:4]
    kgs, vgs, ps = refs[4:6], refs[6:8], refs[8:10]
    e = first + pl.program_id(0)
    chip, core = info[0], info[1]
    dev_rows = local * BLK
    chip_blocks = pair * local
    chip_rows = chip_blocks * BLK
    width = n_slash * BLK
    factor = math.log2(math.e) / math.sqrt(HD)

    for back in range(reach + 1):
        for slot in range(pair):
            owner = core ^ slot if pair > 1 else 0
            at = pl.multiple_of((reach - back) * chip_rows + owner * dev_rows, dev_rows)
            rows = slice(slot * dev_rows, (slot + 1) * dev_rows)
            win[pl.ds(at, dev_rows), :] = w_refs[back][rows, :]
    for i in range(chip_blocks):
        slot, b = divmod(i, local)
        for g in range(group):
            rows = slice(g * BLK, (g + 1) * BLK)
            qx[i, rows, :] = q_refs[slot][b * BLK : (b + 1) * BLK, g * HD : (g + 1) * HD]

    def within(i):
        return (core ^ i // local) * local + i % local if pair > 1 else i

    def take(i, j):
        src = (reach * chip_blocks + within(i) - slash[e, j]) * BLK
        return pl.ds(pl.multiple_of(src, BLK), BLK)

    def place_keys(i, at):
        for j in range(n_slash):
            kgs[at][:, j * BLK : (j + 1) * BLK] = win[take(i, j), :HD]

    def stage(i, at, ahead, behind):
        if ahead:
            place_keys(i + 1, 1 - at)
        if behind:
            acc[i - 1, :, :HD] = jnp.dot(
                ps[1 - at][...], vgs[1 - at][...], preferred_element_type=jnp.float32
            )
        if isinstance(i, int) and i == chip_blocks:
            return
        here = chip * chip_blocks + within(i)

        def bias(j):
            off = slash[e, j]
            return masks[jnp.where(off > here, 2, jnp.where(off == 0, 1, 0))]

        for j in range(n_slash):
            vgs[at][j * BLK : (j + 1) * BLK, :] = win[take(i, j), HD:]
        acc[i, :, HD:] = soften(qx[i], kgs[at][...], bias, ps[at], group, factor)

    place_keys(0, 0)
    pipelined(chip_blocks, stage)


def vertical_kernel(cfg, info, vert, slash, *refs):
    first, pair, local, group, reach, n_slash, n_vert, plane, heads = cfg
    q_refs, refs = refs[:pair], refs[pair:]
    w_refs, refs = refs[: reach + 1], refs[reach + 1 :]
    before, kv_vert, masks, refs = refs[0], refs[1], refs[2], refs[3:]
    out_refs, refs = refs[:pair], refs[pair:]
    ke, ve, qx, res, good = refs[:5]
    ps, sums, (kg, vg, sc, pg) = refs[5:7], refs[7:9], refs[9:]
    e = first + pl.program_id(0)
    chip, core = info[0], info[1]
    dev_rows = local * BLK
    chip_blocks = pair * local
    factor = math.log2(math.e) / math.sqrt(HD)

    def within(i):
        return (core ^ i // local) * local + i % local if pair > 1 else i

    def hidden(i, j):
        here = chip * chip_blocks + within(i)
        found = vert[e, j] >= here
        for u in range(n_slash):
            found = found | (vert[e, j] == here - slash[e, u])
        return found

    per = heads * n_vert // plane
    for j in range(n_vert):
        flat = e * n_vert + j
        src = pl.multiple_of(((flat // per ^ chip % plane) * per + flat % per) * BLK, BLK)
        rows = slice(j * BLK, (j + 1) * BLK)
        ke[:, rows] = kv_vert[pl.ds(src, BLK), :HD]
        ve[rows, :] = kv_vert[pl.ds(src, BLK), HD:]
    for i in range(chip_blocks):
        slot, b = divmod(i, local)
        for g in range(group):
            rows = slice(g * BLK, (g + 1) * BLK)
            qx[i, rows, :] = q_refs[slot][b * BLK : (b + 1) * BLK, g * HD : (g + 1) * HD]
    good[...] = jnp.ones(good.shape, good.dtype)

    def stage(i, at, ahead, behind):
        if behind:
            attended = before[i - 1, :, :HD] + jnp.dot(
                ps[1 - at][...], ve[...], preferred_element_type=jnp.float32
            )
            total = jnp.sum(sums[1 - at][...], axis=1, keepdims=True)
            res[i - 1] = (attended / total).astype(res.dtype)
            fine = jnp.where((total > SMALLEST) & (total < LARGEST), 1.0, 0.0)
            good[...] = jnp.minimum(good[...], jnp.min(fine, axis=0, keepdims=True))
        if isinstance(i, int) and i == chip_blocks:
            return

        def bias(j):
            return jnp.where(hidden(i, j), MASKED, 0.0)

        sums[at][...] = before[i, :, HD:] + soften(qx[i], ke[...], bias, ps[at], group, factor)

    pipelined(chip_blocks, stage)

    @pl.when(jnp.logical_not(jnp.min(good[...]) > 0.5))
    def _():
        kg[:, n_slash * BLK :] = ke[...]
        vg[n_slash * BLK :, :] = ve[...]

        def shifted_block(i, carry):
            here = chip * chip_blocks + within(i)
            biases = []
            for j in range(n_slash):
                off = slash[e, j]
                pos = reach * chip_blocks + within(i) - off
                back = reach - pos // chip_blocks
                src = pos % chip_blocks
                if pair > 1:
                    src = (src // local ^ core) * local + src % local
                at = pl.ds(pl.multiple_of(src * BLK, BLK), BLK)
                found = w_refs[0][at, :]
                for d in range(1, reach + 1):
                    found = jnp.where(back == d, w_refs[d][at, :], found)
                rows = slice(j * BLK, (j + 1) * BLK)
                kg[:, rows] = found[:, :HD]
                vg[rows, :] = found[:, HD:]
                biases.append(masks[jnp.where(off > here, 2, jnp.where(off == 0, 1, 0))])
            for j in range(n_vert):
                biases.append(jnp.where(hidden(i, j), MASKED, 0.0))
            sc[...] = jnp.dot(qx[i], kg[...], preferred_element_type=jnp.float32)
            for g in range(group):
                rows = slice(g * BLK, (g + 1) * BLK)
                top = None
                for j, bias in enumerate(biases):
                    cols = slice(j * BLK, (j + 1) * BLK)
                    sc[rows, cols] = sc[rows, cols] * factor + bias
                    top = sc[rows, cols] if top is None else jnp.maximum(top, sc[rows, cols])
                p = jnp.exp2(sc[rows, :] - jnp.max(top, axis=1, keepdims=True))
                pg[rows, :] = p.astype(pg.dtype)
                sums[0][rows, :] = jnp.broadcast_to(jnp.sum(p, axis=1, keepdims=True), (BLK, HD))
            acc = jnp.dot(pg[...], vg[...], preferred_element_type=jnp.float32)
            res[i] = (acc / sums[0][...]).astype(res.dtype)
            return carry

        lax.fori_loop(0, chip_blocks, shifted_block, 0)

    for i in range(chip_blocks):
        slot, b = divmod(i, local)
        for g in range(group):
            out_refs[slot][b * BLK : (b + 1) * BLK, g * HD : (g + 1) * HD] = res[
                i, g * BLK : (g + 1) * BLK
            ]


class Attention:
    def __init__(self, queries, q_other, info, vert, slash, masks, heads, local, plane):
        self.pair = 1 if q_other is None else 2
        self.qs = [queries] if q_other is None else [queries, q_other]
        self.info, self.vert, self.slash, self.masks = info, vert, slash, masks
        self.heads, self.local, self.plane = heads, local, plane
        self.dev_rows = queries.shape[0]
        self.wide = queries.shape[1] // (self.pair * heads)
        self.group = self.wide // HD
        self.blocks = self.pair * local
        self.dtype = queries.dtype

    def specs(self, first, windows):
        heads, shape = self.heads, (self.dev_rows, self.wide)
        specs = [pl.BlockSpec(shape, lambda i, info, *_: (0, info[1] * heads + first + i))]
        if self.pair > 1:
            at = self.qs[1].shape[1] // self.wide - heads + first
            specs.append(pl.BlockSpec(shape, lambda i, *_: (0, at + i)))
        return specs + [pl.BlockSpec((w.shape[0], 2 * HD), lambda i, *_: (0, i)) for w in windows]

    def whole(self, a):
        return pl.BlockSpec(a.shape, lambda i, *_: (0,) * a.ndim)

    def cost(self, n, width, more):
        rows = n * self.blocks * self.group * BLK
        return pl.CostEstimate(
            flops=8 * rows * width * HD,
            bytes_accessed=rows * HD * 2 + more,
            transcendentals=rows * width,
        )

    def acc_spec(self):
        shape = (self.blocks, self.group * BLK, 2 * HD)
        return pl.BlockSpec((None, *shape), lambda i, *_: (i, 0, 0, 0))

    def over_slash(self, first, n, windows):
        n_slash = self.slash.shape[1]
        width, rows = n_slash * BLK, self.group * BLK
        shape = (n, self.blocks, rows, 2 * HD)
        cfg = (first, self.pair, self.local, self.group, len(windows) - 1, n_slash)
        return pl.pallas_call(
            functools.partial(slash_kernel, cfg),
            grid_spec=pltpu.PrefetchScalarGridSpec(
                num_scalar_prefetch=2,
                grid=(n,),
                in_specs=self.specs(first, windows) + [self.whole(self.masks)],
                out_specs=self.acc_spec(),
                scratch_shapes=[
                    pltpu.VMEM((sum(w.shape[0] for w in windows), 2 * HD), self.dtype),
                    pltpu.VMEM((self.blocks, rows, HD), self.dtype),
                ]
                + [pltpu.VMEM((HD, width), self.dtype)] * 2
                + [pltpu.VMEM((width, HD), self.dtype)] * 2
                + [pltpu.VMEM((rows, width), self.dtype)] * 2,
            ),
            out_shape=jax.ShapeDtypeStruct(shape, jnp.float32),
            compiler_params=pltpu.CompilerParams(vmem_limit_bytes=VMEM_LIMIT),
            cost_estimate=self.cost(n, width, 4 * math.prod(shape)),
            name="attend_slash",
        )(self.info, self.slash, *self.qs, *windows, self.masks)

    def over_vertical(self, first, n, windows, before, kv_vert):
        n_slash, n_vert = self.slash.shape[1], self.vert.shape[1]
        width, both, rows = n_vert * BLK, (n_slash + n_vert) * BLK, self.group * BLK
        cfg = (first, self.pair, self.local, self.group, len(windows) - 1, n_slash, n_vert)
        out = pl.BlockSpec((self.dev_rows, self.wide), lambda i, *_: (0, i))
        return pl.pallas_call(
            functools.partial(vertical_kernel, cfg + (self.plane, self.heads)),
            grid_spec=pltpu.PrefetchScalarGridSpec(
                num_scalar_prefetch=3,
                grid=(n,),
                in_specs=self.specs(first, windows)
                + [self.acc_spec(), self.whole(kv_vert), self.whole(self.masks)],
                out_specs=[out] * self.pair,
                scratch_shapes=[
                    pltpu.VMEM((HD, width), self.dtype),
                    pltpu.VMEM((width, HD), self.dtype),
                    pltpu.VMEM((self.blocks, rows, HD), self.dtype),
                    pltpu.VMEM((self.blocks, rows, HD), self.dtype),
                    pltpu.VMEM((1, 1), jnp.float32),
                    pltpu.VMEM((rows, width), self.dtype),
                    pltpu.VMEM((rows, width), self.dtype),
                    pltpu.VMEM((rows, HD), jnp.float32),
                    pltpu.VMEM((rows, HD), jnp.float32),
                    pltpu.VMEM((HD, both), self.dtype),
                    pltpu.VMEM((both, HD), self.dtype),
                    pltpu.VMEM((rows, both), jnp.float32),
                    pltpu.VMEM((rows, both), self.dtype),
                ],
            ),
            out_shape=[jax.ShapeDtypeStruct((self.dev_rows, n * self.wide), self.dtype)]
            * self.pair,
            compiler_params=pltpu.CompilerParams(vmem_limit_bytes=VMEM_LIMIT),
            cost_estimate=self.cost(n, width, 4 * math.prod(before.shape)),
            name="attend_vertical",
        )(self.info, self.vert, self.slash, *self.qs, *windows, before, kv_vert, self.masks)


def project_kernel(n, has_before, info, *refs):
    lefts, rights, refs = refs[:n], refs[n : 2 * n], refs[2 * n :]
    acc = refs[0][...] if has_before else None
    for left, right in zip(lefts, rights):
        part = jnp.dot(left[...], right[...], preferred_element_type=jnp.float32)
        acc = part if acc is None else acc + part
    refs[-1][...] = acc.astype(refs[-1].dtype)


def project(pieces, before, out_weight, info, chunks, dtype):
    rows, wide = pieces[0][2].shape
    columns = out_weight.shape[1]
    tile = min(1024, columns)
    n = len(pieces)

    def weight_spec(swap, c):
        if swap:
            return pl.BlockSpec((wide, tile), lambda i, info: ((1 - info[1]) * chunks + c, i))
        return pl.BlockSpec((wide, tile), lambda i, info: (info[1] * chunks + c, i))

    in_specs = [pl.BlockSpec((rows, wide), lambda i, info: (0, 0))] * n
    in_specs += [weight_spec(swap, c) for swap, c, _ in pieces]
    args = [a for _, _, a in pieces] + [out_weight] * n
    out_spec = pl.BlockSpec((rows, tile), lambda i, info: (0, i))
    if before is not None:
        in_specs.append(out_spec)
        args.append(before)
    return pl.pallas_call(
        functools.partial(project_kernel, n, before is not None),
        grid_spec=pltpu.PrefetchScalarGridSpec(
            num_scalar_prefetch=1, grid=(columns // tile,), in_specs=in_specs, out_specs=out_spec
        ),
        out_shape=jax.ShapeDtypeStruct((rows, columns), dtype),
        compiler_params=pltpu.CompilerParams(vmem_limit_bytes=VMEM_LIMIT),
        cost_estimate=pl.CostEstimate(
            flops=2 * n * rows * wide * columns,
            bytes_accessed=2 * n * wide * (rows + columns) + 8 * rows * columns,
            transcendentals=0,
        ),
        name="project",
    )(info, *args)


def body(queries, keys, values, vertical_blocks, slash_offsets, out_weight):
    tokens_dev = queries.shape[0]
    kv_heads = keys.shape[1] // HD
    local = tokens_dev // BLK
    size = lax.axis_size("ctx")
    pair = 2 if kv_heads % 2 == 0 and size % 2 == 0 and lax.axis_size("head") == 1 else 1
    chips = size // pair
    heads = kv_heads // pair
    plane = PLANE if chips % PLANE == 0 and heads * vertical_blocks.shape[1] % PLANE == 0 else 1
    chip_blocks = pair * local
    reach = -(-MAXOFF // chip_blocks)
    index = lax.axis_index("ctx")
    chip, core = index // pair, index % pair
    info = jnp.stack([chip, core]).astype(jnp.int32)
    pos = jnp.arange(BLK)
    causal = jnp.where(pos[:, None] < pos[None, :], MASKED, 0.0)
    masks = jnp.stack([jnp.zeros_like(causal), causal, jnp.full_like(causal, MASKED)])

    def part(value, axis, which):
        span = value.shape[axis] // pair
        return lax.dynamic_slice_in_dim(value, which * span, span, axis)

    vert, slash = part(vertical_blocks, 0, core), part(slash_offsets, 0, core)
    kv_other = None
    if pair == 2:
        kv_other = crossed(jnp.concatenate([part(a, 1, 1 - core) for a in (keys, values)], 1), 1)
    per_chunk = 2 if heads % 2 == 0 else 1
    own, listed = prepare(info, vert, keys, values, kv_other, heads, local, plane, per_chunk)

    total = listed[0]
    for k in range(1, plane):
        total = total + crossed(listed[k], k * pair)
    q_sent = part(queries, 1, 1 - core) if pair == 2 else None
    total, own[0], q_sent = lax.optimization_barrier((total, own[0], q_sent))
    q_other = crossed(q_sent, 1) if pair == 2 else None
    step = 1
    while step < chips // plane:
        total = total + shifted(total, step * plane * pair)
        if step == 1:
            total, q_other, own[1:] = lax.optimization_barrier((total, q_other, own[1:]))
        step *= 2

    attention = Attention(queries, q_other, info, vert, slash, masks, heads, local, plane)
    chunks = heads // per_chunk
    all_windows, sums = [], []
    for c in range(chunks):
        windows = [own[c]]
        if pair == 2 and reach == 2 and chips % 2 == 0:
            two_back = shifted(own[c], 2 * pair)
            passed = jnp.where(chip % 2 == 0, own[c], two_back)
            windows += [crossed(passed, pair), two_back]
        else:
            windows += [shifted(own[c], pair * d) for d in range(1, reach + 1)]
        all_windows.append(windows)
        sums.append(attention.over_slash(c * per_chunk, per_chunk, windows))
    gathered = [total] + [crossed(total, k * pair) for k in range(1, plane)]
    gathered, sums[0] = lax.optimization_barrier((gathered, sums[0]))
    kv_vert = jnp.concatenate(gathered, 0)
    near, far = [], []
    for c in range(chunks):
        att = attention.over_vertical(c * per_chunk, per_chunk, all_windows[c], sums[c], kv_vert)
        near.append((False, c, att[0]))
        if pair == 2:
            far.append((True, c, crossed(att[1], 1)))
    if pair == 1:
        attended = jnp.concatenate([a for _, _, a in near], 1)
        attended = lax.all_gather(attended, "head", axis=1, tiled=True)
        output = jnp.dot(attended, out_weight, preferred_element_type=jnp.float32)
        return output.astype(jnp.bfloat16)
    first = None
    if chunks > 1:
        first = project(near[:-1] + far[:-1], None, out_weight, info, chunks, jnp.float32)
    return project(near[-1:] + far[-1:], first, out_weight, info, chunks, jnp.bfloat16)


def solution(mesh):
    placed = (
        P("ctx", "head"),
        P("ctx", "head"),
        P("ctx", "head"),
        P("head", None),
        P("head", None),
        P(None, "head"),
    )
    return jax.shard_map(
        body, mesh=mesh, in_specs=placed, out_specs=P("ctx", "head"), check_vma=False
    )
```

```python
import functools
import math

import jax
import jax.numpy as jnp
from jax import lax
from jax.experimental import pallas as pl
from jax.experimental.pallas import tpu as pltpu
from jax.sharding import PartitionSpec as P

HD = 128
BLK = 128
MAXOFF = 16
PLANE = 4
MASKED = -1e30
SMALLEST, LARGEST = 2.0**-60, 2.0**100
VMEM_LIMIT = 56 * 1024 * 1024


def shifted(value, by):
    size = lax.axis_size("ctx")
    return lax.ppermute(value, "ctx", [(i, i + by) for i in range(size - by)])


def crossed(value, bits):
    size = lax.axis_size("ctx")
    return lax.ppermute(value, "ctx", [(i, i ^ bits) for i in range(size)])


def prepare_kernel(cfg, info, vert, *refs):
    pair, local, heads, plane, per_chunk = cfg
    chip, core = info[0], info[1]
    keys, values = refs[:2]
    refs = refs[2:]
    other = None
    if pair > 1:
        other, refs = refs[0], refs[1:]
    n_chunks = heads // per_chunk
    chip_outs, refs = refs[:n_chunks], refs[n_chunks:]
    list_outs, chip_kv = refs[:plane], refs[plane]
    n_vert = vert.shape[1]
    dev_rows = local * BLK
    chip_blocks = pair * local
    for e in range(heads):
        at = pl.multiple_of((core * heads + e) * HD, HD)
        chip_kv[e, :dev_rows, HD:] = values[:, pl.ds(at, HD)]
        if pair > 1:
            chip_kv[e, dev_rows:, HD:] = other[:, (heads + e) * HD : (heads + e + 1) * HD]
        for b in range(pair * local):
            rows = slice(b % local * BLK, (b % local + 1) * BLK)
            block = keys[rows, pl.ds(at, HD)] if b < local else other[rows, e * HD : (e + 1) * HD]
            chip_kv[e, b * BLK : (b + 1) * BLK, :HD] = block.T
        c, at = divmod(e, per_chunk)
        chip_outs[c][:, at * 2 * HD : (at + 1) * 2 * HD] = chip_kv[e]
    per = heads * n_vert // plane
    for k in range(plane):
        for i in range(per):
            flat = (chip % plane ^ k) * per + i
            e, j = flat // n_vert, flat % n_vert
            block = vert[e, j]
            within = block % chip_blocks
            if pair > 1:
                within = (within // local ^ core) * local + within % local
            rows = slice(i * BLK, (i + 1) * BLK)
            owned = block // chip_blocks == chip
            found = chip_kv[e, pl.ds(pl.multiple_of(within * BLK, BLK), BLK), :]
            list_outs[k][rows, :] = jnp.where(owned, found, jnp.zeros_like(found))


def prepare(info, vert, keys, values, other, heads, local, plane, per_chunk):
    pair = 1 if other is None else 2
    chip_rows = pair * local * BLK
    n_chunks = heads // per_chunk
    per = heads * vert.shape[1] // plane
    dtype = keys.dtype
    smem = pl.BlockSpec(memory_space=pltpu.SMEM)
    vmem = pl.BlockSpec(memory_space=pltpu.VMEM)
    data = [keys, values] + ([] if other is None else [other])
    specs = [vmem] * 2
    if other is not None:
        specs.append(pl.BlockSpec((other.shape[0], heads * 2 * HD), lambda i: (0, 0)))
    outs = pl.pallas_call(
        functools.partial(prepare_kernel, (pair, local, heads, plane, per_chunk)),
        grid=(1,),
        in_specs=[smem] * 2 + specs,
        out_specs=[vmem] * (n_chunks + plane),
        out_shape=[jax.ShapeDtypeStruct((chip_rows, per_chunk * 2 * HD), dtype)] * n_chunks
        + [jax.ShapeDtypeStruct((per * BLK, 2 * HD), dtype)] * plane,
        scratch_shapes=[pltpu.VMEM((heads, chip_rows, 2 * HD), dtype)],
        compiler_params=pltpu.CompilerParams(vmem_limit_bytes=VMEM_LIMIT),
        cost_estimate=pl.CostEstimate(
            flops=0, bytes_accessed=8 * heads * chip_rows * 2 * HD, transcendentals=0
        ),
        name="prepare",
    )(info, vert, *data)
    return list(outs[:n_chunks]), list(outs[n_chunks:])


def soften(q, k, bias, p_ref, group, factor):
    s = jnp.dot(q, k, preferred_element_type=jnp.float32)
    totals = []
    for g in range(group):
        rows = slice(g * BLK, (g + 1) * BLK)
        total = None
        for j in range(k.shape[1] // BLK):
            cols = slice(j * BLK, (j + 1) * BLK)
            p = jnp.exp(s[rows, cols] * factor + bias(j))
            p_ref[rows, cols] = p.astype(p_ref.dtype)
            total = p if total is None else total + p
        totals.append(total)
    return jnp.concatenate(totals, 0)


def pipelined(blocks, stage):
    stage(0, 0, blocks > 1, False)

    def two_blocks(n, carry):
        stage(2 * n + 1, 1, True, True)
        stage(2 * n + 2, 0, True, True)
        return carry

    inner = max(blocks - 2, 0) // 2
    lax.fori_loop(0, inner, two_blocks, 0)
    for i in range(2 * inner + 1, blocks):
        stage(i, i % 2, i + 1 < blocks, True)
    stage(blocks, blocks % 2, False, True)


def slash_kernel(cfg, info, slash, *refs):
    first, pair, local, group, reach, n_slash = cfg
    q_refs, refs = refs[:pair], refs[pair:]
    w_refs, refs = refs[: reach + 1], refs[reach + 1 :]
    masks, acc, win, qx = refs[:4]
    kgs, vgs, ps = refs[4:6], refs[6:8], refs[8:10]
    e = first + pl.program_id(0)
    chip, core = info[0], info[1]
    dev_rows = local * BLK
    chip_blocks = pair * local
    chip_rows = chip_blocks * BLK
    width = n_slash * BLK
    factor = 1.0 / math.sqrt(HD)

    for back in range(reach + 1):
        for slot in range(pair):
            owner = core ^ slot if pair > 1 else 0
            at = pl.multiple_of((reach - back) * chip_rows + owner * dev_rows, dev_rows)
            rows = slice(slot * dev_rows, (slot + 1) * dev_rows)
            win[pl.ds(at, dev_rows), :] = w_refs[back][rows, :]
    for i in range(chip_blocks):
        slot, b = divmod(i, local)
        for g in range(group):
            rows = slice(g * BLK, (g + 1) * BLK)
            qx[i, rows, :] = q_refs[slot][b * BLK : (b + 1) * BLK, g * HD : (g + 1) * HD]

    def within(i):
        return (core ^ i // local) * local + i % local if pair > 1 else i

    def take(i, j):
        src = (reach * chip_blocks + within(i) - slash[e, j]) * BLK
        return pl.ds(pl.multiple_of(src, BLK), BLK)

    def place_keys(i, at):
        for j in range(n_slash):
            kgs[at][:, j * BLK : (j + 1) * BLK] = win[take(i, j), :HD]

    def stage(i, at, ahead, behind):
        if ahead:
            place_keys(i + 1, 1 - at)
        if behind:
            acc[i - 1, :, :HD] = jnp.dot(
                ps[1 - at][...], vgs[1 - at][...], preferred_element_type=jnp.float32
            )
        if isinstance(i, int) and i == chip_blocks:
            return
        here = chip * chip_blocks + within(i)

        def bias(j):
            off = slash[e, j]
            return masks[jnp.where(off > here, 2, jnp.where(off == 0, 1, 0))]

        for j in range(n_slash):
            vgs[at][j * BLK : (j + 1) * BLK, :] = win[take(i, j), HD:]
        acc[i, :, HD:] = soften(qx[i], kgs[at][...], bias, ps[at], group, factor)

    place_keys(0, 0)
    pipelined(chip_blocks, stage)


def vertical_kernel(cfg, info, vert, slash, *refs):
    first, pair, local, group, reach, n_slash, n_vert, plane, heads = cfg
    q_refs, refs = refs[:pair], refs[pair:]
    w_refs, refs = refs[: reach + 1], refs[reach + 1 :]
    before, kv_vert, masks, refs = refs[0], refs[1], refs[2], refs[3:]
    out_refs, refs = refs[:pair], refs[pair:]
    ke, ve, qx, res, good = refs[:5]
    ps, sums, (kg, vg, sc, pg) = refs[5:7], refs[7:9], refs[9:]
    e = first + pl.program_id(0)
    chip, core = info[0], info[1]
    dev_rows = local * BLK
    chip_blocks = pair * local
    factor = 1.0 / math.sqrt(HD)

    def within(i):
        return (core ^ i // local) * local + i % local if pair > 1 else i

    def hidden(i, j):
        here = chip * chip_blocks + within(i)
        found = vert[e, j] >= here
        for u in range(n_slash):
            found = found | (vert[e, j] == here - slash[e, u])
        return found

    per = heads * n_vert // plane
    for j in range(n_vert):
        flat = e * n_vert + j
        src = pl.multiple_of(((flat // per ^ chip % plane) * per + flat % per) * BLK, BLK)
        rows = slice(j * BLK, (j + 1) * BLK)
        ke[:, rows] = kv_vert[pl.ds(src, BLK), :HD]
        ve[rows, :] = kv_vert[pl.ds(src, BLK), HD:]
    for i in range(chip_blocks):
        slot, b = divmod(i, local)
        for g in range(group):
            rows = slice(g * BLK, (g + 1) * BLK)
            qx[i, rows, :] = q_refs[slot][b * BLK : (b + 1) * BLK, g * HD : (g + 1) * HD]
    good[...] = jnp.ones(good.shape, good.dtype)

    def stage(i, at, ahead, behind):
        if behind:
            attended = before[i - 1, :, :HD] + jnp.dot(
                ps[1 - at][...], ve[...], preferred_element_type=jnp.float32
            )
            total = jnp.sum(sums[1 - at][...], axis=1, keepdims=True)
            res[i - 1] = (attended / total).astype(res.dtype)
            fine = jnp.where((total > SMALLEST) & (total < LARGEST), 1.0, 0.0)
            good[...] = jnp.minimum(good[...], jnp.min(fine, axis=0, keepdims=True))
        if isinstance(i, int) and i == chip_blocks:
            return

        def bias(j):
            return jnp.where(hidden(i, j), MASKED, 0.0)

        sums[at][...] = before[i, :, HD:] + soften(qx[i], ke[...], bias, ps[at], group, factor)

    pipelined(chip_blocks, stage)

    @pl.when(jnp.logical_not(jnp.min(good[...]) > 0.5))
    def _():
        kg[:, n_slash * BLK :] = ke[...]
        vg[n_slash * BLK :, :] = ve[...]

        def shifted_block(i, carry):
            here = chip * chip_blocks + within(i)
            biases = []
            for j in range(n_slash):
                off = slash[e, j]
                pos = reach * chip_blocks + within(i) - off
                back = reach - pos // chip_blocks
                src = pos % chip_blocks
                if pair > 1:
                    src = (src // local ^ core) * local + src % local
                at = pl.ds(pl.multiple_of(src * BLK, BLK), BLK)
                found = w_refs[0][at, :]
                for d in range(1, reach + 1):
                    found = jnp.where(back == d, w_refs[d][at, :], found)
                rows = slice(j * BLK, (j + 1) * BLK)
                kg[:, rows] = found[:, :HD]
                vg[rows, :] = found[:, HD:]
                biases.append(masks[jnp.where(off > here, 2, jnp.where(off == 0, 1, 0))])
            for j in range(n_vert):
                biases.append(jnp.where(hidden(i, j), MASKED, 0.0))
            sc[...] = jnp.dot(qx[i], kg[...], preferred_element_type=jnp.float32)
            for g in range(group):
                rows = slice(g * BLK, (g + 1) * BLK)
                top = None
                for j, bias in enumerate(biases):
                    cols = slice(j * BLK, (j + 1) * BLK)
                    sc[rows, cols] = sc[rows, cols] * factor + bias
                    top = sc[rows, cols] if top is None else jnp.maximum(top, sc[rows, cols])
                p = jnp.exp(sc[rows, :] - jnp.max(top, axis=1, keepdims=True))
                pg[rows, :] = p.astype(pg.dtype)
                sums[0][rows, :] = jnp.broadcast_to(jnp.sum(p, axis=1, keepdims=True), (BLK, HD))
            acc = jnp.dot(pg[...], vg[...], preferred_element_type=jnp.float32)
            res[i] = (acc / sums[0][...]).astype(res.dtype)
            return carry

        lax.fori_loop(0, chip_blocks, shifted_block, 0)

    for i in range(chip_blocks):
        slot, b = divmod(i, local)
        for g in range(group):
            out_refs[slot][b * BLK : (b + 1) * BLK, g * HD : (g + 1) * HD] = res[
                i, g * BLK : (g + 1) * BLK
            ]


class Attention:
    def __init__(self, queries, q_other, info, vert, slash, masks, heads, local, plane):
        self.pair = 1 if q_other is None else 2
        self.qs = [queries] if q_other is None else [queries, q_other]
        self.info, self.vert, self.slash, self.masks = info, vert, slash, masks
        self.heads, self.local, self.plane = heads, local, plane
        self.dev_rows = queries.shape[0]
        self.wide = queries.shape[1] // (self.pair * heads)
        self.group = self.wide // HD
        self.blocks = self.pair * local
        self.dtype = queries.dtype

    def specs(self, first, windows):
        heads, shape = self.heads, (self.dev_rows, self.wide)
        specs = [pl.BlockSpec(shape, lambda i, info, *_: (0, info[1] * heads + first + i))]
        if self.pair > 1:
            at = self.qs[1].shape[1] // self.wide - heads + first
            specs.append(pl.BlockSpec(shape, lambda i, *_: (0, at + i)))
        return specs + [pl.BlockSpec((w.shape[0], 2 * HD), lambda i, *_: (0, i)) for w in windows]

    def whole(self, a):
        return pl.BlockSpec(a.shape, lambda i, *_: (0,) * a.ndim)

    def cost(self, n, width, more):
        rows = n * self.blocks * self.group * BLK
        return pl.CostEstimate(
            flops=8 * rows * width * HD,
            bytes_accessed=rows * HD * 2 + more,
            transcendentals=rows * width,
        )

    def acc_spec(self):
        shape = (self.blocks, self.group * BLK, 2 * HD)
        return pl.BlockSpec((None, *shape), lambda i, *_: (i, 0, 0, 0))

    def over_slash(self, first, n, windows):
        n_slash = self.slash.shape[1]
        width, rows = n_slash * BLK, self.group * BLK
        shape = (n, self.blocks, rows, 2 * HD)
        cfg = (first, self.pair, self.local, self.group, len(windows) - 1, n_slash)
        return pl.pallas_call(
            functools.partial(slash_kernel, cfg),
            grid_spec=pltpu.PrefetchScalarGridSpec(
                num_scalar_prefetch=2,
                grid=(n,),
                in_specs=self.specs(first, windows) + [self.whole(self.masks)],
                out_specs=self.acc_spec(),
                scratch_shapes=[
                    pltpu.VMEM((sum(w.shape[0] for w in windows), 2 * HD), self.dtype),
                    pltpu.VMEM((self.blocks, rows, HD), self.dtype),
                ]
                + [pltpu.VMEM((HD, width), self.dtype)] * 2
                + [pltpu.VMEM((width, HD), self.dtype)] * 2
                + [pltpu.VMEM((rows, width), self.dtype)] * 2,
            ),
            out_shape=jax.ShapeDtypeStruct(shape, jnp.float32),
            compiler_params=pltpu.CompilerParams(vmem_limit_bytes=VMEM_LIMIT),
            cost_estimate=self.cost(n, width, 4 * math.prod(shape)),
            name="attend_slash",
        )(self.info, self.slash, *self.qs, *windows, self.masks)

    def over_vertical(self, first, n, windows, before, kv_vert):
        n_slash, n_vert = self.slash.shape[1], self.vert.shape[1]
        width, both, rows = n_vert * BLK, (n_slash + n_vert) * BLK, self.group * BLK
        cfg = (first, self.pair, self.local, self.group, len(windows) - 1, n_slash, n_vert)
        out = pl.BlockSpec((self.dev_rows, self.wide), lambda i, *_: (0, i))
        return pl.pallas_call(
            functools.partial(vertical_kernel, cfg + (self.plane, self.heads)),
            grid_spec=pltpu.PrefetchScalarGridSpec(
                num_scalar_prefetch=3,
                grid=(n,),
                in_specs=self.specs(first, windows)
                + [self.acc_spec(), self.whole(kv_vert), self.whole(self.masks)],
                out_specs=[out] * self.pair,
                scratch_shapes=[
                    pltpu.VMEM((HD, width), self.dtype),
                    pltpu.VMEM((width, HD), self.dtype),
                    pltpu.VMEM((self.blocks, rows, HD), self.dtype),
                    pltpu.VMEM((self.blocks, rows, HD), self.dtype),
                    pltpu.VMEM((1, 1), jnp.float32),
                    pltpu.VMEM((rows, width), self.dtype),
                    pltpu.VMEM((rows, width), self.dtype),
                    pltpu.VMEM((rows, HD), jnp.float32),
                    pltpu.VMEM((rows, HD), jnp.float32),
                    pltpu.VMEM((HD, both), self.dtype),
                    pltpu.VMEM((both, HD), self.dtype),
                    pltpu.VMEM((rows, both), jnp.float32),
                    pltpu.VMEM((rows, both), self.dtype),
                ],
            ),
            out_shape=[jax.ShapeDtypeStruct((self.dev_rows, n * self.wide), self.dtype)]
            * self.pair,
            compiler_params=pltpu.CompilerParams(vmem_limit_bytes=VMEM_LIMIT),
            cost_estimate=self.cost(n, width, 4 * math.prod(before.shape)),
            name="attend_vertical",
        )(self.info, self.vert, self.slash, *self.qs, *windows, before, kv_vert, self.masks)


def body(queries, keys, values, vertical_blocks, slash_offsets, out_weight):
    tokens_dev = queries.shape[0]
    kv_heads = keys.shape[1] // HD
    local = tokens_dev // BLK
    size = lax.axis_size("ctx")
    pair = 2 if kv_heads % 2 == 0 and size % 2 == 0 and lax.axis_size("head") == 1 else 1
    chips = size // pair
    heads = kv_heads // pair
    plane = PLANE if chips % PLANE == 0 and heads * vertical_blocks.shape[1] % PLANE == 0 else 1
    chip_blocks = pair * local
    reach = -(-MAXOFF // chip_blocks)
    index = lax.axis_index("ctx")
    chip, core = index // pair, index % pair
    info = jnp.stack([chip, core]).astype(jnp.int32)
    pos = jnp.arange(BLK)
    causal = jnp.where(pos[:, None] < pos[None, :], MASKED, 0.0)
    masks = jnp.stack([jnp.zeros_like(causal), causal, jnp.full_like(causal, MASKED)])

    def part(value, axis, which):
        span = value.shape[axis] // pair
        return lax.dynamic_slice_in_dim(value, which * span, span, axis)

    vert, slash = part(vertical_blocks, 0, core), part(slash_offsets, 0, core)
    kv_other = None
    if pair == 2:
        kv_other = crossed(jnp.concatenate([part(a, 1, 1 - core) for a in (keys, values)], 1), 1)
    per_chunk = 2 if heads % 2 == 0 else 1
    own, listed = prepare(info, vert, keys, values, kv_other, heads, local, plane, per_chunk)

    total = listed[0]
    for k in range(1, plane):
        total = total + crossed(listed[k], k * pair)
    q_sent = part(queries, 1, 1 - core) if pair == 2 else None
    total, own[0], q_sent = lax.optimization_barrier((total, own[0], q_sent))
    q_other = crossed(q_sent, 1) if pair == 2 else None
    step = 1
    while step < chips // plane:
        total = total + shifted(total, step * plane * pair)
        if step == 1:
            total, q_other, own[1:] = lax.optimization_barrier((total, q_other, own[1:]))
        step *= 2

    attention = Attention(queries, q_other, info, vert, slash, masks, heads, local, plane)
    chunks = heads // per_chunk
    all_windows, sums = [], []
    for c in range(chunks):
        windows = [own[c]]
        if pair == 2 and reach == 2 and chips % 2 == 0:
            two_back = shifted(own[c], 2 * pair)
            passed = jnp.where(chip % 2 == 0, own[c], two_back)
            windows += [crossed(passed, pair), two_back]
        else:
            windows += [shifted(own[c], pair * d) for d in range(1, reach + 1)]
        all_windows.append(windows)
        sums.append(attention.over_slash(c * per_chunk, per_chunk, windows))
    gathered = [total] + [crossed(total, k * pair) for k in range(1, plane)]
    gathered, sums[0] = lax.optimization_barrier((gathered, sums[0]))
    kv_vert = jnp.concatenate(gathered, 0)
    near, far = [], []
    for c in range(chunks):
        att = attention.over_vertical(c * per_chunk, per_chunk, all_windows[c], sums[c], kv_vert)
        near.append(att[0])
        if pair == 2:
            far.append(crossed(att[1], 1))
    attended = near
    if pair == 2:
        attended = [jnp.where(core == 0, a, b) for a, b in zip(near, far)]
        attended += [jnp.where(core == 0, b, a) for a, b in zip(near, far)]
    attended = lax.all_gather(jnp.concatenate(attended, 1), "head", axis=1, tiled=True)
    output = jnp.dot(attended, out_weight, preferred_element_type=jnp.float32)
    return output.astype(jnp.bfloat16)


def solution(mesh):
    placed = (
        P("ctx", "head"),
        P("ctx", "head"),
        P("ctx", "head"),
        P("head", None),
        P("head", None),
        P(None, "head"),
    )
    return jax.shard_map(
        body, mesh=mesh, in_specs=placed, out_specs=P("ctx", "head"), check_vma=False
    )
```

```python
import functools
import math

import jax
import jax.numpy as jnp
from jax import lax
from jax.experimental import pallas as pl
from jax.experimental.pallas import tpu as pltpu
from jax.sharding import PartitionSpec as P

HD = 128
BLK = 128
MAXOFF = 16
PLANE = 4
MASKED = -1e30
SMALLEST, LARGEST = 2.0**-30, 2.0**30
VMEM_LIMIT = 56 * 1024 * 1024


def shifted(value, by):
    size = lax.axis_size("ctx")
    return lax.ppermute(value, "ctx", [(i, i + by) for i in range(size - by)])


def crossed(value, bits):
    size = lax.axis_size("ctx")
    return lax.ppermute(value, "ctx", [(i, i ^ bits) for i in range(size)])


def prepare_kernel(cfg, info, vert, *refs):
    pair, local, heads, plane, per_chunk = cfg
    chip, core = info[0], info[1]
    keys, values = refs[:2]
    refs = refs[2:]
    other = None
    if pair > 1:
        other, refs = refs[0], refs[1:]
    n_chunks = heads // per_chunk
    chip_outs, refs = refs[:n_chunks], refs[n_chunks:]
    list_outs, chip_kv = refs[:plane], refs[plane]
    n_vert = vert.shape[1]
    dev_rows = local * BLK
    chip_blocks = pair * local
    for e in range(heads):
        at = pl.multiple_of((core * heads + e) * HD, HD)
        chip_kv[e, :dev_rows, HD:] = values[:, pl.ds(at, HD)]
        if pair > 1:
            chip_kv[e, dev_rows:, HD:] = other[:, (heads + e) * HD : (heads + e + 1) * HD]
        for b in range(pair * local):
            rows = slice(b % local * BLK, (b % local + 1) * BLK)
            block = keys[rows, pl.ds(at, HD)] if b < local else other[rows, e * HD : (e + 1) * HD]
            chip_kv[e, b * BLK : (b + 1) * BLK, :HD] = block.T
        c, at = divmod(e, per_chunk)
        chip_outs[c][:, at * 2 * HD : (at + 1) * 2 * HD] = chip_kv[e]
    per = heads * n_vert // plane
    for k in range(plane):
        for i in range(per):
            flat = (chip % plane ^ k) * per + i
            e, j = flat // n_vert, flat % n_vert
            block = vert[e, j]
            within = block % chip_blocks
            if pair > 1:
                within = (within // local ^ core) * local + within % local
            rows = slice(i * BLK, (i + 1) * BLK)
            owned = block // chip_blocks == chip
            found = chip_kv[e, pl.ds(pl.multiple_of(within * BLK, BLK), BLK), :]
            list_outs[k][rows, :] = jnp.where(owned, found, jnp.zeros_like(found))


def prepare(info, vert, keys, values, other, heads, local, plane, per_chunk):
    pair = 1 if other is None else 2
    chip_rows = pair * local * BLK
    n_chunks = heads // per_chunk
    per = heads * vert.shape[1] // plane
    dtype = keys.dtype
    smem = pl.BlockSpec(memory_space=pltpu.SMEM)
    vmem = pl.BlockSpec(memory_space=pltpu.VMEM)
    data = [keys, values] + ([] if other is None else [other])
    specs = [vmem] * 2
    if other is not None:
        specs.append(pl.BlockSpec((other.shape[0], heads * 2 * HD), lambda i: (0, 0)))
    outs = pl.pallas_call(
        functools.partial(prepare_kernel, (pair, local, heads, plane, per_chunk)),
        grid=(1,),
        in_specs=[smem] * 2 + specs,
        out_specs=[vmem] * (n_chunks + plane),
        out_shape=[jax.ShapeDtypeStruct((chip_rows, per_chunk * 2 * HD), dtype)] * n_chunks
        + [jax.ShapeDtypeStruct((per * BLK, 2 * HD), dtype)] * plane,
        scratch_shapes=[pltpu.VMEM((heads, chip_rows, 2 * HD), dtype)],
        compiler_params=pltpu.CompilerParams(vmem_limit_bytes=VMEM_LIMIT),
        cost_estimate=pl.CostEstimate(
            flops=0, bytes_accessed=8 * heads * chip_rows * 2 * HD, transcendentals=0
        ),
        name="prepare",
    )(info, vert, *data)
    return list(outs[:n_chunks]), list(outs[n_chunks:])


def onehot_rows(shape, at, dtype):
    row = lax.broadcasted_iota(jnp.int32, shape, 0)
    col = lax.broadcasted_iota(jnp.int32, shape, 1)
    return jnp.where(col == at(row), 1.0, 0.0).astype(dtype)


def exponentials(q, k, factor):
    x = jnp.dot(q, k, preferred_element_type=jnp.float32) * factor
    high = x.astype(jnp.bfloat16)
    low = x - high.astype(jnp.float32)
    return jnp.exp2(high) * (low * math.log(2.0) + 1.0).astype(jnp.bfloat16)


def pipelined(blocks, stage):
    stage(0, 0, blocks > 1, False)

    def two_blocks(n, carry):
        stage(2 * n + 1, 1, True, True)
        stage(2 * n + 2, 0, True, True)
        return carry

    inner = max(blocks - 2, 0) // 2
    lax.fori_loop(0, inner, two_blocks, 0)
    for i in range(2 * inner + 1, blocks):
        stage(i, i % 2, i + 1 < blocks, True)
    stage(blocks, blocks % 2, False, True)


def slash_kernel(cfg, info, slash, *refs):
    first, pair, local, group, reach, n_slash = cfg
    q_refs, refs = refs[:pair], refs[pair:]
    w_refs, refs = refs[: reach + 1], refs[reach + 1 :]
    masks, acc, win, qx = refs[:4]
    kgs, vgs, ps = refs[4:6], refs[6:8], refs[8:10]
    e = first + pl.program_id(0)
    chip, core = info[0], info[1]
    dev_rows = local * BLK
    chip_blocks = pair * local
    chip_rows = chip_blocks * BLK
    width = n_slash * BLK
    factor = math.log2(math.e) / math.sqrt(HD)

    for back in range(reach + 1):
        for slot in range(pair):
            owner = core ^ slot if pair > 1 else 0
            at = pl.multiple_of((reach - back) * chip_rows + owner * dev_rows, dev_rows)
            rows = slice(slot * dev_rows, (slot + 1) * dev_rows)
            win[pl.ds(at, dev_rows), :] = w_refs[back][rows, :]
    for vg in vgs:
        vg[:, HD:] = jnp.ones((width, HD), vg.dtype)
    eye = onehot_rows((BLK, HD), lambda row: row, qx.dtype)
    for i in range(chip_blocks):
        slot, b = divmod(i, local)
        for g in range(group):
            rows = slice(g * BLK, (g + 1) * BLK)
            qx[i, rows, :HD] = q_refs[slot][b * BLK : (b + 1) * BLK, g * HD : (g + 1) * HD]
            qx[i, rows, HD:] = eye

    def within(i):
        return (core ^ i // local) * local + i % local if pair > 1 else i

    def take(i, j):
        src = (reach * chip_blocks + within(i) - slash[e, j]) * BLK
        return pl.ds(pl.multiple_of(src, BLK), BLK)

    def place_keys(i, at):
        here = chip * chip_blocks + within(i)
        for j in range(n_slash):
            off = slash[e, j]
            cols = slice(j * BLK, (j + 1) * BLK)
            kgs[at][:HD, cols] = win[take(i, j), :HD]
            kgs[at][HD:, cols] = masks[jnp.where(off > here, 2, jnp.where(off == 0, 1, 0))]

    def stage(i, at, ahead, behind):
        if ahead:
            place_keys(i + 1, 1 - at)
        if behind:
            acc[i - 1] = jnp.dot(
                ps[1 - at][...], vgs[1 - at][...], preferred_element_type=jnp.float32
            )
        if isinstance(i, int) and i == chip_blocks:
            return
        for j in range(n_slash):
            vgs[at][j * BLK : (j + 1) * BLK, :HD] = win[take(i, j), HD:]
        ps[at][...] = exponentials(qx[i], kgs[at][...], factor).astype(ps[at].dtype)

    place_keys(0, 0)
    pipelined(chip_blocks, stage)


def vertical_kernel(cfg, info, vert, slash, *refs):
    first, pair, local, group, reach, n_slash, n_vert, plane, heads = cfg
    q_refs, refs = refs[:pair], refs[pair:]
    w_refs, refs = refs[: reach + 1], refs[reach + 1 :]
    before, kv_vert, masks, refs = refs[0], refs[1], refs[2], refs[3:]
    out_refs, refs = refs[:pair], refs[pair:]
    ke, ve, qx, res, good = refs[:5]
    ps, (kg, vg, sc, pg) = refs[5:7], refs[7:]
    e = first + pl.program_id(0)
    chip, core = info[0], info[1]
    dev_rows = local * BLK
    chip_blocks = pair * local
    wide = n_vert * BLK
    step = min(2 * BLK, wide)
    factor = math.log2(math.e) / math.sqrt(HD)

    def within(i):
        return (core ^ i // local) * local + i % local if pair > 1 else i

    def hidden(i, j):
        here = chip * chip_blocks + within(i)
        found = vert[e, j] >= here
        for u in range(n_slash):
            found = found | (vert[e, j] == here - slash[e, u])
        return found

    per = heads * n_vert // plane
    row = lax.broadcasted_iota(jnp.int32, (HD, BLK), 0)
    for j in range(n_vert):
        flat = e * n_vert + j
        src = pl.multiple_of(((flat // per ^ chip % plane) * per + flat % per) * BLK, BLK)
        rows = slice(j * BLK, (j + 1) * BLK)
        ke[:HD, rows] = kv_vert[pl.ds(src, BLK), :HD]
        ve[rows, :HD] = kv_vert[pl.ds(src, BLK), HD:]
        bias = jnp.zeros((HD, BLK), jnp.float32)
        for i in range(chip_blocks):
            bias = jnp.where((row == i) & hidden(i, j), MASKED, bias)
        ke[HD:, rows] = bias.astype(ke.dtype)
    ve[:, HD:] = jnp.ones((wide, HD), ve.dtype)
    for i in range(chip_blocks):
        slot, b = divmod(i, local)
        for g in range(group):
            rows = slice(g * BLK, (g + 1) * BLK)
            qx[i, rows, :HD] = q_refs[slot][b * BLK : (b + 1) * BLK, g * HD : (g + 1) * HD]
            qx[i, rows, HD:] = onehot_rows((BLK, HD), lambda row, i=i: i, qx.dtype)
    good[...] = jnp.ones(good.shape, good.dtype)

    def stage(i, at, ahead, behind):
        if behind:
            acc = before[i - 1] + jnp.dot(
                ps[1 - at][...], ve[...], preferred_element_type=jnp.float32
            )
            total = acc[:, HD:]
            res[i - 1] = (acc[:, :HD] / total).astype(res.dtype)
            fine = jnp.where((total > SMALLEST) & (total < LARGEST), 1.0, 0.0)
            good[...] = jnp.minimum(good[...], jnp.min(fine, axis=0, keepdims=True))
        if isinstance(i, int) and i == chip_blocks:
            return
        ps[at][...] = exponentials(qx[i], ke[...], factor).astype(ps[at].dtype)

    pipelined(chip_blocks, stage)

    @pl.when(jnp.logical_not(jnp.min(good[...]) > 0.5))
    def _():
        vg[: n_slash * BLK, HD:] = jnp.ones((n_slash * BLK, HD), vg.dtype)
        kg[:, n_slash * BLK :] = ke[...]
        vg[n_slash * BLK :, :] = ve[...]
        eye = onehot_rows((BLK, HD), lambda row: row, qx.dtype)

        def shifted_block(i, carry):
            here = chip * chip_blocks + within(i)
            for g in range(group):
                qx[i, g * BLK : (g + 1) * BLK, HD:] = eye
            for j in range(n_slash):
                off = slash[e, j]
                pos = reach * chip_blocks + within(i) - off
                back = reach - pos // chip_blocks
                src = pos % chip_blocks
                if pair > 1:
                    src = (src // local ^ core) * local + src % local
                at = pl.ds(pl.multiple_of(src * BLK, BLK), BLK)
                found = w_refs[0][at, :]
                for d in range(1, reach + 1):
                    found = jnp.where(back == d, w_refs[d][at, :], found)
                rows = slice(j * BLK, (j + 1) * BLK)
                kg[:HD, rows] = found[:, :HD]
                vg[rows, :HD] = found[:, HD:]
                kg[HD:, rows] = masks[jnp.where(off > here, 2, jnp.where(off == 0, 1, 0))]
            for j in range(n_vert):
                rows = slice((n_slash + j) * BLK, (n_slash + j + 1) * BLK)
                kg[HD:, rows] = masks[jnp.where(hidden(i, j), 2, 0)]
            top = None
            for t in range(0, kg.shape[1], step):
                s = jnp.dot(qx[i], kg[:, t : t + step], preferred_element_type=jnp.float32)
                sc[:, t : t + step] = s
                for u in range(0, step, HD):
                    piece = s[:, u : u + HD]
                    top = piece if top is None else jnp.maximum(top, piece)
            top = jnp.max(top, axis=1, keepdims=True)
            for t in range(0, kg.shape[1], step):
                p = jnp.exp2((sc[:, t : t + step] - top) * factor)
                pg[:, t : t + step] = p.astype(pg.dtype)
            acc = jnp.dot(pg[...], vg[...], preferred_element_type=jnp.float32)
            res[i] = (acc[:, :HD] / acc[:, HD:]).astype(res.dtype)
            return carry

        lax.fori_loop(0, chip_blocks, shifted_block, 0)

    for i in range(chip_blocks):
        slot, b = divmod(i, local)
        for g in range(group):
            out_refs[slot][b * BLK : (b + 1) * BLK, g * HD : (g + 1) * HD] = res[
                i, g * BLK : (g + 1) * BLK
            ]


class Attention:
    def __init__(self, queries, q_other, info, vert, slash, masks, heads, local, plane):
        self.pair = 1 if q_other is None else 2
        self.qs = [queries] if q_other is None else [queries, q_other]
        self.info, self.vert, self.slash, self.masks = info, vert, slash, masks
        self.heads, self.local, self.plane = heads, local, plane
        self.dev_rows = queries.shape[0]
        self.wide = queries.shape[1] // (self.pair * heads)
        self.group = self.wide // HD
        self.blocks = self.pair * local
        self.dtype = queries.dtype

    def specs(self, first, windows):
        heads, shape = self.heads, (self.dev_rows, self.wide)
        specs = [pl.BlockSpec(shape, lambda i, info, *_: (0, info[1] * heads + first + i))]
        if self.pair > 1:
            at = self.qs[1].shape[1] // self.wide - heads + first
            specs.append(pl.BlockSpec(shape, lambda i, *_: (0, at + i)))
        return specs + [pl.BlockSpec((w.shape[0], 2 * HD), lambda i, *_: (0, i)) for w in windows]

    def whole(self, a):
        return pl.BlockSpec(a.shape, lambda i, *_: (0,) * a.ndim)

    def cost(self, n, width, more):
        rows = n * self.blocks * self.group * BLK
        return pl.CostEstimate(
            flops=8 * rows * width * HD,
            bytes_accessed=rows * HD * 2 + more,
            transcendentals=rows * width,
        )

    def acc_spec(self):
        shape = (self.blocks, self.group * BLK, 2 * HD)
        return pl.BlockSpec((None, *shape), lambda i, *_: (i, 0, 0, 0))

    def over_slash(self, first, n, windows):
        n_slash = self.slash.shape[1]
        width, rows = n_slash * BLK, self.group * BLK
        shape = (n, self.blocks, rows, 2 * HD)
        cfg = (first, self.pair, self.local, self.group, len(windows) - 1, n_slash)
        return pl.pallas_call(
            functools.partial(slash_kernel, cfg),
            grid_spec=pltpu.PrefetchScalarGridSpec(
                num_scalar_prefetch=2,
                grid=(n,),
                in_specs=self.specs(first, windows) + [self.whole(self.masks)],
                out_specs=self.acc_spec(),
                scratch_shapes=[
                    pltpu.VMEM((sum(w.shape[0] for w in windows), 2 * HD), self.dtype),
                    pltpu.VMEM((self.blocks, rows, 2 * HD), self.dtype),
                ]
                + [pltpu.VMEM((2 * HD, width), self.dtype)] * 2
                + [pltpu.VMEM((width, 2 * HD), self.dtype)] * 2
                + [pltpu.VMEM((rows, width), self.dtype)] * 2,
            ),
            out_shape=jax.ShapeDtypeStruct(shape, jnp.float32),
            compiler_params=pltpu.CompilerParams(vmem_limit_bytes=VMEM_LIMIT),
            cost_estimate=self.cost(n, width, 4 * math.prod(shape)),
            name="attend_slash",
        )(self.info, self.slash, *self.qs, *windows, self.masks)

    def over_vertical(self, first, n, windows, before, kv_vert):
        n_slash, n_vert = self.slash.shape[1], self.vert.shape[1]
        width, both, rows = n_vert * BLK, (n_slash + n_vert) * BLK, self.group * BLK
        cfg = (first, self.pair, self.local, self.group, len(windows) - 1, n_slash, n_vert)
        out = pl.BlockSpec((self.dev_rows, self.wide), lambda i, *_: (0, i))
        return pl.pallas_call(
            functools.partial(vertical_kernel, cfg + (self.plane, self.heads)),
            grid_spec=pltpu.PrefetchScalarGridSpec(
                num_scalar_prefetch=3,
                grid=(n,),
                in_specs=self.specs(first, windows)
                + [self.acc_spec(), self.whole(kv_vert), self.whole(self.masks)],
                out_specs=[out] * self.pair,
                scratch_shapes=[
                    pltpu.VMEM((2 * HD, width), self.dtype),
                    pltpu.VMEM((width, 2 * HD), self.dtype),
                    pltpu.VMEM((self.blocks, rows, 2 * HD), self.dtype),
                    pltpu.VMEM((self.blocks, rows, HD), self.dtype),
                    pltpu.VMEM((1, HD), jnp.float32),
                    pltpu.VMEM((rows, width), self.dtype),
                    pltpu.VMEM((rows, width), self.dtype),
                    pltpu.VMEM((2 * HD, both), self.dtype),
                    pltpu.VMEM((both, 2 * HD), self.dtype),
                    pltpu.VMEM((rows, both), jnp.float32),
                    pltpu.VMEM((rows, both), self.dtype),
                ],
            ),
            out_shape=[jax.ShapeDtypeStruct((self.dev_rows, n * self.wide), self.dtype)]
            * self.pair,
            compiler_params=pltpu.CompilerParams(vmem_limit_bytes=VMEM_LIMIT),
            cost_estimate=self.cost(n, width, 4 * math.prod(before.shape)),
            name="attend_vertical",
        )(self.info, self.vert, self.slash, *self.qs, *windows, before, kv_vert, self.masks)


def body(queries, keys, values, vertical_blocks, slash_offsets, out_weight):
    tokens_dev = queries.shape[0]
    kv_heads = keys.shape[1] // HD
    local = tokens_dev // BLK
    size = lax.axis_size("ctx")
    pair = 2 if kv_heads % 2 == 0 and size % 2 == 0 and lax.axis_size("head") == 1 else 1
    chips = size // pair
    heads = kv_heads // pair
    plane = PLANE if chips % PLANE == 0 and heads * vertical_blocks.shape[1] % PLANE == 0 else 1
    chip_blocks = pair * local
    reach = -(-MAXOFF // chip_blocks)
    index = lax.axis_index("ctx")
    chip, core = index // pair, index % pair
    info = jnp.stack([chip, core]).astype(jnp.int32)
    pos = jnp.arange(BLK)
    causal = jnp.where(pos[:, None] < pos[None, :], MASKED, 0.0)
    masks = jnp.stack([jnp.zeros_like(causal), causal, jnp.full_like(causal, MASKED)])
    masks = masks.astype(queries.dtype)

    def part(value, axis, which):
        span = value.shape[axis] // pair
        return lax.dynamic_slice_in_dim(value, which * span, span, axis)

    vert, slash = part(vertical_blocks, 0, core), part(slash_offsets, 0, core)
    kv_other = None
    if pair == 2:
        kv_other = crossed(jnp.concatenate([part(a, 1, 1 - core) for a in (keys, values)], 1), 1)
    per_chunk = 2 if heads % 2 == 0 else 1
    own, listed = prepare(info, vert, keys, values, kv_other, heads, local, plane, per_chunk)

    total = listed[0]
    for k in range(1, plane):
        total = total + crossed(listed[k], k * pair)
    q_sent = part(queries, 1, 1 - core) if pair == 2 else None
    total, own[0], q_sent = lax.optimization_barrier((total, own[0], q_sent))
    q_other = crossed(q_sent, 1) if pair == 2 else None
    step = 1
    while step < chips // plane:
        total = total + shifted(total, step * plane * pair)
        if step == 1:
            total, q_other, own[1:] = lax.optimization_barrier((total, q_other, own[1:]))
        step *= 2

    attention = Attention(queries, q_other, info, vert, slash, masks, heads, local, plane)
    chunks = heads // per_chunk
    all_windows, sums = [], []
    for c in range(chunks):
        windows = [own[c]]
        if pair == 2 and reach == 2 and chips % 2 == 0:
            two_back = shifted(own[c], 2 * pair)
            passed = jnp.where(chip % 2 == 0, own[c], two_back)
            windows += [crossed(passed, pair), two_back]
        else:
            windows += [shifted(own[c], pair * d) for d in range(1, reach + 1)]
        all_windows.append(windows)
        sums.append(attention.over_slash(c * per_chunk, per_chunk, windows))
    gathered = [total] + [crossed(total, k * pair) for k in range(1, plane)]
    gathered, sums[0] = lax.optimization_barrier((gathered, sums[0]))
    kv_vert = jnp.concatenate(gathered, 0)
    near, far = [], []
    for c in range(chunks):
        att = attention.over_vertical(c * per_chunk, per_chunk, all_windows[c], sums[c], kv_vert)
        near.append(att[0])
        if pair == 2:
            far.append(crossed(att[1], 1))
    attended = near
    if pair == 2:
        attended = [jnp.where(core == 0, a, b) for a, b in zip(near, far)]
        attended += [jnp.where(core == 0, b, a) for a, b in zip(near, far)]
    attended = lax.all_gather(jnp.concatenate(attended, 1), "head", axis=1, tiled=True)
    output = jnp.dot(attended, out_weight, preferred_element_type=jnp.float32)
    return output.astype(jnp.bfloat16)


def solution(mesh):
    placed = (
        P("ctx", "head"),
        P("ctx", "head"),
        P("ctx", "head"),
        P("head", None),
        P("head", None),
        P(None, "head"),
    )
    return jax.shard_map(
        body, mesh=mesh, in_specs=placed, out_specs=P("ctx", "head"), check_vma=False
    )
```

```python
import functools
import math

import jax
import jax.numpy as jnp
from jax import lax
from jax.experimental import pallas as pl
from jax.experimental.pallas import tpu as pltpu
from jax.sharding import PartitionSpec as P

HD = 128
BLK = 128
MAXOFF = 16
PLANE = 4
MASKED = -1e30
SMALLEST, LARGEST = 2.0**-60, 2.0**100
VMEM_LIMIT = 56 * 1024 * 1024


def shifted(value, by):
    size = lax.axis_size("ctx")
    return lax.ppermute(value, "ctx", [(i, i + by) for i in range(size - by)])


def crossed(value, bits):
    size = lax.axis_size("ctx")
    return lax.ppermute(value, "ctx", [(i, i ^ bits) for i in range(size)])


def prepare_kernel(cfg, info, vert, *refs):
    pair, local, heads, plane, per_chunk = cfg
    chip, core = info[0], info[1]
    keys, values = refs[:2]
    refs = refs[2:]
    other = None
    if pair > 1:
        other, refs = refs[0], refs[1:]
    n_chunks = heads // per_chunk
    chip_outs, refs = refs[:n_chunks], refs[n_chunks:]
    list_outs, chip_kv = refs[:plane], refs[plane]
    n_vert = vert.shape[1]
    dev_rows = local * BLK
    chip_blocks = pair * local
    for e in range(heads):
        at = pl.multiple_of((core * heads + e) * HD, HD)
        chip_kv[e, :dev_rows, HD:] = values[:, pl.ds(at, HD)]
        if pair > 1:
            chip_kv[e, dev_rows:, HD:] = other[:, (heads + e) * HD : (heads + e + 1) * HD]
        for b in range(pair * local):
            rows = slice(b % local * BLK, (b % local + 1) * BLK)
            block = keys[rows, pl.ds(at, HD)] if b < local else other[rows, e * HD : (e + 1) * HD]
            chip_kv[e, b * BLK : (b + 1) * BLK, :HD] = block.T
        c, at = divmod(e, per_chunk)
        chip_outs[c][:, at * 2 * HD : (at + 1) * 2 * HD] = chip_kv[e]
    per = heads * n_vert // plane
    for k in range(plane):
        for i in range(per):
            flat = (chip % plane ^ k) * per + i
            e, j = flat // n_vert, flat % n_vert
            block = vert[e, j]
            within = block % chip_blocks
            if pair > 1:
                within = (within // local ^ core) * local + within % local
            rows = slice(i * BLK, (i + 1) * BLK)
            owned = block // chip_blocks == chip
            found = chip_kv[e, pl.ds(pl.multiple_of(within * BLK, BLK), BLK), :]
            list_outs[k][rows, :] = jnp.where(owned, found, jnp.zeros_like(found))


def prepare(info, vert, keys, values, other, heads, local, plane, per_chunk):
    pair = 1 if other is None else 2
    chip_rows = pair * local * BLK
    n_chunks = heads // per_chunk
    per = heads * vert.shape[1] // plane
    dtype = keys.dtype
    smem = pl.BlockSpec(memory_space=pltpu.SMEM)
    vmem = pl.BlockSpec(memory_space=pltpu.VMEM)
    data = [keys, values] + ([] if other is None else [other])
    specs = [vmem] * 2
    if other is not None:
        specs.append(pl.BlockSpec((other.shape[0], heads * 2 * HD), lambda i: (0, 0)))
    outs = pl.pallas_call(
        functools.partial(prepare_kernel, (pair, local, heads, plane, per_chunk)),
        grid=(1,),
        in_specs=[smem] * 2 + specs,
        out_specs=[vmem] * (n_chunks + plane),
        out_shape=[jax.ShapeDtypeStruct((chip_rows, per_chunk * 2 * HD), dtype)] * n_chunks
        + [jax.ShapeDtypeStruct((per * BLK, 2 * HD), dtype)] * plane,
        scratch_shapes=[pltpu.VMEM((heads, chip_rows, 2 * HD), dtype)],
        compiler_params=pltpu.CompilerParams(vmem_limit_bytes=VMEM_LIMIT),
        cost_estimate=pl.CostEstimate(
            flops=0, bytes_accessed=8 * heads * chip_rows * 2 * HD, transcendentals=0
        ),
        name="prepare",
    )(info, vert, *data)
    return list(outs[:n_chunks]), list(outs[n_chunks:])


def onehot_rows(shape, at, dtype):
    row = lax.broadcasted_iota(jnp.int32, shape, 0)
    col = lax.broadcasted_iota(jnp.int32, shape, 1)
    return jnp.where(col == at(row), 1.0, 0.0).astype(dtype)


def exponentials(q, k, factor):
    return jnp.exp2(jnp.dot(q, k, preferred_element_type=jnp.float32) * factor)


def pipelined(blocks, stage):
    stage(0, 0, blocks > 1, False)

    def two_blocks(n, carry):
        stage(2 * n + 1, 1, True, True)
        stage(2 * n + 2, 0, True, True)
        return carry

    inner = max(blocks - 2, 0) // 2
    lax.fori_loop(0, inner, two_blocks, 0)
    for i in range(2 * inner + 1, blocks):
        stage(i, i % 2, i + 1 < blocks, True)
    stage(blocks, blocks % 2, False, True)


def slash_kernel(cfg, info, slash, *refs):
    first, pair, local, group, reach, n_slash = cfg
    q_refs, refs = refs[:pair], refs[pair:]
    w_refs, refs = refs[: reach + 1], refs[reach + 1 :]
    masks, acc, win, qx = refs[:4]
    kgs, vgs, ps = refs[4:6], refs[6:8], refs[8:10]
    e = first + pl.program_id(0)
    chip, core = info[0], info[1]
    dev_rows = local * BLK
    chip_blocks = pair * local
    chip_rows = chip_blocks * BLK
    width = n_slash * BLK
    factor = math.log2(math.e) / math.sqrt(HD)

    for back in range(reach + 1):
        for slot in range(pair):
            owner = core ^ slot if pair > 1 else 0
            at = pl.multiple_of((reach - back) * chip_rows + owner * dev_rows, dev_rows)
            rows = slice(slot * dev_rows, (slot + 1) * dev_rows)
            win[pl.ds(at, dev_rows), :] = w_refs[back][rows, :]
    for vg in vgs:
        vg[:, HD:] = jnp.ones((width, HD), vg.dtype)
    eye = onehot_rows((BLK, HD), lambda row: row, qx.dtype)
    for i in range(chip_blocks):
        slot, b = divmod(i, local)
        for g in range(group):
            rows = slice(g * BLK, (g + 1) * BLK)
            qx[i, rows, :HD] = q_refs[slot][b * BLK : (b + 1) * BLK, g * HD : (g + 1) * HD]
            qx[i, rows, HD:] = eye

    def within(i):
        return (core ^ i // local) * local + i % local if pair > 1 else i

    def take(i, j):
        src = (reach * chip_blocks + within(i) - slash[e, j]) * BLK
        return pl.ds(pl.multiple_of(src, BLK), BLK)

    def place_keys(i, at):
        here = chip * chip_blocks + within(i)
        for j in range(n_slash):
            off = slash[e, j]
            cols = slice(j * BLK, (j + 1) * BLK)
            kgs[at][:HD, cols] = win[take(i, j), :HD]
            kgs[at][HD:, cols] = masks[jnp.where(off > here, 2, jnp.where(off == 0, 1, 0))]

    def stage(i, at, ahead, behind):
        if ahead:
            place_keys(i + 1, 1 - at)
        if behind:
            acc[i - 1] = jnp.dot(
                ps[1 - at][...], vgs[1 - at][...], preferred_element_type=jnp.float32
            )
        if isinstance(i, int) and i == chip_blocks:
            return
        for j in range(n_slash):
            vgs[at][j * BLK : (j + 1) * BLK, :HD] = win[take(i, j), HD:]
        ps[at][...] = exponentials(qx[i], kgs[at][...], factor).astype(ps[at].dtype)

    place_keys(0, 0)
    pipelined(chip_blocks, stage)


def vertical_kernel(cfg, info, vert, slash, *refs):
    first, pair, local, group, reach, n_slash, n_vert, plane, heads = cfg
    q_refs, refs = refs[:pair], refs[pair:]
    w_refs, refs = refs[: reach + 1], refs[reach + 1 :]
    before, kv_vert, masks, refs = refs[0], refs[1], refs[2], refs[3:]
    out_refs, refs = refs[:pair], refs[pair:]
    ke, ve, qx, res, good, acc = refs[:6]
    ps, (kg, vg, sc, pg) = refs[6:8], refs[8:]
    e = first + pl.program_id(0)
    chip, core = info[0], info[1]
    dev_rows = local * BLK
    chip_blocks = pair * local
    wide = n_vert * BLK
    step = min(2 * BLK, wide)
    factor = math.log2(math.e) / math.sqrt(HD)

    def within(i):
        return (core ^ i // local) * local + i % local if pair > 1 else i

    def hidden(i, j):
        here = chip * chip_blocks + within(i)
        found = vert[e, j] >= here
        for u in range(n_slash):
            found = found | (vert[e, j] == here - slash[e, u])
        return found

    per = heads * n_vert // plane
    row = lax.broadcasted_iota(jnp.int32, (HD, BLK), 0)
    for j in range(n_vert):
        flat = e * n_vert + j
        src = pl.multiple_of(((flat // per ^ chip % plane) * per + flat % per) * BLK, BLK)
        rows = slice(j * BLK, (j + 1) * BLK)
        ke[:HD, rows] = kv_vert[pl.ds(src, BLK), :HD]
        ve[rows, :HD] = kv_vert[pl.ds(src, BLK), HD:]
        bias = jnp.zeros((HD, BLK), jnp.float32)
        for i in range(chip_blocks):
            bias = jnp.where((row == i) & hidden(i, j), MASKED, bias)
        ke[HD:, rows] = bias.astype(ke.dtype)
    ve[:, HD:] = jnp.ones((wide, HD), ve.dtype)
    block_rows = group * BLK
    for i in range(chip_blocks):
        slot, b = divmod(i, local)
        mark = onehot_rows((BLK, HD), lambda row, i=i: i, qx.dtype)
        for g in range(group):
            rows = slice(i * block_rows + g * BLK, i * block_rows + (g + 1) * BLK)
            qx[rows, :HD] = q_refs[slot][b * BLK : (b + 1) * BLK, g * HD : (g + 1) * HD]
            qx[rows, HD:] = mark

    def stage(t, at, ahead, behind):
        last = isinstance(t, int) and t == tiles
        if behind:
            rows = slice((t - 1) * step, t * step)
            if not isinstance(t, int):
                rows = pl.ds(pl.multiple_of((t - 1) * step, step), step)
            part = jnp.dot(ps[1 - at][...], ve[rows, :], preferred_element_type=jnp.float32)
            acc[...] = acc[...] + part
        else:
            for i in range(chip_blocks):
                acc[i * block_rows : (i + 1) * block_rows, :] = before[i]
        if last:
            return
        cols = slice(t * step, (t + 1) * step)
        if not isinstance(t, int):
            cols = pl.ds(pl.multiple_of(t * step, step), step)
        ps[at][...] = exponentials(qx[...], ke[:, cols], factor).astype(ps[at].dtype)

    tiles = wide // step
    pipelined(tiles, stage)
    good[...] = jnp.ones(good.shape, good.dtype)
    for i in range(chip_blocks):
        rows = slice(i * block_rows, (i + 1) * block_rows)
        total = acc[rows, HD:]
        res[i] = (acc[rows, :HD] / total).astype(res.dtype)
        fine = jnp.where((total > SMALLEST) & (total < LARGEST), 1.0, 0.0)
        good[...] = jnp.minimum(good[...], jnp.min(fine, axis=0, keepdims=True))

    @pl.when(jnp.logical_not(jnp.min(good[...]) > 0.5))
    def _():
        vg[: n_slash * BLK, HD:] = jnp.ones((n_slash * BLK, HD), vg.dtype)
        kg[:, n_slash * BLK :] = ke[...]
        vg[n_slash * BLK :, :] = ve[...]
        eye = onehot_rows((BLK, HD), lambda row: row, qx.dtype)

        def shifted_block(i, carry):
            here = chip * chip_blocks + within(i)
            q_rows = pl.ds(pl.multiple_of(i * block_rows, block_rows), block_rows)
            for g in range(group):
                at = pl.ds(pl.multiple_of(i * block_rows + g * BLK, BLK), BLK)
                qx[at, HD:] = eye
            for j in range(n_slash):
                off = slash[e, j]
                pos = reach * chip_blocks + within(i) - off
                back = reach - pos // chip_blocks
                src = pos % chip_blocks
                if pair > 1:
                    src = (src // local ^ core) * local + src % local
                at = pl.ds(pl.multiple_of(src * BLK, BLK), BLK)
                found = w_refs[0][at, :]
                for d in range(1, reach + 1):
                    found = jnp.where(back == d, w_refs[d][at, :], found)
                rows = slice(j * BLK, (j + 1) * BLK)
                kg[:HD, rows] = found[:, :HD]
                vg[rows, :HD] = found[:, HD:]
                kg[HD:, rows] = masks[jnp.where(off > here, 2, jnp.where(off == 0, 1, 0))]
            for j in range(n_vert):
                rows = slice((n_slash + j) * BLK, (n_slash + j + 1) * BLK)
                kg[HD:, rows] = masks[jnp.where(hidden(i, j), 2, 0)]
            top = None
            for t in range(0, kg.shape[1], step):
                s = jnp.dot(qx[q_rows, :], kg[:, t : t + step], preferred_element_type=jnp.float32)
                sc[:, t : t + step] = s
                for u in range(0, step, HD):
                    piece = s[:, u : u + HD]
                    top = piece if top is None else jnp.maximum(top, piece)
            top = jnp.max(top, axis=1, keepdims=True)
            for t in range(0, kg.shape[1], step):
                p = jnp.exp2((sc[:, t : t + step] - top) * factor)
                pg[:, t : t + step] = p.astype(pg.dtype)
            sums = jnp.dot(pg[...], vg[...], preferred_element_type=jnp.float32)
            res[i] = (sums[:, :HD] / sums[:, HD:]).astype(res.dtype)
            return carry

        lax.fori_loop(0, chip_blocks, shifted_block, 0)

    for i in range(chip_blocks):
        slot, b = divmod(i, local)
        for g in range(group):
            out_refs[slot][b * BLK : (b + 1) * BLK, g * HD : (g + 1) * HD] = res[
                i, g * BLK : (g + 1) * BLK
            ]


class Attention:
    def __init__(self, queries, q_other, info, vert, slash, masks, heads, local, plane):
        self.pair = 1 if q_other is None else 2
        self.qs = [queries] if q_other is None else [queries, q_other]
        self.info, self.vert, self.slash, self.masks = info, vert, slash, masks
        self.heads, self.local, self.plane = heads, local, plane
        self.dev_rows = queries.shape[0]
        self.wide = queries.shape[1] // (self.pair * heads)
        self.group = self.wide // HD
        self.blocks = self.pair * local
        self.dtype = queries.dtype

    def specs(self, first, windows):
        heads, shape = self.heads, (self.dev_rows, self.wide)
        specs = [pl.BlockSpec(shape, lambda i, info, *_: (0, info[1] * heads + first + i))]
        if self.pair > 1:
            at = self.qs[1].shape[1] // self.wide - heads + first
            specs.append(pl.BlockSpec(shape, lambda i, *_: (0, at + i)))
        return specs + [pl.BlockSpec((w.shape[0], 2 * HD), lambda i, *_: (0, i)) for w in windows]

    def whole(self, a):
        return pl.BlockSpec(a.shape, lambda i, *_: (0,) * a.ndim)

    def cost(self, n, width, more):
        rows = n * self.blocks * self.group * BLK
        return pl.CostEstimate(
            flops=8 * rows * width * HD,
            bytes_accessed=rows * HD * 2 + more,
            transcendentals=rows * width,
        )

    def acc_spec(self):
        shape = (self.blocks, self.group * BLK, 2 * HD)
        return pl.BlockSpec((None, *shape), lambda i, *_: (i, 0, 0, 0))

    def over_slash(self, first, n, windows):
        n_slash = self.slash.shape[1]
        width, rows = n_slash * BLK, self.group * BLK
        shape = (n, self.blocks, rows, 2 * HD)
        cfg = (first, self.pair, self.local, self.group, len(windows) - 1, n_slash)
        return pl.pallas_call(
            functools.partial(slash_kernel, cfg),
            grid_spec=pltpu.PrefetchScalarGridSpec(
                num_scalar_prefetch=2,
                grid=(n,),
                in_specs=self.specs(first, windows) + [self.whole(self.masks)],
                out_specs=self.acc_spec(),
                scratch_shapes=[
                    pltpu.VMEM((sum(w.shape[0] for w in windows), 2 * HD), self.dtype),
                    pltpu.VMEM((self.blocks, rows, 2 * HD), self.dtype),
                ]
                + [pltpu.VMEM((2 * HD, width), self.dtype)] * 2
                + [pltpu.VMEM((width, 2 * HD), self.dtype)] * 2
                + [pltpu.VMEM((rows, width), self.dtype)] * 2,
            ),
            out_shape=jax.ShapeDtypeStruct(shape, jnp.float32),
            compiler_params=pltpu.CompilerParams(vmem_limit_bytes=VMEM_LIMIT),
            cost_estimate=self.cost(n, width, 4 * math.prod(shape)),
            name="attend_slash",
        )(self.info, self.slash, *self.qs, *windows, self.masks)

    def over_vertical(self, first, n, windows, before, kv_vert):
        n_slash, n_vert = self.slash.shape[1], self.vert.shape[1]
        width, both, rows = n_vert * BLK, (n_slash + n_vert) * BLK, self.group * BLK
        cfg = (first, self.pair, self.local, self.group, len(windows) - 1, n_slash, n_vert)
        out = pl.BlockSpec((self.dev_rows, self.wide), lambda i, *_: (0, i))
        return pl.pallas_call(
            functools.partial(vertical_kernel, cfg + (self.plane, self.heads)),
            grid_spec=pltpu.PrefetchScalarGridSpec(
                num_scalar_prefetch=3,
                grid=(n,),
                in_specs=self.specs(first, windows)
                + [self.acc_spec(), self.whole(kv_vert), self.whole(self.masks)],
                out_specs=[out] * self.pair,
                scratch_shapes=[
                    pltpu.VMEM((2 * HD, width), self.dtype),
                    pltpu.VMEM((width, 2 * HD), self.dtype),
                    pltpu.VMEM((self.blocks * rows, 2 * HD), self.dtype),
                    pltpu.VMEM((self.blocks, rows, HD), self.dtype),
                    pltpu.VMEM((1, HD), jnp.float32),
                    pltpu.VMEM((self.blocks * rows, 2 * HD), jnp.float32),
                    pltpu.VMEM((self.blocks * rows, 2 * BLK), self.dtype),
                    pltpu.VMEM((self.blocks * rows, 2 * BLK), self.dtype),
                    pltpu.VMEM((2 * HD, both), self.dtype),
                    pltpu.VMEM((both, 2 * HD), self.dtype),
                    pltpu.VMEM((rows, both), jnp.float32),
                    pltpu.VMEM((rows, both), self.dtype),
                ],
            ),
            out_shape=[jax.ShapeDtypeStruct((self.dev_rows, n * self.wide), self.dtype)]
            * self.pair,
            compiler_params=pltpu.CompilerParams(vmem_limit_bytes=VMEM_LIMIT),
            cost_estimate=self.cost(n, width, 4 * math.prod(before.shape)),
            name="attend_vertical",
        )(self.info, self.vert, self.slash, *self.qs, *windows, before, kv_vert, self.masks)


def body(queries, keys, values, vertical_blocks, slash_offsets, out_weight):
    tokens_dev = queries.shape[0]
    kv_heads = keys.shape[1] // HD
    local = tokens_dev // BLK
    size = lax.axis_size("ctx")
    pair = 2 if kv_heads % 2 == 0 and size % 2 == 0 and lax.axis_size("head") == 1 else 1
    chips = size // pair
    heads = kv_heads // pair
    plane = PLANE if chips % PLANE == 0 and heads * vertical_blocks.shape[1] % PLANE == 0 else 1
    chip_blocks = pair * local
    reach = -(-MAXOFF // chip_blocks)
    index = lax.axis_index("ctx")
    chip, core = index // pair, index % pair
    info = jnp.stack([chip, core]).astype(jnp.int32)
    pos = jnp.arange(BLK)
    causal = jnp.where(pos[:, None] < pos[None, :], MASKED, 0.0)
    masks = jnp.stack([jnp.zeros_like(causal), causal, jnp.full_like(causal, MASKED)])
    masks = masks.astype(queries.dtype)

    def part(value, axis, which):
        span = value.shape[axis] // pair
        return lax.dynamic_slice_in_dim(value, which * span, span, axis)

    vert, slash = part(vertical_blocks, 0, core), part(slash_offsets, 0, core)
    kv_other = None
    if pair == 2:
        kv_other = crossed(jnp.concatenate([part(a, 1, 1 - core) for a in (keys, values)], 1), 1)
    per_chunk = 2 if heads % 2 == 0 else 1
    own, listed = prepare(info, vert, keys, values, kv_other, heads, local, plane, per_chunk)

    total = listed[0]
    for k in range(1, plane):
        total = total + crossed(listed[k], k * pair)
    q_sent = part(queries, 1, 1 - core) if pair == 2 else None
    total, own[0], q_sent = lax.optimization_barrier((total, own[0], q_sent))
    q_other = crossed(q_sent, 1) if pair == 2 else None
    step = 1
    while step < chips // plane:
        total = total + shifted(total, step * plane * pair)
        if step == 1:
            total, q_other, own[1:] = lax.optimization_barrier((total, q_other, own[1:]))
        step *= 2

    attention = Attention(queries, q_other, info, vert, slash, masks, heads, local, plane)
    chunks = heads // per_chunk
    all_windows, sums = [], []
    for c in range(chunks):
        windows = [own[c]]
        if pair == 2 and reach == 2 and chips % 2 == 0:
            two_back = shifted(own[c], 2 * pair)
            passed = jnp.where(chip % 2 == 0, own[c], two_back)
            windows += [crossed(passed, pair), two_back]
        else:
            windows += [shifted(own[c], pair * d) for d in range(1, reach + 1)]
        all_windows.append(windows)
        sums.append(attention.over_slash(c * per_chunk, per_chunk, windows))
    gathered = [total] + [crossed(total, k * pair) for k in range(1, plane)]
    gathered, sums[0] = lax.optimization_barrier((gathered, sums[0]))
    kv_vert = jnp.concatenate(gathered, 0)
    near, far = [], []
    for c in range(chunks):
        att = attention.over_vertical(c * per_chunk, per_chunk, all_windows[c], sums[c], kv_vert)
        near.append(att[0])
        if pair == 2:
            far.append(crossed(att[1], 1))
    attended = near
    if pair == 2:
        attended = [jnp.where(core == 0, a, b) for a, b in zip(near, far)]
        attended += [jnp.where(core == 0, b, a) for a, b in zip(near, far)]
    attended = lax.all_gather(jnp.concatenate(attended, 1), "head", axis=1, tiled=True)
    output = jnp.dot(attended, out_weight, preferred_element_type=jnp.float32)
    return output.astype(jnp.bfloat16)


def solution(mesh):
    placed = (
        P("ctx", "head"),
        P("ctx", "head"),
        P("ctx", "head"),
        P("head", None),
        P("head", None),
        P(None, "head"),
    )
    return jax.shard_map(
        body, mesh=mesh, in_specs=placed, out_specs=P("ctx", "head"), check_vma=False
    )
```

```python
import functools
import math

import jax
import jax.numpy as jnp
from jax import lax
from jax.experimental import pallas as pl
from jax.experimental.pallas import tpu as pltpu
from jax.sharding import PartitionSpec as P

HD = 128
BLK = 128
MAXOFF = 16
PLANE = 4
MASKED = -1e30
SMALLEST, LARGEST = 2.0**-60, 2.0**100
VMEM_LIMIT = 56 * 1024 * 1024


def shifted(value, by):
    size = lax.axis_size("ctx")
    return lax.ppermute(value, "ctx", [(i, i + by) for i in range(size - by)])


def crossed(value, bits):
    size = lax.axis_size("ctx")
    return lax.ppermute(value, "ctx", [(i, i ^ bits) for i in range(size)])


def prepare_kernel(cfg, info, vert, *refs):
    pair, local, heads, plane, per_chunk = cfg
    chip, core = info[0], info[1]
    keys, values = refs[:2]
    refs = refs[2:]
    other = None
    if pair > 1:
        other, refs = refs[0], refs[1:]
    n_chunks = heads // per_chunk
    chip_outs, refs = refs[:n_chunks], refs[n_chunks:]
    list_outs, chip_kv = refs[:plane], refs[plane]
    n_vert = vert.shape[1]
    dev_rows = local * BLK
    chip_blocks = pair * local
    for e in range(heads):
        at = pl.multiple_of((core * heads + e) * HD, HD)
        chip_kv[e, :dev_rows, HD:] = values[:, pl.ds(at, HD)]
        if pair > 1:
            chip_kv[e, dev_rows:, HD:] = other[:, (heads + e) * HD : (heads + e + 1) * HD]
        for b in range(pair * local):
            rows = slice(b % local * BLK, (b % local + 1) * BLK)
            block = keys[rows, pl.ds(at, HD)] if b < local else other[rows, e * HD : (e + 1) * HD]
            chip_kv[e, b * BLK : (b + 1) * BLK, :HD] = block.T
        c, at = divmod(e, per_chunk)
        chip_outs[c][:, at * 2 * HD : (at + 1) * 2 * HD] = chip_kv[e]
    per = heads * n_vert // plane
    for k in range(plane):
        for i in range(per):
            flat = (chip % plane ^ k) * per + i
            e, j = flat // n_vert, flat % n_vert
            block = vert[e, j]
            within = block % chip_blocks
            if pair > 1:
                within = (within // local ^ core) * local + within % local
            rows = slice(i * BLK, (i + 1) * BLK)
            owned = block // chip_blocks == chip
            found = chip_kv[e, pl.ds(pl.multiple_of(within * BLK, BLK), BLK), :]
            list_outs[k][rows, :] = jnp.where(owned, found, jnp.zeros_like(found))


def prepare(info, vert, keys, values, other, heads, local, plane, per_chunk):
    pair = 1 if other is None else 2
    chip_rows = pair * local * BLK
    n_chunks = heads // per_chunk
    per = heads * vert.shape[1] // plane
    dtype = keys.dtype
    smem = pl.BlockSpec(memory_space=pltpu.SMEM)
    vmem = pl.BlockSpec(memory_space=pltpu.VMEM)
    data = [keys, values] + ([] if other is None else [other])
    specs = [vmem] * 2
    if other is not None:
        specs.append(pl.BlockSpec((other.shape[0], heads * 2 * HD), lambda i: (0, 0)))
    outs = pl.pallas_call(
        functools.partial(prepare_kernel, (pair, local, heads, plane, per_chunk)),
        grid=(1,),
        in_specs=[smem] * 2 + specs,
        out_specs=[vmem] * (n_chunks + plane),
        out_shape=[jax.ShapeDtypeStruct((chip_rows, per_chunk * 2 * HD), dtype)] * n_chunks
        + [jax.ShapeDtypeStruct((per * BLK, 2 * HD), dtype)] * plane,
        scratch_shapes=[pltpu.VMEM((heads, chip_rows, 2 * HD), dtype)],
        compiler_params=pltpu.CompilerParams(vmem_limit_bytes=VMEM_LIMIT),
        cost_estimate=pl.CostEstimate(
            flops=0, bytes_accessed=8 * heads * chip_rows * 2 * HD, transcendentals=0
        ),
        name="prepare",
    )(info, vert, *data)
    return list(outs[:n_chunks]), list(outs[n_chunks:])


def onehot_rows(shape, at, dtype):
    row = lax.broadcasted_iota(jnp.int32, shape, 0)
    col = lax.broadcasted_iota(jnp.int32, shape, 1)
    return jnp.where(col == at(row), 1.0, 0.0).astype(dtype)


def exponentials(q, k, factor):
    return jnp.exp2(jnp.dot(q, k, preferred_element_type=jnp.float32) * factor)


def pipelined(blocks, stage):
    stage(0, 0, blocks > 1, False)

    def two_blocks(n, carry):
        stage(2 * n + 1, 1, True, True)
        stage(2 * n + 2, 0, True, True)
        return carry

    inner = max(blocks - 2, 0) // 2
    lax.fori_loop(0, inner, two_blocks, 0)
    for i in range(2 * inner + 1, blocks):
        stage(i, i % 2, i + 1 < blocks, True)
    stage(blocks, blocks % 2, False, True)


def slash_kernel(cfg, info, slash, *refs):
    first, pair, local, group, reach, n_slash = cfg
    q_refs, refs = refs[:pair], refs[pair:]
    w_refs, refs = refs[: reach + 1], refs[reach + 1 :]
    masks, acc, win, qx = refs[:4]
    kgs, vgs, ps = refs[4:6], refs[6:8], refs[8:10]
    e = first + pl.program_id(0)
    chip, core = info[0], info[1]
    dev_rows = local * BLK
    chip_blocks = pair * local
    chip_rows = chip_blocks * BLK
    width = n_slash * BLK
    factor = math.log2(math.e) / math.sqrt(HD)

    for back in range(reach + 1):
        for slot in range(pair):
            owner = core ^ slot if pair > 1 else 0
            at = pl.multiple_of((reach - back) * chip_rows + owner * dev_rows, dev_rows)
            rows = slice(slot * dev_rows, (slot + 1) * dev_rows)
            win[pl.ds(at, dev_rows), :] = w_refs[back][rows, :]
    for vg in vgs:
        vg[:, HD:] = jnp.ones((width, HD), vg.dtype)
    eye = onehot_rows((BLK, HD), lambda row: row, qx.dtype)
    for i in range(chip_blocks):
        slot, b = divmod(i, local)
        for g in range(group):
            rows = slice(g * BLK, (g + 1) * BLK)
            qx[i, rows, :HD] = q_refs[slot][b * BLK : (b + 1) * BLK, g * HD : (g + 1) * HD]
            qx[i, rows, HD:] = eye

    def within(i):
        return (core ^ i // local) * local + i % local if pair > 1 else i

    def take(i, j):
        src = (reach * chip_blocks + within(i) - slash[e, j]) * BLK
        return pl.ds(pl.multiple_of(src, BLK), BLK)

    def place_keys(i, at):
        here = chip * chip_blocks + within(i)
        for j in range(n_slash):
            off = slash[e, j]
            cols = slice(j * BLK, (j + 1) * BLK)
            kgs[at][:HD, cols] = win[take(i, j), :HD]
            kgs[at][HD:, cols] = masks[jnp.where(off > here, 2, jnp.where(off == 0, 1, 0))]

    def stage(i, at, ahead, behind):
        if ahead:
            place_keys(i + 1, 1 - at)
        if behind:
            acc[i - 1] = jnp.dot(
                ps[1 - at][...], vgs[1 - at][...], preferred_element_type=jnp.float32
            )
        if isinstance(i, int) and i == chip_blocks:
            return
        for j in range(n_slash):
            vgs[at][j * BLK : (j + 1) * BLK, :HD] = win[take(i, j), HD:]
        ps[at][...] = exponentials(qx[i], kgs[at][...], factor).astype(ps[at].dtype)

    place_keys(0, 0)
    pipelined(chip_blocks, stage)


def vertical_kernel(cfg, info, vert, slash, *refs):
    first, pair, local, group, reach, n_slash, n_vert, plane, heads = cfg
    q_refs, refs = refs[:pair], refs[pair:]
    w_refs, refs = refs[: reach + 1], refs[reach + 1 :]
    before, kv_vert, masks, refs = refs[0], refs[1], refs[2], refs[3:]
    out_refs, refs = refs[:pair], refs[pair:]
    ke, ve, qx, res, good, acc = refs[:6]
    ps, (kg, vg, sc, pg) = refs[6:8], refs[8:]
    e = first + pl.program_id(0)
    chip, core = info[0], info[1]
    dev_rows = local * BLK
    chip_blocks = pair * local
    wide = n_vert * BLK
    step = min(2 * BLK, wide)
    factor = math.log2(math.e) / math.sqrt(HD)

    def within(i):
        return (core ^ i // local) * local + i % local if pair > 1 else i

    def hidden(i, j):
        here = chip * chip_blocks + within(i)
        found = vert[e, j] >= here
        for u in range(n_slash):
            found = found | (vert[e, j] == here - slash[e, u])
        return found

    per = heads * n_vert // plane
    row = lax.broadcasted_iota(jnp.int32, (HD, BLK), 0)
    for j in range(n_vert):
        flat = e * n_vert + j
        src = pl.multiple_of(((flat // per ^ chip % plane) * per + flat % per) * BLK, BLK)
        rows = slice(j * BLK, (j + 1) * BLK)
        ke[:HD, rows] = kv_vert[pl.ds(src, BLK), :HD]
        ve[rows, :HD] = kv_vert[pl.ds(src, BLK), HD:]
        bias = jnp.zeros((HD, BLK), jnp.float32)
        for i in range(chip_blocks):
            bias = jnp.where((row == i) & hidden(i, j), MASKED, bias)
        ke[HD:, rows] = bias.astype(ke.dtype)
    ve[:, HD:] = jnp.ones((wide, HD), ve.dtype)
    block_rows = group * BLK
    for i in range(chip_blocks):
        slot, b = divmod(i, local)
        mark = onehot_rows((BLK, HD), lambda row, i=i: i, qx.dtype)
        for g in range(group):
            rows = slice(i * block_rows + g * BLK, i * block_rows + (g + 1) * BLK)
            qx[rows, :HD] = q_refs[slot][b * BLK : (b + 1) * BLK, g * HD : (g + 1) * HD]
            qx[rows, HD:] = mark

    def stage(t, at, ahead, behind):
        last = isinstance(t, int) and t == tiles
        if behind:
            rows = slice((t - 1) * step, t * step)
            if not isinstance(t, int):
                rows = pl.ds(pl.multiple_of((t - 1) * step, step), step)
            part = jnp.dot(ps[1 - at][...], ve[rows, :], preferred_element_type=jnp.float32)
            acc[...] = acc[...] + part
        else:
            for i in range(chip_blocks):
                acc[i * block_rows : (i + 1) * block_rows, :] = before[i]
        if last:
            return
        cols = slice(t * step, (t + 1) * step)
        if not isinstance(t, int):
            cols = pl.ds(pl.multiple_of(t * step, step), step)
        ps[at][...] = exponentials(qx[...], ke[:, cols], factor).astype(ps[at].dtype)

    tiles = wide // step
    pipelined(tiles, stage)
    good[...] = jnp.ones(good.shape, good.dtype)
    for i in range(chip_blocks):
        rows = slice(i * block_rows, (i + 1) * block_rows)
        total = acc[rows, HD:]
        res[i] = (acc[rows, :HD] / total).astype(res.dtype)
        fine = jnp.where((total > SMALLEST) & (total < LARGEST), 1.0, 0.0)
        good[...] = jnp.minimum(good[...], jnp.min(fine, axis=0, keepdims=True))

    @pl.when(jnp.logical_not(jnp.min(good[...]) > 0.5))
    def _():
        vg[: n_slash * BLK, HD:] = jnp.ones((n_slash * BLK, HD), vg.dtype)
        kg[:, n_slash * BLK :] = ke[...]
        vg[n_slash * BLK :, :] = ve[...]
        eye = onehot_rows((BLK, HD), lambda row: row, qx.dtype)

        def shifted_block(i, carry):
            here = chip * chip_blocks + within(i)
            q_rows = pl.ds(pl.multiple_of(i * block_rows, block_rows), block_rows)
            for g in range(group):
                at = pl.ds(pl.multiple_of(i * block_rows + g * BLK, BLK), BLK)
                qx[at, HD:] = eye
            for j in range(n_slash):
                off = slash[e, j]
                pos = reach * chip_blocks + within(i) - off
                back = reach - pos // chip_blocks
                src = pos % chip_blocks
                if pair > 1:
                    src = (src // local ^ core) * local + src % local
                at = pl.ds(pl.multiple_of(src * BLK, BLK), BLK)
                found = w_refs[0][at, :]
                for d in range(1, reach + 1):
                    found = jnp.where(back == d, w_refs[d][at, :], found)
                rows = slice(j * BLK, (j + 1) * BLK)
                kg[:HD, rows] = found[:, :HD]
                vg[rows, :HD] = found[:, HD:]
                kg[HD:, rows] = masks[jnp.where(off > here, 2, jnp.where(off == 0, 1, 0))]
            for j in range(n_vert):
                rows = slice((n_slash + j) * BLK, (n_slash + j + 1) * BLK)
                kg[HD:, rows] = masks[jnp.where(hidden(i, j), 2, 0)]
            top = None
            for t in range(0, kg.shape[1], step):
                s = jnp.dot(qx[q_rows, :], kg[:, t : t + step], preferred_element_type=jnp.float32)
                sc[:, t : t + step] = s
                for u in range(0, step, HD):
                    piece = s[:, u : u + HD]
                    top = piece if top is None else jnp.maximum(top, piece)
            top = jnp.max(top, axis=1, keepdims=True)
            for t in range(0, kg.shape[1], step):
                p = jnp.exp2((sc[:, t : t + step] - top) * factor)
                pg[:, t : t + step] = p.astype(pg.dtype)
            sums = jnp.dot(pg[...], vg[...], preferred_element_type=jnp.float32)
            res[i] = (sums[:, :HD] / sums[:, HD:]).astype(res.dtype)
            return carry

        lax.fori_loop(0, chip_blocks, shifted_block, 0)

    for i in range(chip_blocks):
        slot, b = divmod(i, local)
        for g in range(group):
            out_refs[slot][b * BLK : (b + 1) * BLK, g * HD : (g + 1) * HD] = res[
                i, g * BLK : (g + 1) * BLK
            ]


class Attention:
    def __init__(self, queries, q_other, info, vert, slash, masks, heads, local, plane):
        self.pair = 1 if q_other is None else 2
        self.qs = [queries] if q_other is None else [queries, q_other]
        self.info, self.vert, self.slash, self.masks = info, vert, slash, masks
        self.heads, self.local, self.plane = heads, local, plane
        self.dev_rows = queries.shape[0]
        self.wide = queries.shape[1] // (self.pair * heads)
        self.group = self.wide // HD
        self.blocks = self.pair * local
        self.dtype = queries.dtype

    def specs(self, first, windows):
        heads, shape = self.heads, (self.dev_rows, self.wide)
        specs = [pl.BlockSpec(shape, lambda i, info, *_: (0, info[1] * heads + first + i))]
        if self.pair > 1:
            at = self.qs[1].shape[1] // self.wide - heads + first
            specs.append(pl.BlockSpec(shape, lambda i, *_: (0, at + i)))
        return specs + [pl.BlockSpec((w.shape[0], 2 * HD), lambda i, *_: (0, i)) for w in windows]

    def whole(self, a):
        return pl.BlockSpec(a.shape, lambda i, *_: (0,) * a.ndim)

    def cost(self, n, width, more):
        rows = n * self.blocks * self.group * BLK
        return pl.CostEstimate(
            flops=8 * rows * width * HD,
            bytes_accessed=rows * HD * 2 + more,
            transcendentals=rows * width,
        )

    def acc_spec(self):
        shape = (self.blocks, self.group * BLK, 2 * HD)
        return pl.BlockSpec((None, *shape), lambda i, *_: (i, 0, 0, 0))

    def over_slash(self, first, n, windows):
        n_slash = self.slash.shape[1]
        width, rows = n_slash * BLK, self.group * BLK
        shape = (n, self.blocks, rows, 2 * HD)
        cfg = (first, self.pair, self.local, self.group, len(windows) - 1, n_slash)
        return pl.pallas_call(
            functools.partial(slash_kernel, cfg),
            grid_spec=pltpu.PrefetchScalarGridSpec(
                num_scalar_prefetch=2,
                grid=(n,),
                in_specs=self.specs(first, windows) + [self.whole(self.masks)],
                out_specs=self.acc_spec(),
                scratch_shapes=[
                    pltpu.VMEM((sum(w.shape[0] for w in windows), 2 * HD), self.dtype),
                    pltpu.VMEM((self.blocks, rows, 2 * HD), self.dtype),
                ]
                + [pltpu.VMEM((2 * HD, width), self.dtype)] * 2
                + [pltpu.VMEM((width, 2 * HD), self.dtype)] * 2
                + [pltpu.VMEM((rows, width), self.dtype)] * 2,
            ),
            out_shape=jax.ShapeDtypeStruct(shape, jnp.float32),
            compiler_params=pltpu.CompilerParams(vmem_limit_bytes=VMEM_LIMIT),
            cost_estimate=self.cost(n, width, 4 * math.prod(shape)),
            name="attend_slash",
        )(self.info, self.slash, *self.qs, *windows, self.masks)

    def over_vertical(self, first, n, windows, before, kv_vert):
        n_slash, n_vert = self.slash.shape[1], self.vert.shape[1]
        width, both, rows = n_vert * BLK, (n_slash + n_vert) * BLK, self.group * BLK
        cfg = (first, self.pair, self.local, self.group, len(windows) - 1, n_slash, n_vert)
        out = pl.BlockSpec((self.dev_rows, self.wide), lambda i, *_: (0, i))
        return pl.pallas_call(
            functools.partial(vertical_kernel, cfg + (self.plane, self.heads)),
            grid_spec=pltpu.PrefetchScalarGridSpec(
                num_scalar_prefetch=3,
                grid=(n,),
                in_specs=self.specs(first, windows)
                + [self.acc_spec(), self.whole(kv_vert), self.whole(self.masks)],
                out_specs=[out] * self.pair,
                scratch_shapes=[
                    pltpu.VMEM((2 * HD, width), self.dtype),
                    pltpu.VMEM((width, 2 * HD), self.dtype),
                    pltpu.VMEM((self.blocks * rows, 2 * HD), self.dtype),
                    pltpu.VMEM((self.blocks, rows, HD), self.dtype),
                    pltpu.VMEM((1, HD), jnp.float32),
                    pltpu.VMEM((self.blocks * rows, 2 * HD), jnp.float32),
                    pltpu.VMEM((self.blocks * rows, 2 * BLK), self.dtype),
                    pltpu.VMEM((self.blocks * rows, 2 * BLK), self.dtype),
                    pltpu.VMEM((2 * HD, both), self.dtype),
                    pltpu.VMEM((both, 2 * HD), self.dtype),
                    pltpu.VMEM((rows, both), jnp.float32),
                    pltpu.VMEM((rows, both), self.dtype),
                ],
            ),
            out_shape=[jax.ShapeDtypeStruct((self.dev_rows, n * self.wide), self.dtype)]
            * self.pair,
            compiler_params=pltpu.CompilerParams(vmem_limit_bytes=VMEM_LIMIT),
            cost_estimate=self.cost(n, width, 4 * math.prod(before.shape)),
            name="attend_vertical",
        )(self.info, self.vert, self.slash, *self.qs, *windows, before, kv_vert, self.masks)


def body(queries, keys, values, vertical_blocks, slash_offsets, out_weight):
    tokens_dev = queries.shape[0]
    kv_heads = keys.shape[1] // HD
    local = tokens_dev // BLK
    size = lax.axis_size("ctx")
    pair = 2 if kv_heads % 2 == 0 and size % 2 == 0 and lax.axis_size("head") == 1 else 1
    chips = size // pair
    heads = kv_heads // pair
    plane = PLANE if chips % PLANE == 0 and heads * vertical_blocks.shape[1] % PLANE == 0 else 1
    chip_blocks = pair * local
    reach = -(-MAXOFF // chip_blocks)
    index = lax.axis_index("ctx")
    chip, core = index // pair, index % pair
    info = jnp.stack([chip, core]).astype(jnp.int32)
    pos = jnp.arange(BLK)
    causal = jnp.where(pos[:, None] < pos[None, :], MASKED, 0.0)
    masks = jnp.stack([jnp.zeros_like(causal), causal, jnp.full_like(causal, MASKED)])
    masks = masks.astype(queries.dtype)

    def part(value, axis, which):
        span = value.shape[axis] // pair
        return lax.dynamic_slice_in_dim(value, which * span, span, axis)

    vert, slash = part(vertical_blocks, 0, core), part(slash_offsets, 0, core)
    kv_other = None
    if pair == 2:
        kv_other = crossed(jnp.concatenate([part(a, 1, 1 - core) for a in (keys, values)], 1), 1)
    per_chunk = 2 if heads % 2 == 0 else 1
    own, listed = prepare(info, vert, keys, values, kv_other, heads, local, plane, per_chunk)

    total = listed[0]
    for k in range(1, plane):
        total = total + crossed(listed[k], k * pair)
    two_back = [None] * len(own)
    passes_on = pair == 2 and reach == 2 and chips % 2 == 0
    if passes_on:
        two_back[0] = shifted(own[0], 2 * pair)
        two_back[0], own[1:], total = lax.optimization_barrier((two_back[0], own[1:], total))
        two_back[1:] = [shifted(w, 2 * pair) for w in own[1:]]
    q_other = crossed(part(queries, 1, 1 - core), 1) if pair == 2 else None
    step = 1
    while step < chips // plane:
        total = total + shifted(total, step * plane * pair)
        step *= 2

    attention = Attention(queries, q_other, info, vert, slash, masks, heads, local, plane)
    chunks = heads // per_chunk
    all_windows, sums = [], []
    for c in range(chunks):
        windows = [own[c]]
        if passes_on:
            passed = jnp.where(chip % 2 == 0, own[c], two_back[c])
            windows += [crossed(passed, pair), two_back[c]]
        else:
            windows += [shifted(own[c], pair * d) for d in range(1, reach + 1)]
        all_windows.append(windows)
        sums.append(attention.over_slash(c * per_chunk, per_chunk, windows))
    gathered = [total] + [crossed(total, k * pair) for k in range(1, plane)]
    gathered, sums = lax.optimization_barrier((gathered, sums))
    kv_vert = jnp.concatenate(gathered, 0)
    near, far = [], []
    for c in range(chunks):
        att = attention.over_vertical(c * per_chunk, per_chunk, all_windows[c], sums[c], kv_vert)
        near.append(att[0])
        if pair == 2:
            far.append(crossed(att[1], 1))
    attended = near
    if pair == 2:
        attended = [jnp.where(core == 0, a, b) for a, b in zip(near, far)]
        attended += [jnp.where(core == 0, b, a) for a, b in zip(near, far)]
    attended = lax.all_gather(jnp.concatenate(attended, 1), "head", axis=1, tiled=True)
    output = jnp.dot(attended, out_weight, preferred_element_type=jnp.float32)
    return output.astype(jnp.bfloat16)


def solution(mesh):
    placed = (
        P("ctx", "head"),
        P("ctx", "head"),
        P("ctx", "head"),
        P("head", None),
        P("head", None),
        P(None, "head"),
    )
    return jax.shard_map(
        body, mesh=mesh, in_specs=placed, out_specs=P("ctx", "head"), check_vma=False
    )
```

```python
import functools
import math

import jax
import jax.numpy as jnp
from jax import lax
from jax.experimental import pallas as pl
from jax.experimental.pallas import tpu as pltpu
from jax.sharding import PartitionSpec as P

HD = 128
BLK = 128
MAXOFF = 16
PLANE = 4
MASKED = -1e30
SMALLEST, LARGEST = 2.0**-60, 2.0**100
VMEM_LIMIT = 56 * 1024 * 1024


def shifted(value, by):
    size = lax.axis_size("ctx")
    return lax.ppermute(value, "ctx", [(i, i + by) for i in range(size - by)])


def crossed(value, bits):
    size = lax.axis_size("ctx")
    return lax.ppermute(value, "ctx", [(i, i ^ bits) for i in range(size)])


def prepare_kernel(cfg, info, vert, *refs):
    pair, local, heads, plane, per_chunk = cfg
    chip, core = info[0], info[1]
    keys, values = refs[:2]
    refs = refs[2:]
    other = None
    if pair > 1:
        other, refs = refs[0], refs[1:]
    n_chunks = heads // per_chunk
    chip_outs, refs = refs[:n_chunks], refs[n_chunks:]
    list_outs, chip_kv = refs[:plane], refs[plane]
    n_vert = vert.shape[1]
    dev_rows = local * BLK
    chip_blocks = pair * local
    for e in range(heads):
        at = pl.multiple_of((core * heads + e) * HD, HD)
        chip_kv[e, :dev_rows, HD:] = values[:, pl.ds(at, HD)]
        if pair > 1:
            chip_kv[e, dev_rows:, HD:] = other[:, (heads + e) * HD : (heads + e + 1) * HD]
        for b in range(pair * local):
            rows = slice(b % local * BLK, (b % local + 1) * BLK)
            block = keys[rows, pl.ds(at, HD)] if b < local else other[rows, e * HD : (e + 1) * HD]
            chip_kv[e, b * BLK : (b + 1) * BLK, :HD] = block.T
        c, at = divmod(e, per_chunk)
        chip_outs[c][:, at * 2 * HD : (at + 1) * 2 * HD] = chip_kv[e]
    per = heads * n_vert // plane
    for k in range(plane):
        for i in range(per):
            flat = (chip % plane ^ k) * per + i
            e, j = flat // n_vert, flat % n_vert
            block = vert[e, j]
            within = block % chip_blocks
            if pair > 1:
                within = (within // local ^ core) * local + within % local
            rows = slice(i * BLK, (i + 1) * BLK)
            owned = block // chip_blocks == chip
            found = chip_kv[e, pl.ds(pl.multiple_of(within * BLK, BLK), BLK), :]
            list_outs[k][rows, :] = jnp.where(owned, found, jnp.zeros_like(found))


def prepare(info, vert, keys, values, other, heads, local, plane, per_chunk):
    pair = 1 if other is None else 2
    chip_rows = pair * local * BLK
    n_chunks = heads // per_chunk
    per = heads * vert.shape[1] // plane
    dtype = keys.dtype
    smem = pl.BlockSpec(memory_space=pltpu.SMEM)
    vmem = pl.BlockSpec(memory_space=pltpu.VMEM)
    data = [keys, values] + ([] if other is None else [other])
    specs = [vmem] * 2
    if other is not None:
        specs.append(pl.BlockSpec((other.shape[0], heads * 2 * HD), lambda i: (0, 0)))
    outs = pl.pallas_call(
        functools.partial(prepare_kernel, (pair, local, heads, plane, per_chunk)),
        grid=(1,),
        in_specs=[smem] * 2 + specs,
        out_specs=[vmem] * (n_chunks + plane),
        out_shape=[jax.ShapeDtypeStruct((chip_rows, per_chunk * 2 * HD), dtype)] * n_chunks
        + [jax.ShapeDtypeStruct((per * BLK, 2 * HD), dtype)] * plane,
        scratch_shapes=[pltpu.VMEM((heads, chip_rows, 2 * HD), dtype)],
        compiler_params=pltpu.CompilerParams(vmem_limit_bytes=VMEM_LIMIT),
        cost_estimate=pl.CostEstimate(
            flops=0, bytes_accessed=8 * heads * chip_rows * 2 * HD, transcendentals=0
        ),
        name="prepare",
    )(info, vert, *data)
    return list(outs[:n_chunks]), list(outs[n_chunks:])


def onehot_rows(shape, at, dtype):
    row = lax.broadcasted_iota(jnp.int32, shape, 0)
    col = lax.broadcasted_iota(jnp.int32, shape, 1)
    return jnp.where(col == at(row), 1.0, 0.0).astype(dtype)


def exponentials(q, k, factor):
    return jnp.exp2(jnp.dot(q, k, preferred_element_type=jnp.float32) * factor)


def pipelined(blocks, stage):
    stage(0, 0, blocks > 1, False)

    def two_blocks(n, carry):
        stage(2 * n + 1, 1, True, True)
        stage(2 * n + 2, 0, True, True)
        return carry

    inner = max(blocks - 2, 0) // 2
    lax.fori_loop(0, inner, two_blocks, 0)
    for i in range(2 * inner + 1, blocks):
        stage(i, i % 2, i + 1 < blocks, True)
    stage(blocks, blocks % 2, False, True)


def slash_kernel(cfg, info, slash, *refs):
    first, pair, local, group, reach, n_slash = cfg
    q_refs, refs = refs[:pair], refs[pair:]
    w_refs, refs = refs[: reach + 1], refs[reach + 1 :]
    masks, acc, win, qx = refs[:4]
    kgs, vgs, ps = refs[4:6], refs[6:8], refs[8:10]
    e = first + pl.program_id(0)
    chip, core = info[0], info[1]
    dev_rows = local * BLK
    chip_blocks = pair * local
    chip_rows = chip_blocks * BLK
    width = n_slash * BLK
    factor = math.log2(math.e) / math.sqrt(HD)

    for back in range(reach + 1):
        for slot in range(pair):
            owner = core ^ slot if pair > 1 else 0
            at = pl.multiple_of((reach - back) * chip_rows + owner * dev_rows, dev_rows)
            rows = slice(slot * dev_rows, (slot + 1) * dev_rows)
            win[pl.ds(at, dev_rows), :] = w_refs[back][rows, :]
    for vg in vgs:
        vg[:, HD:] = jnp.ones((width, HD), vg.dtype)
    eye = onehot_rows((BLK, HD), lambda row: row, qx.dtype)
    for i in range(chip_blocks):
        slot, b = divmod(i, local)
        for g in range(group):
            rows = slice(g * BLK, (g + 1) * BLK)
            qx[i, rows, :HD] = q_refs[slot][b * BLK : (b + 1) * BLK, g * HD : (g + 1) * HD]
            qx[i, rows, HD:] = eye

    def within(i):
        return (core ^ i // local) * local + i % local if pair > 1 else i

    def take(i, j):
        src = (reach * chip_blocks + within(i) - slash[e, j]) * BLK
        return pl.ds(pl.multiple_of(src, BLK), BLK)

    def place_keys(i, at):
        here = chip * chip_blocks + within(i)
        for j in range(n_slash):
            off = slash[e, j]
            cols = slice(j * BLK, (j + 1) * BLK)
            kgs[at][:HD, cols] = win[take(i, j), :HD]
            kgs[at][HD:, cols] = masks[jnp.where(off > here, 2, jnp.where(off == 0, 1, 0))]

    def stage(i, at, ahead, behind):
        if ahead:
            place_keys(i + 1, 1 - at)
        if behind:
            acc[i - 1] = jnp.dot(
                ps[1 - at][...], vgs[1 - at][...], preferred_element_type=jnp.float32
            )
        if isinstance(i, int) and i == chip_blocks:
            return
        for j in range(n_slash):
            vgs[at][j * BLK : (j + 1) * BLK, :HD] = win[take(i, j), HD:]
        ps[at][...] = exponentials(qx[i], kgs[at][...], factor).astype(ps[at].dtype)

    place_keys(0, 0)
    pipelined(chip_blocks, stage)


def vertical_kernel(cfg, info, vert, slash, *refs):
    first, pair, local, group, reach, n_slash, n_vert, plane, heads = cfg
    q_refs, refs = refs[:pair], refs[pair:]
    w_refs, refs = refs[: reach + 1], refs[reach + 1 :]
    before, kv_vert, masks, refs = refs[0], refs[1], refs[2], refs[3:]
    out_refs, refs = refs[:pair], refs[pair:]
    ke, ve, qx, res, good, acc = refs[:6]
    ps, (kg, vg, sc, pg) = refs[6:8], refs[8:]
    e = first + pl.program_id(0)
    chip, core = info[0], info[1]
    dev_rows = local * BLK
    chip_blocks = pair * local
    wide = n_vert * BLK
    step = min(2 * BLK, wide)
    factor = math.log2(math.e) / math.sqrt(HD)

    def within(i):
        return (core ^ i // local) * local + i % local if pair > 1 else i

    def hidden(i, j):
        here = chip * chip_blocks + within(i)
        found = vert[e, j] >= here
        for u in range(n_slash):
            found = found | (vert[e, j] == here - slash[e, u])
        return found

    per = heads * n_vert // plane
    row = lax.broadcasted_iota(jnp.int32, (HD, BLK), 0)
    for j in range(n_vert):
        flat = e * n_vert + j
        src = pl.multiple_of(((flat // per ^ chip % plane) * per + flat % per) * BLK, BLK)
        rows = slice(j * BLK, (j + 1) * BLK)
        ke[:HD, rows] = kv_vert[pl.ds(src, BLK), :HD]
        ve[rows, :HD] = kv_vert[pl.ds(src, BLK), HD:]
        bias = jnp.zeros((HD, BLK), jnp.float32)
        for i in range(chip_blocks):
            bias = jnp.where((row == i) & hidden(i, j), MASKED, bias)
        ke[HD:, rows] = bias.astype(ke.dtype)
    ve[:, HD:] = jnp.ones((wide, HD), ve.dtype)
    block_rows = group * BLK
    for i in range(chip_blocks):
        slot, b = divmod(i, local)
        mark = onehot_rows((BLK, HD), lambda row, i=i: i, qx.dtype)
        for g in range(group):
            rows = slice(i * block_rows + g * BLK, i * block_rows + (g + 1) * BLK)
            qx[rows, :HD] = q_refs[slot][b * BLK : (b + 1) * BLK, g * HD : (g + 1) * HD]
            qx[rows, HD:] = mark

    def stage(t, at, ahead, behind):
        last = isinstance(t, int) and t == tiles
        if behind:
            rows = slice((t - 1) * step, t * step)
            if not isinstance(t, int):
                rows = pl.ds(pl.multiple_of((t - 1) * step, step), step)
            part = jnp.dot(ps[1 - at][...], ve[rows, :], preferred_element_type=jnp.float32)
            acc[...] = acc[...] + part
        else:
            for i in range(chip_blocks):
                acc[i * block_rows : (i + 1) * block_rows, :] = before[i]
        if last:
            return
        cols = slice(t * step, (t + 1) * step)
        if not isinstance(t, int):
            cols = pl.ds(pl.multiple_of(t * step, step), step)
        ps[at][...] = exponentials(qx[...], ke[:, cols], factor).astype(ps[at].dtype)

    tiles = wide // step
    pipelined(tiles, stage)
    good[...] = jnp.ones(good.shape, good.dtype)
    for i in range(chip_blocks):
        rows = slice(i * block_rows, (i + 1) * block_rows)
        total = acc[rows, HD:]
        res[i] = (acc[rows, :HD] / total).astype(res.dtype)
        fine = jnp.where((total > SMALLEST) & (total < LARGEST), 1.0, 0.0)
        good[...] = jnp.minimum(good[...], jnp.min(fine, axis=0, keepdims=True))

    @pl.when(jnp.logical_not(jnp.min(good[...]) > 0.5))
    def _():
        vg[: n_slash * BLK, HD:] = jnp.ones((n_slash * BLK, HD), vg.dtype)
        kg[:, n_slash * BLK :] = ke[...]
        vg[n_slash * BLK :, :] = ve[...]
        eye = onehot_rows((BLK, HD), lambda row: row, qx.dtype)

        def shifted_block(i, carry):
            here = chip * chip_blocks + within(i)
            q_rows = pl.ds(pl.multiple_of(i * block_rows, block_rows), block_rows)
            for g in range(group):
                at = pl.ds(pl.multiple_of(i * block_rows + g * BLK, BLK), BLK)
                qx[at, HD:] = eye
            for j in range(n_slash):
                off = slash[e, j]
                pos = reach * chip_blocks + within(i) - off
                back = reach - pos // chip_blocks
                src = pos % chip_blocks
                if pair > 1:
                    src = (src // local ^ core) * local + src % local
                at = pl.ds(pl.multiple_of(src * BLK, BLK), BLK)
                found = w_refs[0][at, :]
                for d in range(1, reach + 1):
                    found = jnp.where(back == d, w_refs[d][at, :], found)
                rows = slice(j * BLK, (j + 1) * BLK)
                kg[:HD, rows] = found[:, :HD]
                vg[rows, :HD] = found[:, HD:]
                kg[HD:, rows] = masks[jnp.where(off > here, 2, jnp.where(off == 0, 1, 0))]
            for j in range(n_vert):
                rows = slice((n_slash + j) * BLK, (n_slash + j + 1) * BLK)
                kg[HD:, rows] = masks[jnp.where(hidden(i, j), 2, 0)]
            top = None
            for t in range(0, kg.shape[1], step):
                s = jnp.dot(qx[q_rows, :], kg[:, t : t + step], preferred_element_type=jnp.float32)
                sc[:, t : t + step] = s
                for u in range(0, step, HD):
                    piece = s[:, u : u + HD]
                    top = piece if top is None else jnp.maximum(top, piece)
            top = jnp.max(top, axis=1, keepdims=True)
            for t in range(0, kg.shape[1], step):
                p = jnp.exp2((sc[:, t : t + step] - top) * factor)
                pg[:, t : t + step] = p.astype(pg.dtype)
            sums = jnp.dot(pg[...], vg[...], preferred_element_type=jnp.float32)
            res[i] = (sums[:, :HD] / sums[:, HD:]).astype(res.dtype)
            return carry

        lax.fori_loop(0, chip_blocks, shifted_block, 0)

    for i in range(chip_blocks):
        slot, b = divmod(i, local)
        for g in range(group):
            out_refs[slot][b * BLK : (b + 1) * BLK, g * HD : (g + 1) * HD] = res[
                i, g * BLK : (g + 1) * BLK
            ]


class Attention:
    def __init__(self, queries, q_other, info, vert, slash, masks, heads, local, plane):
        self.pair = 1 if q_other is None else 2
        self.qs = [queries] if q_other is None else [queries, q_other]
        self.info, self.vert, self.slash, self.masks = info, vert, slash, masks
        self.heads, self.local, self.plane = heads, local, plane
        self.dev_rows = queries.shape[0]
        self.wide = queries.shape[1] // (self.pair * heads)
        self.group = self.wide // HD
        self.blocks = self.pair * local
        self.dtype = queries.dtype

    def specs(self, first, windows):
        heads, shape = self.heads, (self.dev_rows, self.wide)
        specs = [pl.BlockSpec(shape, lambda i, info, *_: (0, info[1] * heads + first + i))]
        if self.pair > 1:
            at = self.qs[1].shape[1] // self.wide - heads + first
            specs.append(pl.BlockSpec(shape, lambda i, *_: (0, at + i)))
        return specs + [pl.BlockSpec((w.shape[0], 2 * HD), lambda i, *_: (0, i)) for w in windows]

    def whole(self, a):
        return pl.BlockSpec(a.shape, lambda i, *_: (0,) * a.ndim)

    def cost(self, n, width, more):
        rows = n * self.blocks * self.group * BLK
        return pl.CostEstimate(
            flops=8 * rows * width * HD,
            bytes_accessed=rows * HD * 2 + more,
            transcendentals=rows * width,
        )

    def acc_spec(self):
        shape = (self.blocks, self.group * BLK, 2 * HD)
        return pl.BlockSpec((None, *shape), lambda i, *_: (i, 0, 0, 0))

    def over_slash(self, first, n, windows):
        n_slash = self.slash.shape[1]
        width, rows = n_slash * BLK, self.group * BLK
        shape = (n, self.blocks, rows, 2 * HD)
        cfg = (first, self.pair, self.local, self.group, len(windows) - 1, n_slash)
        return pl.pallas_call(
            functools.partial(slash_kernel, cfg),
            grid_spec=pltpu.PrefetchScalarGridSpec(
                num_scalar_prefetch=2,
                grid=(n,),
                in_specs=self.specs(first, windows) + [self.whole(self.masks)],
                out_specs=self.acc_spec(),
                scratch_shapes=[
                    pltpu.VMEM((sum(w.shape[0] for w in windows), 2 * HD), self.dtype),
                    pltpu.VMEM((self.blocks, rows, 2 * HD), self.dtype),
                ]
                + [pltpu.VMEM((2 * HD, width), self.dtype)] * 2
                + [pltpu.VMEM((width, 2 * HD), self.dtype)] * 2
                + [pltpu.VMEM((rows, width), self.dtype)] * 2,
            ),
            out_shape=jax.ShapeDtypeStruct(shape, jnp.float32),
            compiler_params=pltpu.CompilerParams(vmem_limit_bytes=VMEM_LIMIT),
            cost_estimate=self.cost(n, width, 4 * math.prod(shape)),
            name="attend_slash",
        )(self.info, self.slash, *self.qs, *windows, self.masks)

    def over_vertical(self, first, n, windows, before, kv_vert):
        n_slash, n_vert = self.slash.shape[1], self.vert.shape[1]
        width, both, rows = n_vert * BLK, (n_slash + n_vert) * BLK, self.group * BLK
        cfg = (first, self.pair, self.local, self.group, len(windows) - 1, n_slash, n_vert)
        out = pl.BlockSpec((self.dev_rows, self.wide), lambda i, *_: (0, i))
        return pl.pallas_call(
            functools.partial(vertical_kernel, cfg + (self.plane, self.heads)),
            grid_spec=pltpu.PrefetchScalarGridSpec(
                num_scalar_prefetch=3,
                grid=(n,),
                in_specs=self.specs(first, windows)
                + [self.acc_spec(), self.whole(kv_vert), self.whole(self.masks)],
                out_specs=[out] * self.pair,
                scratch_shapes=[
                    pltpu.VMEM((2 * HD, width), self.dtype),
                    pltpu.VMEM((width, 2 * HD), self.dtype),
                    pltpu.VMEM((self.blocks * rows, 2 * HD), self.dtype),
                    pltpu.VMEM((self.blocks, rows, HD), self.dtype),
                    pltpu.VMEM((1, HD), jnp.float32),
                    pltpu.VMEM((self.blocks * rows, 2 * HD), jnp.float32),
                    pltpu.VMEM((self.blocks * rows, 2 * BLK), self.dtype),
                    pltpu.VMEM((self.blocks * rows, 2 * BLK), self.dtype),
                    pltpu.VMEM((2 * HD, both), self.dtype),
                    pltpu.VMEM((both, 2 * HD), self.dtype),
                    pltpu.VMEM((rows, both), jnp.float32),
                    pltpu.VMEM((rows, both), self.dtype),
                ],
            ),
            out_shape=[jax.ShapeDtypeStruct((self.dev_rows, n * self.wide), self.dtype)]
            * self.pair,
            compiler_params=pltpu.CompilerParams(vmem_limit_bytes=VMEM_LIMIT),
            cost_estimate=self.cost(n, width, 4 * math.prod(before.shape)),
            name="attend_vertical",
        )(self.info, self.vert, self.slash, *self.qs, *windows, before, kv_vert, self.masks)


def body(queries, keys, values, vertical_blocks, slash_offsets, out_weight):
    tokens_dev = queries.shape[0]
    kv_heads = keys.shape[1] // HD
    local = tokens_dev // BLK
    size = lax.axis_size("ctx")
    pair = 2 if kv_heads % 2 == 0 and size % 2 == 0 and lax.axis_size("head") == 1 else 1
    chips = size // pair
    heads = kv_heads // pair
    plane = PLANE if chips % PLANE == 0 and heads * vertical_blocks.shape[1] % PLANE == 0 else 1
    chip_blocks = pair * local
    reach = -(-MAXOFF // chip_blocks)
    index = lax.axis_index("ctx")
    chip, core = index // pair, index % pair
    info = jnp.stack([chip, core]).astype(jnp.int32)
    pos = jnp.arange(BLK)
    causal = jnp.where(pos[:, None] < pos[None, :], MASKED, 0.0)
    masks = jnp.stack([jnp.zeros_like(causal), causal, jnp.full_like(causal, MASKED)])
    masks = masks.astype(queries.dtype)

    def part(value, axis, which):
        span = value.shape[axis] // pair
        return lax.dynamic_slice_in_dim(value, which * span, span, axis)

    vert, slash = part(vertical_blocks, 0, core), part(slash_offsets, 0, core)
    kv_other = None
    if pair == 2:
        kv_other = crossed(jnp.concatenate([part(a, 1, 1 - core) for a in (keys, values)], 1), 1)
    per_chunk = 2 if heads % 2 == 0 else 1
    own, listed = prepare(info, vert, keys, values, kv_other, heads, local, plane, per_chunk)

    total = listed[0]
    for k in range(1, plane):
        total = total + crossed(listed[k], k * pair)
    two_back = [None] * len(own)
    passes_on = pair == 2 and reach == 2 and plane == 4
    if passes_on:
        upper = chip % plane >= 2
        stride = plane * pair
        pairs = [(i, i + stride) for i in range(size - stride) if i // pair % plane >= 2]
        risen = [lax.ppermute(w, "ctx", pairs) for w in own[1:]]
        two_back[0] = shifted(own[0], 2 * pair)
        two_back[0], risen, total = lax.optimization_barrier((two_back[0], risen, total))
        for c, w in enumerate(risen, 1):
            two_back[c] = crossed(jnp.where(upper, w, own[c]), 2 * pair)
    q_other = crossed(part(queries, 1, 1 - core), 1) if pair == 2 else None
    step = 1
    while step < chips // plane:
        total = total + shifted(total, step * plane * pair)
        step *= 2

    attention = Attention(queries, q_other, info, vert, slash, masks, heads, local, plane)
    chunks = heads // per_chunk
    all_windows, sums = [], []
    for c in range(chunks):
        windows = [own[c]]
        if passes_on:
            passed = jnp.where(chip % 2 == 0, own[c], two_back[c])
            windows += [crossed(passed, pair), two_back[c]]
        else:
            windows += [shifted(own[c], pair * d) for d in range(1, reach + 1)]
        all_windows.append(windows)
        sums.append(attention.over_slash(c * per_chunk, per_chunk, windows))
    gathered = [total] + [crossed(total, k * pair) for k in range(1, plane)]
    gathered, sums = lax.optimization_barrier((gathered, sums))
    kv_vert = jnp.concatenate(gathered, 0)
    near, far = [], []
    for c in range(chunks):
        att = attention.over_vertical(c * per_chunk, per_chunk, all_windows[c], sums[c], kv_vert)
        near.append(att[0])
        if pair == 2:
            far.append(crossed(att[1], 1))
    attended = near
    if pair == 2:
        attended = [jnp.where(core == 0, a, b) for a, b in zip(near, far)]
        attended += [jnp.where(core == 0, b, a) for a, b in zip(near, far)]
    attended = lax.all_gather(jnp.concatenate(attended, 1), "head", axis=1, tiled=True)
    output = jnp.dot(attended, out_weight, preferred_element_type=jnp.float32)
    return output.astype(jnp.bfloat16)


def solution(mesh):
    placed = (
        P("ctx", "head"),
        P("ctx", "head"),
        P("ctx", "head"),
        P("head", None),
        P("head", None),
        P(None, "head"),
    )
    return jax.shard_map(
        body, mesh=mesh, in_specs=placed, out_specs=P("ctx", "head"), check_vma=False
    )
```

```python
import functools
import math

import jax
import jax.numpy as jnp
from jax import lax
from jax.experimental import pallas as pl
from jax.experimental.pallas import tpu as pltpu
from jax.sharding import PartitionSpec as P

HD = 128
BLK = 128
MAXOFF = 16
PLANE = 4
MASKED = -1e30
SMALLEST, LARGEST = 2.0**-60, 2.0**100
VMEM_LIMIT = 56 * 1024 * 1024


def shifted(value, by):
    size = lax.axis_size("ctx")
    return lax.ppermute(value, "ctx", [(i, i + by) for i in range(size - by)])


def crossed(value, bits):
    size = lax.axis_size("ctx")
    return lax.ppermute(value, "ctx", [(i, i ^ bits) for i in range(size)])


def after(value, other):
    return lax.optimization_barrier((value, other))[0]


def prepare_kernel(cfg, info, vert, *refs):
    pair, local, heads, plane, per_chunk = cfg
    chip, core = info[0], info[1]
    keys, values = refs[:2]
    refs = refs[2:]
    other = None
    if pair > 1:
        other, refs = refs[0], refs[1:]
    n_chunks = heads // per_chunk
    chip_outs, refs = refs[:n_chunks], refs[n_chunks:]
    list_outs, chip_kv = refs[:plane], refs[plane]
    n_vert = vert.shape[1]
    dev_rows = local * BLK
    chip_blocks = pair * local
    for e in range(heads):
        at = pl.multiple_of((core * heads + e) * HD, HD)
        chip_kv[e, :dev_rows, HD:] = values[:, pl.ds(at, HD)]
        if pair > 1:
            chip_kv[e, dev_rows:, HD:] = other[:, (heads + e) * HD : (heads + e + 1) * HD]
        for b in range(pair * local):
            rows = slice(b % local * BLK, (b % local + 1) * BLK)
            block = keys[rows, pl.ds(at, HD)] if b < local else other[rows, e * HD : (e + 1) * HD]
            chip_kv[e, b * BLK : (b + 1) * BLK, :HD] = block.T
        c, at = divmod(e, per_chunk)
        chip_outs[c][:, at * 2 * HD : (at + 1) * 2 * HD] = chip_kv[e]
    per = heads * n_vert // plane
    for k in range(plane):
        for i in range(per):
            flat = (chip % plane ^ k) * per + i
            e, j = flat // n_vert, flat % n_vert
            block = vert[e, j]
            within = block % chip_blocks
            if pair > 1:
                within = (within // local ^ core) * local + within % local
            rows = slice(i * BLK, (i + 1) * BLK)
            owned = block // chip_blocks == chip
            found = chip_kv[e, pl.ds(pl.multiple_of(within * BLK, BLK), BLK), :]
            list_outs[k][rows, :] = jnp.where(owned, found, jnp.zeros_like(found))


def prepare(info, vert, keys, values, other, heads, local, plane, per_chunk):
    pair = 1 if other is None else 2
    chip_rows = pair * local * BLK
    n_chunks = heads // per_chunk
    per = heads * vert.shape[1] // plane
    dtype = keys.dtype
    smem = pl.BlockSpec(memory_space=pltpu.SMEM)
    vmem = pl.BlockSpec(memory_space=pltpu.VMEM)
    data = [keys, values] + ([] if other is None else [other])
    specs = [vmem] * 2
    if other is not None:
        specs.append(pl.BlockSpec((other.shape[0], heads * 2 * HD), lambda i: (0, 0)))
    outs = pl.pallas_call(
        functools.partial(prepare_kernel, (pair, local, heads, plane, per_chunk)),
        grid=(1,),
        in_specs=[smem] * 2 + specs,
        out_specs=[vmem] * (n_chunks + plane),
        out_shape=[jax.ShapeDtypeStruct((chip_rows, per_chunk * 2 * HD), dtype)] * n_chunks
        + [jax.ShapeDtypeStruct((per * BLK, 2 * HD), dtype)] * plane,
        scratch_shapes=[pltpu.VMEM((heads, chip_rows, 2 * HD), dtype)],
        compiler_params=pltpu.CompilerParams(vmem_limit_bytes=VMEM_LIMIT),
        cost_estimate=pl.CostEstimate(
            flops=0, bytes_accessed=8 * heads * chip_rows * 2 * HD, transcendentals=0
        ),
        name="prepare",
    )(info, vert, *data)
    return list(outs[:n_chunks]), list(outs[n_chunks:])


def onehot_rows(shape, at, dtype):
    row = lax.broadcasted_iota(jnp.int32, shape, 0)
    col = lax.broadcasted_iota(jnp.int32, shape, 1)
    return jnp.where(col == at(row), 1.0, 0.0).astype(dtype)


def exponentials(q, k, factor):
    return jnp.exp2(jnp.dot(q, k, preferred_element_type=jnp.float32) * factor)


def pipelined(blocks, stage):
    stage(0, 0, blocks > 1, False)

    def two_blocks(n, carry):
        stage(2 * n + 1, 1, True, True)
        stage(2 * n + 2, 0, True, True)
        return carry

    inner = max(blocks - 2, 0) // 2
    lax.fori_loop(0, inner, two_blocks, 0)
    for i in range(2 * inner + 1, blocks):
        stage(i, i % 2, i + 1 < blocks, True)
    stage(blocks, blocks % 2, False, True)


def slash_kernel(cfg, info, slash, *refs):
    first, pair, local, group, reach, n_slash = cfg
    q_refs, refs = refs[:pair], refs[pair:]
    w_refs, refs = refs[: reach + 1], refs[reach + 1 :]
    masks, acc, win, qx = refs[:4]
    kgs, vgs, ps = refs[4:6], refs[6:8], refs[8:10]
    e = first + pl.program_id(0)
    chip, core = info[0], info[1]
    dev_rows = local * BLK
    chip_blocks = pair * local
    chip_rows = chip_blocks * BLK
    width = n_slash * BLK
    factor = math.log2(math.e) / math.sqrt(HD)

    for back in range(reach + 1):
        for slot in range(pair):
            owner = core ^ slot if pair > 1 else 0
            at = pl.multiple_of((reach - back) * chip_rows + owner * dev_rows, dev_rows)
            rows = slice(slot * dev_rows, (slot + 1) * dev_rows)
            win[pl.ds(at, dev_rows), :] = w_refs[back][rows, :]
    for vg in vgs:
        vg[:, HD:] = jnp.ones((width, HD), vg.dtype)
    eye = onehot_rows((BLK, HD), lambda row: row, qx.dtype)
    for i in range(chip_blocks):
        slot, b = divmod(i, local)
        for g in range(group):
            rows = slice(g * BLK, (g + 1) * BLK)
            qx[i, rows, :HD] = q_refs[slot][b * BLK : (b + 1) * BLK, g * HD : (g + 1) * HD]
            qx[i, rows, HD:] = eye

    def within(i):
        return (core ^ i // local) * local + i % local if pair > 1 else i

    def take(i, j):
        src = (reach * chip_blocks + within(i) - slash[e, j]) * BLK
        return pl.ds(pl.multiple_of(src, BLK), BLK)

    def place_keys(i, at):
        here = chip * chip_blocks + within(i)
        for j in range(n_slash):
            off = slash[e, j]
            cols = slice(j * BLK, (j + 1) * BLK)
            kgs[at][:HD, cols] = win[take(i, j), :HD]
            kgs[at][HD:, cols] = masks[jnp.where(off > here, 2, jnp.where(off == 0, 1, 0))]

    def stage(i, at, ahead, behind):
        if ahead:
            place_keys(i + 1, 1 - at)
        if behind:
            acc[i - 1] = jnp.dot(
                ps[1 - at][...], vgs[1 - at][...], preferred_element_type=jnp.float32
            )
        if isinstance(i, int) and i == chip_blocks:
            return
        for j in range(n_slash):
            vgs[at][j * BLK : (j + 1) * BLK, :HD] = win[take(i, j), HD:]
        ps[at][...] = exponentials(qx[i], kgs[at][...], factor).astype(ps[at].dtype)

    place_keys(0, 0)
    pipelined(chip_blocks, stage)


def vertical_kernel(cfg, info, vert, slash, *refs):
    first, pair, local, group, reach, n_slash, n_vert, plane, heads = cfg
    q_refs, refs = refs[:pair], refs[pair:]
    w_refs, refs = refs[: reach + 1], refs[reach + 1 :]
    before, kv_vert, masks, refs = refs[0], refs[1], refs[2], refs[3:]
    out_refs, refs = refs[:pair], refs[pair:]
    ke, ve, qx, res, good, acc = refs[:6]
    ps, (kg, vg, sc, pg) = refs[6:8], refs[8:]
    e = first + pl.program_id(0)
    chip, core = info[0], info[1]
    dev_rows = local * BLK
    chip_blocks = pair * local
    wide = n_vert * BLK
    step = min(2 * BLK, wide)
    factor = math.log2(math.e) / math.sqrt(HD)

    def within(i):
        return (core ^ i // local) * local + i % local if pair > 1 else i

    def hidden(i, j):
        here = chip * chip_blocks + within(i)
        found = vert[e, j] >= here
        for u in range(n_slash):
            found = found | (vert[e, j] == here - slash[e, u])
        return found

    per = heads * n_vert // plane
    row = lax.broadcasted_iota(jnp.int32, (HD, BLK), 0)
    for j in range(n_vert):
        flat = e * n_vert + j
        src = pl.multiple_of(((flat // per ^ chip % plane) * per + flat % per) * BLK, BLK)
        rows = slice(j * BLK, (j + 1) * BLK)
        ke[:HD, rows] = kv_vert[pl.ds(src, BLK), :HD]
        ve[rows, :HD] = kv_vert[pl.ds(src, BLK), HD:]
        bias = jnp.zeros((HD, BLK), jnp.float32)
        for i in range(chip_blocks):
            bias = jnp.where((row == i) & hidden(i, j), MASKED, bias)
        ke[HD:, rows] = bias.astype(ke.dtype)
    ve[:, HD:] = jnp.ones((wide, HD), ve.dtype)
    block_rows = group * BLK
    for i in range(chip_blocks):
        slot, b = divmod(i, local)
        mark = onehot_rows((BLK, HD), lambda row, i=i: i, qx.dtype)
        for g in range(group):
            rows = slice(i * block_rows + g * BLK, i * block_rows + (g + 1) * BLK)
            qx[rows, :HD] = q_refs[slot][b * BLK : (b + 1) * BLK, g * HD : (g + 1) * HD]
            qx[rows, HD:] = mark

    def stage(t, at, ahead, behind):
        last = isinstance(t, int) and t == tiles
        if behind:
            rows = slice((t - 1) * step, t * step)
            if not isinstance(t, int):
                rows = pl.ds(pl.multiple_of((t - 1) * step, step), step)
            part = jnp.dot(ps[1 - at][...], ve[rows, :], preferred_element_type=jnp.float32)
            acc[...] = acc[...] + part
        else:
            for i in range(chip_blocks):
                acc[i * block_rows : (i + 1) * block_rows, :] = before[i]
        if last:
            return
        cols = slice(t * step, (t + 1) * step)
        if not isinstance(t, int):
            cols = pl.ds(pl.multiple_of(t * step, step), step)
        ps[at][...] = exponentials(qx[...], ke[:, cols], factor).astype(ps[at].dtype)

    tiles = wide // step
    pipelined(tiles, stage)
    good[...] = jnp.ones(good.shape, good.dtype)
    for i in range(chip_blocks):
        rows = slice(i * block_rows, (i + 1) * block_rows)
        total = acc[rows, HD:]
        res[i] = (acc[rows, :HD] / total).astype(res.dtype)
        fine = jnp.where((total > SMALLEST) & (total < LARGEST), 1.0, 0.0)
        good[...] = jnp.minimum(good[...], jnp.min(fine, axis=0, keepdims=True))

    @pl.when(jnp.logical_not(jnp.min(good[...]) > 0.5))
    def _():
        vg[: n_slash * BLK, HD:] = jnp.ones((n_slash * BLK, HD), vg.dtype)
        kg[:, n_slash * BLK :] = ke[...]
        vg[n_slash * BLK :, :] = ve[...]
        eye = onehot_rows((BLK, HD), lambda row: row, qx.dtype)

        def shifted_block(i, carry):
            here = chip * chip_blocks + within(i)
            q_rows = pl.ds(pl.multiple_of(i * block_rows, block_rows), block_rows)
            for g in range(group):
                at = pl.ds(pl.multiple_of(i * block_rows + g * BLK, BLK), BLK)
                qx[at, HD:] = eye
            for j in range(n_slash):
                off = slash[e, j]
                pos = reach * chip_blocks + within(i) - off
                back = reach - pos // chip_blocks
                src = pos % chip_blocks
                if pair > 1:
                    src = (src // local ^ core) * local + src % local
                at = pl.ds(pl.multiple_of(src * BLK, BLK), BLK)
                found = w_refs[0][at, :]
                for d in range(1, reach + 1):
                    found = jnp.where(back == d, w_refs[d][at, :], found)
                rows = slice(j * BLK, (j + 1) * BLK)
                kg[:HD, rows] = found[:, :HD]
                vg[rows, :HD] = found[:, HD:]
                kg[HD:, rows] = masks[jnp.where(off > here, 2, jnp.where(off == 0, 1, 0))]
            for j in range(n_vert):
                rows = slice((n_slash + j) * BLK, (n_slash + j + 1) * BLK)
                kg[HD:, rows] = masks[jnp.where(hidden(i, j), 2, 0)]
            top = None
            for t in range(0, kg.shape[1], step):
                s = jnp.dot(qx[q_rows, :], kg[:, t : t + step], preferred_element_type=jnp.float32)
                sc[:, t : t + step] = s
                for u in range(0, step, HD):
                    piece = s[:, u : u + HD]
                    top = piece if top is None else jnp.maximum(top, piece)
            top = jnp.max(top, axis=1, keepdims=True)
            for t in range(0, kg.shape[1], step):
                p = jnp.exp2((sc[:, t : t + step] - top) * factor)
                pg[:, t : t + step] = p.astype(pg.dtype)
            sums = jnp.dot(pg[...], vg[...], preferred_element_type=jnp.float32)
            res[i] = (sums[:, :HD] / sums[:, HD:]).astype(res.dtype)
            return carry

        lax.fori_loop(0, chip_blocks, shifted_block, 0)

    for i in range(chip_blocks):
        slot, b = divmod(i, local)
        for g in range(group):
            out_refs[slot][b * BLK : (b + 1) * BLK, g * HD : (g + 1) * HD] = res[
                i, g * BLK : (g + 1) * BLK
            ]


class Attention:
    def __init__(self, queries, q_other, info, vert, slash, masks, heads, local, plane):
        self.pair = 1 if q_other is None else 2
        self.qs = [queries] if q_other is None else [queries, q_other]
        self.info, self.vert, self.slash, self.masks = info, vert, slash, masks
        self.heads, self.local, self.plane = heads, local, plane
        self.dev_rows = queries.shape[0]
        self.wide = queries.shape[1] // (self.pair * heads)
        self.group = self.wide // HD
        self.blocks = self.pair * local
        self.dtype = queries.dtype

    def specs(self, first, windows):
        heads, shape = self.heads, (self.dev_rows, self.wide)
        specs = [pl.BlockSpec(shape, lambda i, info, *_: (0, info[1] * heads + first + i))]
        if self.pair > 1:
            at = self.qs[1].shape[1] // self.wide - heads + first
            specs.append(pl.BlockSpec(shape, lambda i, *_: (0, at + i)))
        return specs + [pl.BlockSpec((w.shape[0], 2 * HD), lambda i, *_: (0, i)) for w in windows]

    def whole(self, a):
        return pl.BlockSpec(a.shape, lambda i, *_: (0,) * a.ndim)

    def cost(self, n, width, more):
        rows = n * self.blocks * self.group * BLK
        return pl.CostEstimate(
            flops=8 * rows * width * HD,
            bytes_accessed=rows * HD * 2 + more,
            transcendentals=rows * width,
        )

    def acc_spec(self):
        shape = (self.blocks, self.group * BLK, 2 * HD)
        return pl.BlockSpec((None, *shape), lambda i, *_: (i, 0, 0, 0))

    def over_slash(self, first, n, windows):
        n_slash = self.slash.shape[1]
        width, rows = n_slash * BLK, self.group * BLK
        shape = (n, self.blocks, rows, 2 * HD)
        cfg = (first, self.pair, self.local, self.group, len(windows) - 1, n_slash)
        return pl.pallas_call(
            functools.partial(slash_kernel, cfg),
            grid_spec=pltpu.PrefetchScalarGridSpec(
                num_scalar_prefetch=2,
                grid=(n,),
                in_specs=self.specs(first, windows) + [self.whole(self.masks)],
                out_specs=self.acc_spec(),
                scratch_shapes=[
                    pltpu.VMEM((sum(w.shape[0] for w in windows), 2 * HD), self.dtype),
                    pltpu.VMEM((self.blocks, rows, 2 * HD), self.dtype),
                ]
                + [pltpu.VMEM((2 * HD, width), self.dtype)] * 2
                + [pltpu.VMEM((width, 2 * HD), self.dtype)] * 2
                + [pltpu.VMEM((rows, width), self.dtype)] * 2,
            ),
            out_shape=jax.ShapeDtypeStruct(shape, jnp.float32),
            compiler_params=pltpu.CompilerParams(vmem_limit_bytes=VMEM_LIMIT),
            cost_estimate=self.cost(n, width, 4 * math.prod(shape)),
            name="attend_slash",
        )(self.info, self.slash, *self.qs, *windows, self.masks)

    def over_vertical(self, first, n, windows, before, kv_vert):
        n_slash, n_vert = self.slash.shape[1], self.vert.shape[1]
        width, both, rows = n_vert * BLK, (n_slash + n_vert) * BLK, self.group * BLK
        cfg = (first, self.pair, self.local, self.group, len(windows) - 1, n_slash, n_vert)
        out = pl.BlockSpec((self.dev_rows, self.wide), lambda i, *_: (0, i))
        return pl.pallas_call(
            functools.partial(vertical_kernel, cfg + (self.plane, self.heads)),
            grid_spec=pltpu.PrefetchScalarGridSpec(
                num_scalar_prefetch=3,
                grid=(n,),
                in_specs=self.specs(first, windows)
                + [self.acc_spec(), self.whole(kv_vert), self.whole(self.masks)],
                out_specs=[out] * self.pair,
                scratch_shapes=[
                    pltpu.VMEM((2 * HD, width), self.dtype),
                    pltpu.VMEM((width, 2 * HD), self.dtype),
                    pltpu.VMEM((self.blocks * rows, 2 * HD), self.dtype),
                    pltpu.VMEM((self.blocks, rows, HD), self.dtype),
                    pltpu.VMEM((1, HD), jnp.float32),
                    pltpu.VMEM((self.blocks * rows, 2 * HD), jnp.float32),
                    pltpu.VMEM((self.blocks * rows, 2 * BLK), self.dtype),
                    pltpu.VMEM((self.blocks * rows, 2 * BLK), self.dtype),
                    pltpu.VMEM((2 * HD, both), self.dtype),
                    pltpu.VMEM((both, 2 * HD), self.dtype),
                    pltpu.VMEM((rows, both), jnp.float32),
                    pltpu.VMEM((rows, both), self.dtype),
                ],
            ),
            out_shape=[jax.ShapeDtypeStruct((self.dev_rows, n * self.wide), self.dtype)]
            * self.pair,
            compiler_params=pltpu.CompilerParams(vmem_limit_bytes=VMEM_LIMIT),
            cost_estimate=self.cost(n, width, 4 * math.prod(before.shape)),
            name="attend_vertical",
        )(self.info, self.vert, self.slash, *self.qs, *windows, before, kv_vert, self.masks)


def body(queries, keys, values, vertical_blocks, slash_offsets, out_weight):
    tokens_dev = queries.shape[0]
    kv_heads = keys.shape[1] // HD
    local = tokens_dev // BLK
    size = lax.axis_size("ctx")
    pair = 2 if kv_heads % 2 == 0 and size % 2 == 0 and lax.axis_size("head") == 1 else 1
    chips = size // pair
    heads = kv_heads // pair
    plane = PLANE if chips % PLANE == 0 and heads * vertical_blocks.shape[1] % PLANE == 0 else 1
    chip_blocks = pair * local
    reach = -(-MAXOFF // chip_blocks)
    index = lax.axis_index("ctx")
    chip, core = index // pair, index % pair
    info = jnp.stack([chip, core]).astype(jnp.int32)
    pos = jnp.arange(BLK)
    causal = jnp.where(pos[:, None] < pos[None, :], MASKED, 0.0)
    masks = jnp.stack([jnp.zeros_like(causal), causal, jnp.full_like(causal, MASKED)])
    masks = masks.astype(queries.dtype)

    def part(value, axis, which):
        span = value.shape[axis] // pair
        return lax.dynamic_slice_in_dim(value, which * span, span, axis)

    vert, slash = part(vertical_blocks, 0, core), part(slash_offsets, 0, core)
    kv_other = None
    if pair == 2:
        kv_other = crossed(jnp.concatenate([part(a, 1, 1 - core) for a in (keys, values)], 1), 1)
    per_chunk = 2 if heads % 2 == 0 else 1
    own, listed = prepare(info, vert, keys, values, kv_other, heads, local, plane, per_chunk)

    total = listed[0]
    for k in range(1, plane):
        total = total + crossed(listed[k], k * pair)
    two_back = [None] * len(own)
    passes_on = pair == 2 and reach == 2 and plane == 4
    if passes_on:
        upper = chip % plane >= 2
        stride = plane * pair
        pairs = [(i, i + stride) for i in range(size - stride) if i // pair % plane >= 2]
        before, risen = total, None
        first_step = total + shifted(total, stride)
        for c, w in enumerate(own):
            risen = lax.ppermute(w if risen is None else after(w, risen), "ctx", pairs)
            two_back[c] = crossed(after(jnp.where(upper, risen, w), before), 2 * pair)
            before = (two_back[c], first_step)
    q_other = crossed(part(queries, 1, 1 - core), 1) if pair == 2 else None
    step = 1
    while step < chips // plane:
        total = total + shifted(total, step * plane * pair)
        step *= 2

    attention = Attention(queries, q_other, info, vert, slash, masks, heads, local, plane)
    chunks = heads // per_chunk
    all_windows, sums = [], []
    for c in range(chunks):
        windows = [own[c]]
        if passes_on:
            passed = jnp.where(chip % 2 == 0, own[c], two_back[c])
            windows += [crossed(passed, pair), two_back[c]]
        else:
            windows += [shifted(own[c], pair * d) for d in range(1, reach + 1)]
        all_windows.append(windows)
        sums.append(attention.over_slash(c * per_chunk, per_chunk, windows))
    gathered = [total] + [crossed(total, k * pair) for k in range(1, plane)]
    gathered, sums = lax.optimization_barrier((gathered, sums))
    kv_vert = jnp.concatenate(gathered, 0)
    near, far = [], []
    for c in range(chunks):
        att = attention.over_vertical(c * per_chunk, per_chunk, all_windows[c], sums[c], kv_vert)
        near.append(att[0])
        if pair == 2:
            far.append(crossed(att[1], 1))
    attended = near
    if pair == 2:
        attended = [jnp.where(core == 0, a, b) for a, b in zip(near, far)]
        attended += [jnp.where(core == 0, b, a) for a, b in zip(near, far)]
    attended = lax.all_gather(jnp.concatenate(attended, 1), "head", axis=1, tiled=True)
    output = jnp.dot(attended, out_weight, preferred_element_type=jnp.float32)
    return output.astype(jnp.bfloat16)


def solution(mesh):
    placed = (
        P("ctx", "head"),
        P("ctx", "head"),
        P("ctx", "head"),
        P("head", None),
        P("head", None),
        P(None, "head"),
    )
    return jax.shard_map(
        body, mesh=mesh, in_specs=placed, out_specs=P("ctx", "head"), check_vma=False
    )
```

```python
import functools
import math

import jax
import jax.numpy as jnp
from jax import lax
from jax.experimental import pallas as pl
from jax.experimental.pallas import tpu as pltpu
from jax.sharding import PartitionSpec as P

HD = 128
BLK = 128
MAXOFF = 16
PLANE = 4
MASKED = -1e30
SMALLEST, LARGEST = 2.0**-60, 2.0**100
VMEM_LIMIT = 56 * 1024 * 1024


def shifted(value, by):
    size = lax.axis_size("ctx")
    return lax.ppermute(value, "ctx", [(i, i + by) for i in range(size - by)])


def crossed(value, bits):
    size = lax.axis_size("ctx")
    return lax.ppermute(value, "ctx", [(i, i ^ bits) for i in range(size)])


def after(value, other):
    return lax.optimization_barrier((value, other))[0]


def prepare_kernel(cfg, info, vert, *refs):
    pair, local, heads, plane, per_chunk = cfg
    chip, core = info[0], info[1]
    keys, values = refs[:2]
    refs = refs[2:]
    other = None
    if pair > 1:
        other, refs = refs[0], refs[1:]
    n_chunks = heads // per_chunk
    chip_outs, refs = refs[:n_chunks], refs[n_chunks:]
    list_outs, chip_kv = refs[:plane], refs[plane]
    n_vert = vert.shape[1]
    dev_rows = local * BLK
    chip_blocks = pair * local
    for e in range(heads):
        at = pl.multiple_of((core * heads + e) * HD, HD)
        chip_kv[e, :dev_rows, HD:] = values[:, pl.ds(at, HD)]
        if pair > 1:
            chip_kv[e, dev_rows:, HD:] = other[:, (heads + e) * HD : (heads + e + 1) * HD]
        for b in range(pair * local):
            rows = slice(b % local * BLK, (b % local + 1) * BLK)
            block = keys[rows, pl.ds(at, HD)] if b < local else other[rows, e * HD : (e + 1) * HD]
            chip_kv[e, b * BLK : (b + 1) * BLK, :HD] = block.T
        c, at = divmod(e, per_chunk)
        chip_outs[c][:, at * 2 * HD : (at + 1) * 2 * HD] = chip_kv[e]
    per = heads * n_vert // plane
    for k in range(plane):
        for i in range(per):
            flat = (chip % plane ^ k) * per + i
            e, j = flat // n_vert, flat % n_vert
            block = vert[e, j]
            within = block % chip_blocks
            if pair > 1:
                within = (within // local ^ core) * local + within % local
            rows = slice(i * BLK, (i + 1) * BLK)
            owned = block // chip_blocks == chip
            found = chip_kv[e, pl.ds(pl.multiple_of(within * BLK, BLK), BLK), :]
            list_outs[k][rows, :] = jnp.where(owned, found, jnp.zeros_like(found))


def prepare(info, vert, keys, values, other, heads, local, plane, per_chunk):
    pair = 1 if other is None else 2
    chip_rows = pair * local * BLK
    n_chunks = heads // per_chunk
    per = heads * vert.shape[1] // plane
    dtype = keys.dtype
    smem = pl.BlockSpec(memory_space=pltpu.SMEM)
    vmem = pl.BlockSpec(memory_space=pltpu.VMEM)
    data = [keys, values] + ([] if other is None else [other])
    specs = [vmem] * 2
    if other is not None:
        specs.append(pl.BlockSpec((other.shape[0], heads * 2 * HD), lambda i: (0, 0)))
    outs = pl.pallas_call(
        functools.partial(prepare_kernel, (pair, local, heads, plane, per_chunk)),
        grid=(1,),
        in_specs=[smem] * 2 + specs,
        out_specs=[vmem] * (n_chunks + plane),
        out_shape=[jax.ShapeDtypeStruct((chip_rows, per_chunk * 2 * HD), dtype)] * n_chunks
        + [jax.ShapeDtypeStruct((per * BLK, 2 * HD), dtype)] * plane,
        scratch_shapes=[pltpu.VMEM((heads, chip_rows, 2 * HD), dtype)],
        compiler_params=pltpu.CompilerParams(vmem_limit_bytes=VMEM_LIMIT),
        cost_estimate=pl.CostEstimate(
            flops=0, bytes_accessed=8 * heads * chip_rows * 2 * HD, transcendentals=0
        ),
        name="prepare",
    )(info, vert, *data)
    return list(outs[:n_chunks]), list(outs[n_chunks:])


def onehot_rows(shape, at, dtype):
    row = lax.broadcasted_iota(jnp.int32, shape, 0)
    col = lax.broadcasted_iota(jnp.int32, shape, 1)
    return jnp.where(col == at(row), 1.0, 0.0).astype(dtype)


def exponentials(q, k, factor):
    return jnp.exp2(jnp.dot(q, k, preferred_element_type=jnp.float32) * factor)


def pipelined(blocks, stage):
    stage(0, 0, blocks > 1, False)

    def two_blocks(n, carry):
        stage(2 * n + 1, 1, True, True)
        stage(2 * n + 2, 0, True, True)
        return carry

    inner = max(blocks - 2, 0) // 2
    lax.fori_loop(0, inner, two_blocks, 0)
    for i in range(2 * inner + 1, blocks):
        stage(i, i % 2, i + 1 < blocks, True)
    stage(blocks, blocks % 2, False, True)


def slash_kernel(cfg, info, slash, *refs):
    first, pair, local, group, reach, n_slash = cfg
    q_refs, refs = refs[:pair], refs[pair:]
    w_refs, refs = refs[: reach + 1], refs[reach + 1 :]
    masks, acc, win, qx = refs[:4]
    kgs, vgs, ps = refs[4:6], refs[6:8], refs[8:10]
    e = first + pl.program_id(0)
    chip, core = info[0], info[1]
    dev_rows = local * BLK
    chip_blocks = pair * local
    chip_rows = chip_blocks * BLK
    width = n_slash * BLK
    factor = math.log2(math.e) / math.sqrt(HD)

    for back in range(reach + 1):
        for slot in range(pair):
            owner = core ^ slot if pair > 1 else 0
            at = pl.multiple_of((reach - back) * chip_rows + owner * dev_rows, dev_rows)
            rows = slice(slot * dev_rows, (slot + 1) * dev_rows)
            win[pl.ds(at, dev_rows), :] = w_refs[back][rows, :]
    for vg in vgs:
        vg[:, HD:] = jnp.ones((width, HD), vg.dtype)
    eye = onehot_rows((BLK, HD), lambda row: row, qx.dtype)
    for i in range(chip_blocks):
        slot, b = divmod(i, local)
        for g in range(group):
            rows = slice(g * BLK, (g + 1) * BLK)
            qx[i, rows, :HD] = q_refs[slot][b * BLK : (b + 1) * BLK, g * HD : (g + 1) * HD]
            qx[i, rows, HD:] = eye

    def within(i):
        return (core ^ i // local) * local + i % local if pair > 1 else i

    def take(i, j):
        src = (reach * chip_blocks + within(i) - slash[e, j]) * BLK
        return pl.ds(pl.multiple_of(src, BLK), BLK)

    def place_keys(i, at):
        here = chip * chip_blocks + within(i)
        for j in range(n_slash):
            off = slash[e, j]
            cols = slice(j * BLK, (j + 1) * BLK)
            kgs[at][:HD, cols] = win[take(i, j), :HD]
            kgs[at][HD:, cols] = masks[jnp.where(off > here, 2, jnp.where(off == 0, 1, 0))]

    def stage(i, at, ahead, behind):
        if ahead:
            place_keys(i + 1, 1 - at)
        if behind:
            acc[i - 1] = jnp.dot(
                ps[1 - at][...], vgs[1 - at][...], preferred_element_type=jnp.float32
            )
        if isinstance(i, int) and i == chip_blocks:
            return
        for j in range(n_slash):
            vgs[at][j * BLK : (j + 1) * BLK, :HD] = win[take(i, j), HD:]
        ps[at][...] = exponentials(qx[i], kgs[at][...], factor).astype(ps[at].dtype)

    place_keys(0, 0)
    pipelined(chip_blocks, stage)


def vertical_kernel(cfg, info, vert, slash, *refs):
    first, pair, local, group, reach, n_slash, n_vert, plane, heads = cfg
    q_refs, refs = refs[:pair], refs[pair:]
    w_refs, refs = refs[: reach + 1], refs[reach + 1 :]
    before, kv_vert, masks, refs = refs[0], refs[1], refs[2], refs[3:]
    out_refs, refs = refs[:pair], refs[pair:]
    ke, ve, qx, res, good, acc = refs[:6]
    ps, (kg, vg, sc, pg) = refs[6:8], refs[8:]
    e = first + pl.program_id(0)
    chip, core = info[0], info[1]
    dev_rows = local * BLK
    chip_blocks = pair * local
    wide = n_vert * BLK
    step = min(2 * BLK, wide)
    factor = math.log2(math.e) / math.sqrt(HD)

    def within(i):
        return (core ^ i // local) * local + i % local if pair > 1 else i

    def hidden(i, j):
        here = chip * chip_blocks + within(i)
        found = vert[e, j] >= here
        for u in range(n_slash):
            found = found | (vert[e, j] == here - slash[e, u])
        return found

    per = heads * n_vert // plane
    row = lax.broadcasted_iota(jnp.int32, (HD, BLK), 0)
    for j in range(n_vert):
        flat = e * n_vert + j
        src = pl.multiple_of(((flat // per ^ chip % plane) * per + flat % per) * BLK, BLK)
        rows = slice(j * BLK, (j + 1) * BLK)
        ke[:HD, rows] = kv_vert[pl.ds(src, BLK), :HD]
        ve[rows, :HD] = kv_vert[pl.ds(src, BLK), HD:]
        bias = jnp.zeros((HD, BLK), jnp.float32)
        for i in range(chip_blocks):
            bias = jnp.where((row == i) & hidden(i, j), MASKED, bias)
        ke[HD:, rows] = bias.astype(ke.dtype)
    ve[:, HD:] = jnp.ones((wide, HD), ve.dtype)
    block_rows = group * BLK
    for i in range(chip_blocks):
        slot, b = divmod(i, local)
        mark = onehot_rows((BLK, HD), lambda row, i=i: i, qx.dtype)
        for g in range(group):
            rows = slice(i * block_rows + g * BLK, i * block_rows + (g + 1) * BLK)
            qx[rows, :HD] = q_refs[slot][b * BLK : (b + 1) * BLK, g * HD : (g + 1) * HD]
            qx[rows, HD:] = mark

    def stage(t, at, ahead, behind):
        last = isinstance(t, int) and t == tiles
        if behind:
            rows = slice((t - 1) * step, t * step)
            if not isinstance(t, int):
                rows = pl.ds(pl.multiple_of((t - 1) * step, step), step)
            part = jnp.dot(ps[1 - at][...], ve[rows, :], preferred_element_type=jnp.float32)
            acc[...] = acc[...] + part
        else:
            for i in range(chip_blocks):
                acc[i * block_rows : (i + 1) * block_rows, :] = before[i]
        if last:
            return
        cols = slice(t * step, (t + 1) * step)
        if not isinstance(t, int):
            cols = pl.ds(pl.multiple_of(t * step, step), step)
        ps[at][...] = exponentials(qx[...], ke[:, cols], factor).astype(ps[at].dtype)

    tiles = wide // step
    pipelined(tiles, stage)
    good[...] = jnp.ones(good.shape, good.dtype)
    for i in range(chip_blocks):
        rows = slice(i * block_rows, (i + 1) * block_rows)
        total = acc[rows, HD:]
        res[i] = (acc[rows, :HD] / total).astype(res.dtype)
        fine = jnp.where((total > SMALLEST) & (total < LARGEST), 1.0, 0.0)
        good[...] = jnp.minimum(good[...], jnp.min(fine, axis=0, keepdims=True))

    @pl.when(jnp.logical_not(jnp.min(good[...]) > 0.5))
    def _():
        vg[: n_slash * BLK, HD:] = jnp.ones((n_slash * BLK, HD), vg.dtype)
        kg[:, n_slash * BLK :] = ke[...]
        vg[n_slash * BLK :, :] = ve[...]
        eye = onehot_rows((BLK, HD), lambda row: row, qx.dtype)

        def shifted_block(i, carry):
            here = chip * chip_blocks + within(i)
            q_rows = pl.ds(pl.multiple_of(i * block_rows, block_rows), block_rows)
            for g in range(group):
                at = pl.ds(pl.multiple_of(i * block_rows + g * BLK, BLK), BLK)
                qx[at, HD:] = eye
            for j in range(n_slash):
                off = slash[e, j]
                pos = reach * chip_blocks + within(i) - off
                back = reach - pos // chip_blocks
                src = pos % chip_blocks
                if pair > 1:
                    src = (src // local ^ core) * local + src % local
                at = pl.ds(pl.multiple_of(src * BLK, BLK), BLK)
                found = w_refs[0][at, :]
                for d in range(1, reach + 1):
                    found = jnp.where(back == d, w_refs[d][at, :], found)
                rows = slice(j * BLK, (j + 1) * BLK)
                kg[:HD, rows] = found[:, :HD]
                vg[rows, :HD] = found[:, HD:]
                kg[HD:, rows] = masks[jnp.where(off > here, 2, jnp.where(off == 0, 1, 0))]
            for j in range(n_vert):
                rows = slice((n_slash + j) * BLK, (n_slash + j + 1) * BLK)
                kg[HD:, rows] = masks[jnp.where(hidden(i, j), 2, 0)]
            top = None
            for t in range(0, kg.shape[1], step):
                s = jnp.dot(qx[q_rows, :], kg[:, t : t + step], preferred_element_type=jnp.float32)
                sc[:, t : t + step] = s
                for u in range(0, step, HD):
                    piece = s[:, u : u + HD]
                    top = piece if top is None else jnp.maximum(top, piece)
            top = jnp.max(top, axis=1, keepdims=True)
            for t in range(0, kg.shape[1], step):
                p = jnp.exp2((sc[:, t : t + step] - top) * factor)
                pg[:, t : t + step] = p.astype(pg.dtype)
            sums = jnp.dot(pg[...], vg[...], preferred_element_type=jnp.float32)
            res[i] = (sums[:, :HD] / sums[:, HD:]).astype(res.dtype)
            return carry

        lax.fori_loop(0, chip_blocks, shifted_block, 0)

    for i in range(chip_blocks):
        slot, b = divmod(i, local)
        for g in range(group):
            out_refs[slot][b * BLK : (b + 1) * BLK, g * HD : (g + 1) * HD] = res[
                i, g * BLK : (g + 1) * BLK
            ]


class Attention:
    def __init__(self, queries, q_other, info, vert, slash, masks, heads, local, plane):
        self.pair = 1 if q_other is None else 2
        self.qs = [queries] if q_other is None else [queries, q_other]
        self.info, self.vert, self.slash, self.masks = info, vert, slash, masks
        self.heads, self.local, self.plane = heads, local, plane
        self.dev_rows = queries.shape[0]
        self.wide = queries.shape[1] // (self.pair * heads)
        self.group = self.wide // HD
        self.blocks = self.pair * local
        self.dtype = queries.dtype

    def specs(self, first, windows):
        heads, shape = self.heads, (self.dev_rows, self.wide)
        specs = [pl.BlockSpec(shape, lambda i, info, *_: (0, info[1] * heads + first + i))]
        if self.pair > 1:
            at = self.qs[1].shape[1] // self.wide - heads + first
            specs.append(pl.BlockSpec(shape, lambda i, *_: (0, at + i)))
        return specs + [pl.BlockSpec((w.shape[0], 2 * HD), lambda i, *_: (0, i)) for w in windows]

    def whole(self, a):
        return pl.BlockSpec(a.shape, lambda i, *_: (0,) * a.ndim)

    def cost(self, n, width, more):
        rows = n * self.blocks * self.group * BLK
        return pl.CostEstimate(
            flops=8 * rows * width * HD,
            bytes_accessed=rows * HD * 2 + more,
            transcendentals=rows * width,
        )

    def acc_spec(self):
        shape = (self.blocks, self.group * BLK, 2 * HD)
        return pl.BlockSpec((None, *shape), lambda i, *_: (i, 0, 0, 0))

    def over_slash(self, first, n, windows):
        n_slash = self.slash.shape[1]
        width, rows = n_slash * BLK, self.group * BLK
        shape = (n, self.blocks, rows, 2 * HD)
        cfg = (first, self.pair, self.local, self.group, len(windows) - 1, n_slash)
        return pl.pallas_call(
            functools.partial(slash_kernel, cfg),
            grid_spec=pltpu.PrefetchScalarGridSpec(
                num_scalar_prefetch=2,
                grid=(n,),
                in_specs=self.specs(first, windows) + [self.whole(self.masks)],
                out_specs=self.acc_spec(),
                scratch_shapes=[
                    pltpu.VMEM((sum(w.shape[0] for w in windows), 2 * HD), self.dtype),
                    pltpu.VMEM((self.blocks, rows, 2 * HD), self.dtype),
                ]
                + [pltpu.VMEM((2 * HD, width), self.dtype)] * 2
                + [pltpu.VMEM((width, 2 * HD), self.dtype)] * 2
                + [pltpu.VMEM((rows, width), self.dtype)] * 2,
            ),
            out_shape=jax.ShapeDtypeStruct(shape, jnp.float32),
            compiler_params=pltpu.CompilerParams(vmem_limit_bytes=VMEM_LIMIT),
            cost_estimate=self.cost(n, width, 4 * math.prod(shape)),
            name="attend_slash",
        )(self.info, self.slash, *self.qs, *windows, self.masks)

    def over_vertical(self, first, n, windows, before, kv_vert):
        n_slash, n_vert = self.slash.shape[1], self.vert.shape[1]
        width, both, rows = n_vert * BLK, (n_slash + n_vert) * BLK, self.group * BLK
        cfg = (first, self.pair, self.local, self.group, len(windows) - 1, n_slash, n_vert)
        out = pl.BlockSpec((self.dev_rows, self.wide), lambda i, *_: (0, i))
        return pl.pallas_call(
            functools.partial(vertical_kernel, cfg + (self.plane, self.heads)),
            grid_spec=pltpu.PrefetchScalarGridSpec(
                num_scalar_prefetch=3,
                grid=(n,),
                in_specs=self.specs(first, windows)
                + [self.acc_spec(), self.whole(kv_vert), self.whole(self.masks)],
                out_specs=[out] * self.pair,
                scratch_shapes=[
                    pltpu.VMEM((2 * HD, width), self.dtype),
                    pltpu.VMEM((width, 2 * HD), self.dtype),
                    pltpu.VMEM((self.blocks * rows, 2 * HD), self.dtype),
                    pltpu.VMEM((self.blocks, rows, HD), self.dtype),
                    pltpu.VMEM((1, HD), jnp.float32),
                    pltpu.VMEM((self.blocks * rows, 2 * HD), jnp.float32),
                    pltpu.VMEM((self.blocks * rows, 2 * BLK), self.dtype),
                    pltpu.VMEM((self.blocks * rows, 2 * BLK), self.dtype),
                    pltpu.VMEM((2 * HD, both), self.dtype),
                    pltpu.VMEM((both, 2 * HD), self.dtype),
                    pltpu.VMEM((rows, both), jnp.float32),
                    pltpu.VMEM((rows, both), self.dtype),
                ],
            ),
            out_shape=[jax.ShapeDtypeStruct((self.dev_rows, n * self.wide), self.dtype)]
            * self.pair,
            compiler_params=pltpu.CompilerParams(vmem_limit_bytes=VMEM_LIMIT),
            cost_estimate=self.cost(n, width, 4 * math.prod(before.shape)),
            name="attend_vertical",
        )(self.info, self.vert, self.slash, *self.qs, *windows, before, kv_vert, self.masks)


def body(queries, keys, values, vertical_blocks, slash_offsets, out_weight):
    tokens_dev = queries.shape[0]
    kv_heads = keys.shape[1] // HD
    local = tokens_dev // BLK
    size = lax.axis_size("ctx")
    pair = 2 if kv_heads % 2 == 0 and size % 2 == 0 and lax.axis_size("head") == 1 else 1
    chips = size // pair
    heads = kv_heads // pair
    plane = PLANE if chips % PLANE == 0 and heads * vertical_blocks.shape[1] % PLANE == 0 else 1
    chip_blocks = pair * local
    reach = -(-MAXOFF // chip_blocks)
    index = lax.axis_index("ctx")
    chip, core = index // pair, index % pair
    info = jnp.stack([chip, core]).astype(jnp.int32)
    pos = jnp.arange(BLK)
    causal = jnp.where(pos[:, None] < pos[None, :], MASKED, 0.0)
    masks = jnp.stack([jnp.zeros_like(causal), causal, jnp.full_like(causal, MASKED)])
    masks = masks.astype(queries.dtype)

    def part(value, axis, which):
        span = value.shape[axis] // pair
        return lax.dynamic_slice_in_dim(value, which * span, span, axis)

    vert, slash = part(vertical_blocks, 0, core), part(slash_offsets, 0, core)
    kv_other = None
    if pair == 2:
        kv_other = crossed(jnp.concatenate([part(a, 1, 1 - core) for a in (keys, values)], 1), 1)
    per_chunk = 2 if heads % 2 == 0 else 1
    own, listed = prepare(info, vert, keys, values, kv_other, heads, local, plane, per_chunk)

    total = listed[0]
    for k in range(1, plane):
        total = total + crossed(listed[k], k * pair)
    two_back = [None] * len(own)
    passes_on = pair == 2 and reach == 2 and plane == 4
    if passes_on:
        upper = chip % plane >= 2
        stride = plane * pair

        def sent_on(value, half):
            pairs = [(i, i + stride) for i in range(size - stride) if i // pair % plane // 2 == half]
            return lax.ppermute(value, "ctx", pairs)

        risen = sent_on(own[0], 1)
        two_back[0] = crossed(after(jnp.where(upper, risen, own[0]), total), 2 * pair)
        met = (two_back[0], total + shifted(total, stride))
        for c in range(1, len(own)):
            met = crossed(after(own[c], met), 2 * pair)
            two_back[c] = jnp.where(upper, met, sent_on(met, 0))
    q_other = crossed(part(queries, 1, 1 - core), 1) if pair == 2 else None
    step = 1
    while step < chips // plane:
        total = total + shifted(total, step * plane * pair)
        step *= 2

    attention = Attention(queries, q_other, info, vert, slash, masks, heads, local, plane)
    chunks = heads // per_chunk
    all_windows, sums = [], []
    for c in range(chunks):
        windows = [own[c]]
        if passes_on:
            passed = jnp.where(chip % 2 == 0, own[c], two_back[c])
            one_back = crossed(passed, pair)
            if c == 0:
                one_back = after(one_back, met)
            windows += [one_back, two_back[c]]
        else:
            windows += [shifted(own[c], pair * d) for d in range(1, reach + 1)]
        all_windows.append(windows)
        sums.append(attention.over_slash(c * per_chunk, per_chunk, windows))
    gathered = [total] + [crossed(total, k * pair) for k in range(1, plane)]
    gathered = after(gathered, (sums[0], two_back[1:]))
    kv_vert = jnp.concatenate(gathered, 0)
    near, far = [], []
    for c in range(chunks):
        att = attention.over_vertical(c * per_chunk, per_chunk, all_windows[c], sums[c], kv_vert)
        near.append(att[0])
        if pair == 2:
            far.append(crossed(att[1], 1))
    attended = near
    if pair == 2:
        attended = [jnp.where(core == 0, a, b) for a, b in zip(near, far)]
        attended += [jnp.where(core == 0, b, a) for a, b in zip(near, far)]
    attended = lax.all_gather(jnp.concatenate(attended, 1), "head", axis=1, tiled=True)
    output = jnp.dot(attended, out_weight, preferred_element_type=jnp.float32)
    return output.astype(jnp.bfloat16)


def solution(mesh):
    placed = (
        P("ctx", "head"),
        P("ctx", "head"),
        P("ctx", "head"),
        P("head", None),
        P("head", None),
        P(None, "head"),
    )
    return jax.shard_map(
        body, mesh=mesh, in_specs=placed, out_specs=P("ctx", "head"), check_vma=False
    )
```

```python
import functools
import math

import jax
import jax.numpy as jnp
from jax import lax
from jax.experimental import pallas as pl
from jax.experimental.pallas import tpu as pltpu
from jax.sharding import PartitionSpec as P

HD = 128
BLK = 128
MAXOFF = 16
PLANE = 4
MASKED = -1e30
SMALLEST, LARGEST = 2.0**-60, 2.0**100
VMEM_LIMIT = 56 * 1024 * 1024


def shifted(value, by):
    size = lax.axis_size("ctx")
    return lax.ppermute(value, "ctx", [(i, i + by) for i in range(size - by)])


def crossed(value, bits):
    size = lax.axis_size("ctx")
    return lax.ppermute(value, "ctx", [(i, i ^ bits) for i in range(size)])


def after(value, other):
    return lax.optimization_barrier((value, other))[0]


def prepare_kernel(cfg, info, vert, *refs):
    pair, local, heads, plane, per_chunk = cfg
    chip, core = info[0], info[1]
    keys, values = refs[:2]
    refs = refs[2:]
    other = None
    if pair > 1:
        other, refs = refs[0], refs[1:]
    n_chunks = heads // per_chunk
    chip_outs, refs = refs[:n_chunks], refs[n_chunks:]
    list_outs, chip_kv = refs[:plane], refs[plane]
    n_vert = vert.shape[1]
    dev_rows = local * BLK
    chip_blocks = pair * local
    for e in range(heads):
        at = pl.multiple_of((core * heads + e) * HD, HD)
        chip_kv[e, :dev_rows, HD:] = values[:, pl.ds(at, HD)]
        if pair > 1:
            chip_kv[e, dev_rows:, HD:] = other[:, (heads + e) * HD : (heads + e + 1) * HD]
        for b in range(pair * local):
            rows = slice(b % local * BLK, (b % local + 1) * BLK)
            block = keys[rows, pl.ds(at, HD)] if b < local else other[rows, e * HD : (e + 1) * HD]
            chip_kv[e, b * BLK : (b + 1) * BLK, :HD] = block.T
        c, at = divmod(e, per_chunk)
        chip_outs[c][:, at * 2 * HD : (at + 1) * 2 * HD] = chip_kv[e]
    per = heads * n_vert // plane
    for k in range(plane):
        for i in range(per):
            flat = (chip % plane ^ k) * per + i
            e, j = flat // n_vert, flat % n_vert
            block = vert[e, j]
            within = block % chip_blocks
            if pair > 1:
                within = (within // local ^ core) * local + within % local
            rows = slice(i * BLK, (i + 1) * BLK)
            owned = block // chip_blocks == chip
            found = chip_kv[e, pl.ds(pl.multiple_of(within * BLK, BLK), BLK), :]
            list_outs[k][rows, :] = jnp.where(owned, found, jnp.zeros_like(found))


def prepare(info, vert, keys, values, other, heads, local, plane, per_chunk):
    pair = 1 if other is None else 2
    chip_rows = pair * local * BLK
    n_chunks = heads // per_chunk
    per = heads * vert.shape[1] // plane
    dtype = keys.dtype
    smem = pl.BlockSpec(memory_space=pltpu.SMEM)
    vmem = pl.BlockSpec(memory_space=pltpu.VMEM)
    data = [keys, values] + ([] if other is None else [other])
    specs = [vmem] * 2
    if other is not None:
        specs.append(pl.BlockSpec((other.shape[0], heads * 2 * HD), lambda i: (0, 0)))
    outs = pl.pallas_call(
        functools.partial(prepare_kernel, (pair, local, heads, plane, per_chunk)),
        grid=(1,),
        in_specs=[smem] * 2 + specs,
        out_specs=[vmem] * (n_chunks + plane),
        out_shape=[jax.ShapeDtypeStruct((chip_rows, per_chunk * 2 * HD), dtype)] * n_chunks
        + [jax.ShapeDtypeStruct((per * BLK, 2 * HD), dtype)] * plane,
        scratch_shapes=[pltpu.VMEM((heads, chip_rows, 2 * HD), dtype)],
        compiler_params=pltpu.CompilerParams(vmem_limit_bytes=VMEM_LIMIT),
        cost_estimate=pl.CostEstimate(
            flops=0, bytes_accessed=8 * heads * chip_rows * 2 * HD, transcendentals=0
        ),
        name="prepare",
    )(info, vert, *data)
    return list(outs[:n_chunks]), list(outs[n_chunks:])


def onehot_rows(shape, at, dtype):
    row = lax.broadcasted_iota(jnp.int32, shape, 0)
    col = lax.broadcasted_iota(jnp.int32, shape, 1)
    return jnp.where(col == at(row), 1.0, 0.0).astype(dtype)


def exponentials(q, k, factor):
    return jnp.exp2(jnp.dot(q, k, preferred_element_type=jnp.float32) * factor)


def pipelined(blocks, stage):
    stage(0, 0, blocks > 1, False)

    def two_blocks(n, carry):
        stage(2 * n + 1, 1, True, True)
        stage(2 * n + 2, 0, True, True)
        return carry

    inner = max(blocks - 2, 0) // 2
    lax.fori_loop(0, inner, two_blocks, 0)
    for i in range(2 * inner + 1, blocks):
        stage(i, i % 2, i + 1 < blocks, True)
    stage(blocks, blocks % 2, False, True)


def slash_kernel(cfg, info, slash, *refs):
    first, pair, local, group, reach, n_slash = cfg
    q_refs, refs = refs[:pair], refs[pair:]
    w_refs, refs = refs[: reach + 1], refs[reach + 1 :]
    masks, acc, win, qx = refs[:4]
    kgs, vgs, ps = refs[4:6], refs[6:8], refs[8:10]
    e = first + pl.program_id(0)
    chip, core = info[0], info[1]
    dev_rows = local * BLK
    chip_blocks = pair * local
    chip_rows = chip_blocks * BLK
    width = n_slash * BLK
    factor = math.log2(math.e) / math.sqrt(HD)

    for back in range(reach + 1):
        for slot in range(pair):
            owner = core ^ slot if pair > 1 else 0
            at = pl.multiple_of((reach - back) * chip_rows + owner * dev_rows, dev_rows)
            rows = slice(slot * dev_rows, (slot + 1) * dev_rows)
            win[pl.ds(at, dev_rows), :] = w_refs[back][rows, :]
    for vg in vgs:
        vg[:, HD:] = jnp.ones((width, HD), vg.dtype)
    eye = onehot_rows((BLK, HD), lambda row: row, qx.dtype)
    for i in range(chip_blocks):
        slot, b = divmod(i, local)
        for g in range(group):
            rows = slice(g * BLK, (g + 1) * BLK)
            qx[i, rows, :HD] = q_refs[slot][b * BLK : (b + 1) * BLK, g * HD : (g + 1) * HD]
            qx[i, rows, HD:] = eye

    def within(i):
        return (core ^ i // local) * local + i % local if pair > 1 else i

    def take(i, j):
        src = (reach * chip_blocks + within(i) - slash[e, j]) * BLK
        return pl.ds(pl.multiple_of(src, BLK), BLK)

    def place_keys(i, at):
        here = chip * chip_blocks + within(i)
        for j in range(n_slash):
            off = slash[e, j]
            cols = slice(j * BLK, (j + 1) * BLK)
            kgs[at][:HD, cols] = win[take(i, j), :HD]
            kgs[at][HD:, cols] = masks[jnp.where(off > here, 2, jnp.where(off == 0, 1, 0))]

    def stage(i, at, ahead, behind):
        if ahead:
            place_keys(i + 1, 1 - at)
        if behind:
            acc[i - 1] = jnp.dot(
                ps[1 - at][...], vgs[1 - at][...], preferred_element_type=jnp.float32
            )
        if isinstance(i, int) and i == chip_blocks:
            return
        for j in range(n_slash):
            vgs[at][j * BLK : (j + 1) * BLK, :HD] = win[take(i, j), HD:]
        ps[at][...] = exponentials(qx[i], kgs[at][...], factor).astype(ps[at].dtype)

    place_keys(0, 0)
    pipelined(chip_blocks, stage)


def vertical_kernel(cfg, info, vert, slash, *refs):
    first, pair, local, group, reach, n_slash, n_vert, plane, heads = cfg
    q_refs, refs = refs[:pair], refs[pair:]
    w_refs, refs = refs[: reach + 1], refs[reach + 1 :]
    before, kv_vert, masks, refs = refs[0], refs[1], refs[2], refs[3:]
    out_refs, refs = refs[:pair], refs[pair:]
    ke, ve, qx, res, good = refs[:5]
    ps, (kg, vg, sc, pg) = refs[5:7], refs[7:]
    e = first + pl.program_id(0)
    chip, core = info[0], info[1]
    dev_rows = local * BLK
    chip_blocks = pair * local
    wide = n_vert * BLK
    step = min(2 * BLK, wide)
    factor = math.log2(math.e) / math.sqrt(HD)

    def within(i):
        return (core ^ i // local) * local + i % local if pair > 1 else i

    def hidden(i, j):
        here = chip * chip_blocks + within(i)
        found = vert[e, j] >= here
        for u in range(n_slash):
            found = found | (vert[e, j] == here - slash[e, u])
        return found

    per = heads * n_vert // plane
    row = lax.broadcasted_iota(jnp.int32, (HD, BLK), 0)
    for j in range(n_vert):
        flat = e * n_vert + j
        src = pl.multiple_of(((flat // per ^ chip % plane) * per + flat % per) * BLK, BLK)
        rows = slice(j * BLK, (j + 1) * BLK)
        ke[:HD, rows] = kv_vert[pl.ds(src, BLK), :HD]
        ve[rows, :HD] = kv_vert[pl.ds(src, BLK), HD:]
        bias = jnp.zeros((HD, BLK), jnp.float32)
        for i in range(chip_blocks):
            bias = jnp.where((row == i) & hidden(i, j), MASKED, bias)
        ke[HD:, rows] = bias.astype(ke.dtype)
    ve[:, HD:] = jnp.ones((wide, HD), ve.dtype)
    block_rows = group * BLK
    for i in range(chip_blocks):
        slot, b = divmod(i, local)
        mark = onehot_rows((BLK, HD), lambda row, i=i: i, qx.dtype)
        for g in range(group):
            rows = slice(i * block_rows + g * BLK, i * block_rows + (g + 1) * BLK)
            qx[rows, :HD] = q_refs[slot][b * BLK : (b + 1) * BLK, g * HD : (g + 1) * HD]
            qx[rows, HD:] = mark

    n_rows = ps[0].shape[0]

    def stage(t, at, behind):
        if behind:
            part = jnp.dot(ps[1 - at][...], ve[...], preferred_element_type=jnp.float32)
            for u in range(n_rows // block_rows):
                i = (t - 1) * (n_rows // block_rows) + u
                finish(i, before[i] + part[u * block_rows : (u + 1) * block_rows, :])
        if t * n_rows == qx.shape[0]:
            return
        q = qx[t * n_rows : (t + 1) * n_rows, :]
        ps[at][...] = exponentials(q, ke[...], factor).astype(ps[at].dtype)

    def finish(i, acc):
        total = acc[:, HD:]
        res[i] = (acc[:, :HD] / total).astype(res.dtype)
        fine = jnp.where((total > SMALLEST) & (total < LARGEST), 1.0, 0.0)
        good[...] = jnp.minimum(good[...], jnp.min(fine, axis=0, keepdims=True))

    good[...] = jnp.ones(good.shape, good.dtype)
    for t in range(qx.shape[0] // n_rows + 1):
        stage(t, t % 2, t > 0)

    @pl.when(jnp.logical_not(jnp.min(good[...]) > 0.5))
    def _():
        vg[: n_slash * BLK, HD:] = jnp.ones((n_slash * BLK, HD), vg.dtype)
        kg[:, n_slash * BLK :] = ke[...]
        vg[n_slash * BLK :, :] = ve[...]
        eye = onehot_rows((BLK, HD), lambda row: row, qx.dtype)

        def shifted_block(i, carry):
            here = chip * chip_blocks + within(i)
            q_rows = pl.ds(pl.multiple_of(i * block_rows, block_rows), block_rows)
            for g in range(group):
                at = pl.ds(pl.multiple_of(i * block_rows + g * BLK, BLK), BLK)
                qx[at, HD:] = eye
            for j in range(n_slash):
                off = slash[e, j]
                pos = reach * chip_blocks + within(i) - off
                back = reach - pos // chip_blocks
                src = pos % chip_blocks
                if pair > 1:
                    src = (src // local ^ core) * local + src % local
                at = pl.ds(pl.multiple_of(src * BLK, BLK), BLK)
                found = w_refs[0][at, :]
                for d in range(1, reach + 1):
                    found = jnp.where(back == d, w_refs[d][at, :], found)
                rows = slice(j * BLK, (j + 1) * BLK)
                kg[:HD, rows] = found[:, :HD]
                vg[rows, :HD] = found[:, HD:]
                kg[HD:, rows] = masks[jnp.where(off > here, 2, jnp.where(off == 0, 1, 0))]
            for j in range(n_vert):
                rows = slice((n_slash + j) * BLK, (n_slash + j + 1) * BLK)
                kg[HD:, rows] = masks[jnp.where(hidden(i, j), 2, 0)]
            top = None
            for t in range(0, kg.shape[1], step):
                s = jnp.dot(qx[q_rows, :], kg[:, t : t + step], preferred_element_type=jnp.float32)
                sc[:, t : t + step] = s
                for u in range(0, step, HD):
                    piece = s[:, u : u + HD]
                    top = piece if top is None else jnp.maximum(top, piece)
            top = jnp.max(top, axis=1, keepdims=True)
            for t in range(0, kg.shape[1], step):
                p = jnp.exp2((sc[:, t : t + step] - top) * factor)
                pg[:, t : t + step] = p.astype(pg.dtype)
            sums = jnp.dot(pg[...], vg[...], preferred_element_type=jnp.float32)
            res[i] = (sums[:, :HD] / sums[:, HD:]).astype(res.dtype)
            return carry

        lax.fori_loop(0, chip_blocks, shifted_block, 0)

    for i in range(chip_blocks):
        slot, b = divmod(i, local)
        for g in range(group):
            out_refs[slot][b * BLK : (b + 1) * BLK, g * HD : (g + 1) * HD] = res[
                i, g * BLK : (g + 1) * BLK
            ]


class Attention:
    def __init__(self, queries, q_other, info, vert, slash, masks, heads, local, plane):
        self.pair = 1 if q_other is None else 2
        self.qs = [queries] if q_other is None else [queries, q_other]
        self.info, self.vert, self.slash, self.masks = info, vert, slash, masks
        self.heads, self.local, self.plane = heads, local, plane
        self.dev_rows = queries.shape[0]
        self.wide = queries.shape[1] // (self.pair * heads)
        self.group = self.wide // HD
        self.blocks = self.pair * local
        self.dtype = queries.dtype

    def specs(self, first, windows):
        heads, shape = self.heads, (self.dev_rows, self.wide)
        specs = [pl.BlockSpec(shape, lambda i, info, *_: (0, info[1] * heads + first + i))]
        if self.pair > 1:
            at = self.qs[1].shape[1] // self.wide - heads + first
            specs.append(pl.BlockSpec(shape, lambda i, *_: (0, at + i)))
        return specs + [pl.BlockSpec((w.shape[0], 2 * HD), lambda i, *_: (0, i)) for w in windows]

    def whole(self, a):
        return pl.BlockSpec(a.shape, lambda i, *_: (0,) * a.ndim)

    def cost(self, n, width, more):
        rows = n * self.blocks * self.group * BLK
        return pl.CostEstimate(
            flops=8 * rows * width * HD,
            bytes_accessed=rows * HD * 2 + more,
            transcendentals=rows * width,
        )

    def acc_spec(self):
        shape = (self.blocks, self.group * BLK, 2 * HD)
        return pl.BlockSpec((None, *shape), lambda i, *_: (i, 0, 0, 0))

    def over_slash(self, first, n, windows):
        n_slash = self.slash.shape[1]
        width, rows = n_slash * BLK, self.group * BLK
        shape = (n, self.blocks, rows, 2 * HD)
        cfg = (first, self.pair, self.local, self.group, len(windows) - 1, n_slash)
        return pl.pallas_call(
            functools.partial(slash_kernel, cfg),
            grid_spec=pltpu.PrefetchScalarGridSpec(
                num_scalar_prefetch=2,
                grid=(n,),
                in_specs=self.specs(first, windows) + [self.whole(self.masks)],
                out_specs=self.acc_spec(),
                scratch_shapes=[
                    pltpu.VMEM((sum(w.shape[0] for w in windows), 2 * HD), self.dtype),
                    pltpu.VMEM((self.blocks, rows, 2 * HD), self.dtype),
                ]
                + [pltpu.VMEM((2 * HD, width), self.dtype)] * 2
                + [pltpu.VMEM((width, 2 * HD), self.dtype)] * 2
                + [pltpu.VMEM((rows, width), self.dtype)] * 2,
            ),
            out_shape=jax.ShapeDtypeStruct(shape, jnp.float32),
            compiler_params=pltpu.CompilerParams(vmem_limit_bytes=VMEM_LIMIT),
            cost_estimate=self.cost(n, width, 4 * math.prod(shape)),
            name="attend_slash",
        )(self.info, self.slash, *self.qs, *windows, self.masks)

    def over_vertical(self, first, n, windows, before, kv_vert):
        n_slash, n_vert = self.slash.shape[1], self.vert.shape[1]
        width, both, rows = n_vert * BLK, (n_slash + n_vert) * BLK, self.group * BLK
        cfg = (first, self.pair, self.local, self.group, len(windows) - 1, n_slash, n_vert)
        out = pl.BlockSpec((self.dev_rows, self.wide), lambda i, *_: (0, i))
        return pl.pallas_call(
            functools.partial(vertical_kernel, cfg + (self.plane, self.heads)),
            grid_spec=pltpu.PrefetchScalarGridSpec(
                num_scalar_prefetch=3,
                grid=(n,),
                in_specs=self.specs(first, windows)
                + [self.acc_spec(), self.whole(kv_vert), self.whole(self.masks)],
                out_specs=[out] * self.pair,
                scratch_shapes=[
                    pltpu.VMEM((2 * HD, width), self.dtype),
                    pltpu.VMEM((width, 2 * HD), self.dtype),
                    pltpu.VMEM((self.blocks * rows, 2 * HD), self.dtype),
                    pltpu.VMEM((self.blocks, rows, HD), self.dtype),
                    pltpu.VMEM((1, HD), jnp.float32),
                    pltpu.VMEM((self.blocks // 2 * rows, width), self.dtype),
                    pltpu.VMEM((self.blocks // 2 * rows, width), self.dtype),
                    pltpu.VMEM((2 * HD, both), self.dtype),
                    pltpu.VMEM((both, 2 * HD), self.dtype),
                    pltpu.VMEM((rows, both), jnp.float32),
                    pltpu.VMEM((rows, both), self.dtype),
                ],
            ),
            out_shape=[jax.ShapeDtypeStruct((self.dev_rows, n * self.wide), self.dtype)]
            * self.pair,
            compiler_params=pltpu.CompilerParams(vmem_limit_bytes=VMEM_LIMIT),
            cost_estimate=self.cost(n, width, 4 * math.prod(before.shape)),
            name="attend_vertical",
        )(self.info, self.vert, self.slash, *self.qs, *windows, before, kv_vert, self.masks)


def body(queries, keys, values, vertical_blocks, slash_offsets, out_weight):
    tokens_dev = queries.shape[0]
    kv_heads = keys.shape[1] // HD
    local = tokens_dev // BLK
    size = lax.axis_size("ctx")
    pair = 2 if kv_heads % 2 == 0 and size % 2 == 0 and lax.axis_size("head") == 1 else 1
    chips = size // pair
    heads = kv_heads // pair
    plane = PLANE if chips % PLANE == 0 and heads * vertical_blocks.shape[1] % PLANE == 0 else 1
    chip_blocks = pair * local
    reach = -(-MAXOFF // chip_blocks)
    index = lax.axis_index("ctx")
    chip, core = index // pair, index % pair
    info = jnp.stack([chip, core]).astype(jnp.int32)
    pos = jnp.arange(BLK)
    causal = jnp.where(pos[:, None] < pos[None, :], MASKED, 0.0)
    masks = jnp.stack([jnp.zeros_like(causal), causal, jnp.full_like(causal, MASKED)])
    masks = masks.astype(queries.dtype)

    def part(value, axis, which):
        span = value.shape[axis] // pair
        return lax.dynamic_slice_in_dim(value, which * span, span, axis)

    vert, slash = part(vertical_blocks, 0, core), part(slash_offsets, 0, core)
    kv_other = None
    if pair == 2:
        kv_other = crossed(jnp.concatenate([part(a, 1, 1 - core) for a in (keys, values)], 1), 1)
    per_chunk = 2 if heads % 2 == 0 else 1
    own, listed = prepare(info, vert, keys, values, kv_other, heads, local, plane, per_chunk)

    total = listed[0]
    for k in range(1, plane):
        total = total + crossed(listed[k], k * pair)
    q_other = None
    if pair == 2:
        q_other = crossed(after(part(queries, 1, 1 - core), own[0]), 1)
        total = after(total, q_other)
    two_back = [None] * len(own)
    passes_on = pair == 2 and reach == 2 and plane == 4
    if passes_on:
        upper = chip % plane >= 2
        stride = plane * pair

        def sent_on(value, half):
            pairs = [(i, i + stride) for i in range(size - stride) if i // pair % plane // 2 == half]
            return lax.ppermute(value, "ctx", pairs)

        risen = sent_on(own[0], 1)
        two_back[0] = crossed(after(jnp.where(upper, risen, own[0]), total), 2 * pair)
        met = (two_back[0], total + shifted(total, stride))
        for c in range(1, len(own)):
            met = crossed(after(own[c], met), 2 * pair)
            two_back[c] = jnp.where(upper, met, sent_on(met, 0))
    step = 1
    while step < chips // plane:
        total = total + shifted(total, step * plane * pair)
        step *= 2

    attention = Attention(queries, q_other, info, vert, slash, masks, heads, local, plane)
    chunks = heads // per_chunk
    all_windows, sums = [], []
    for c in range(chunks):
        windows = [own[c]]
        if passes_on:
            passed = jnp.where(chip % 2 == 0, own[c], two_back[c])
            one_back = crossed(passed, pair)
            if c == 0:
                one_back = after(one_back, met)
            windows += [one_back, two_back[c]]
        else:
            windows += [shifted(own[c], pair * d) for d in range(1, reach + 1)]
        all_windows.append(windows)
        sums.append(attention.over_slash(c * per_chunk, per_chunk, windows))
    gathered = [total] + [crossed(total, k * pair) for k in range(1, plane)]
    gathered = after(gathered, (sums[0], two_back[1:]))
    kv_vert = jnp.concatenate(gathered, 0)
    near, far = [], []
    for c in range(chunks):
        att = attention.over_vertical(c * per_chunk, per_chunk, all_windows[c], sums[c], kv_vert)
        near.append(att[0])
        if pair == 2:
            far.append(crossed(att[1], 1))
    attended = near
    if pair == 2:
        attended = [jnp.where(core == 0, a, b) for a, b in zip(near, far)]
        attended += [jnp.where(core == 0, b, a) for a, b in zip(near, far)]
    attended = lax.all_gather(jnp.concatenate(attended, 1), "head", axis=1, tiled=True)
    output = jnp.dot(attended, out_weight, preferred_element_type=jnp.float32)
    return output.astype(jnp.bfloat16)


def solution(mesh):
    placed = (
        P("ctx", "head"),
        P("ctx", "head"),
        P("ctx", "head"),
        P("head", None),
        P("head", None),
        P(None, "head"),
    )
    return jax.shard_map(
        body, mesh=mesh, in_specs=placed, out_specs=P("ctx", "head"), check_vma=False
    )
```

```python
import functools
import math

import jax
import jax.numpy as jnp
from jax import lax
from jax.experimental import pallas as pl
from jax.experimental.pallas import tpu as pltpu
from jax.sharding import PartitionSpec as P

HD = 128
BLK = 128
MAXOFF = 16
PLANE = 4
MASKED = -1e30
SMALLEST, LARGEST = 2.0**-60, 2.0**100
VMEM_LIMIT = 56 * 1024 * 1024


def shifted(value, by):
    size = lax.axis_size("ctx")
    return lax.ppermute(value, "ctx", [(i, i + by) for i in range(size - by)])


def crossed(value, bits):
    size = lax.axis_size("ctx")
    return lax.ppermute(value, "ctx", [(i, i ^ bits) for i in range(size)])


def after(value, other):
    return lax.optimization_barrier((value, other))[0]


def prepare_kernel(cfg, info, vert, *refs):
    pair, local, heads, plane, per_chunk = cfg
    chip, core = info[0], info[1]
    keys, values = refs[:2]
    refs = refs[2:]
    other = None
    if pair > 1:
        other, refs = refs[0], refs[1:]
    n_chunks = heads // per_chunk
    chip_outs, refs = refs[:n_chunks], refs[n_chunks:]
    list_outs, chip_kv = refs[:plane], refs[plane]
    n_vert = vert.shape[1]
    dev_rows = local * BLK
    chip_blocks = pair * local
    for e in range(heads):
        at = pl.multiple_of((core * heads + e) * HD, HD)
        chip_kv[e, :dev_rows, HD:] = values[:, pl.ds(at, HD)]
        if pair > 1:
            chip_kv[e, dev_rows:, HD:] = other[:, (heads + e) * HD : (heads + e + 1) * HD]
        for b in range(pair * local):
            rows = slice(b % local * BLK, (b % local + 1) * BLK)
            block = keys[rows, pl.ds(at, HD)] if b < local else other[rows, e * HD : (e + 1) * HD]
            chip_kv[e, b * BLK : (b + 1) * BLK, :HD] = block.T
        c, at = divmod(e, per_chunk)
        chip_outs[c][:, at * 2 * HD : (at + 1) * 2 * HD] = chip_kv[e]
    per = heads * n_vert // plane
    for k in range(plane):
        for i in range(per):
            flat = (chip % plane ^ k) * per + i
            e, j = flat // n_vert, flat % n_vert
            block = vert[e, j]
            within = block % chip_blocks
            if pair > 1:
                within = (within // local ^ core) * local + within % local
            rows = slice(i * BLK, (i + 1) * BLK)
            owned = block // chip_blocks == chip
            found = chip_kv[e, pl.ds(pl.multiple_of(within * BLK, BLK), BLK), :]
            list_outs[k][rows, :] = jnp.where(owned, found, jnp.zeros_like(found))


def prepare(info, vert, keys, values, other, heads, local, plane, per_chunk):
    pair = 1 if other is None else 2
    chip_rows = pair * local * BLK
    n_chunks = heads // per_chunk
    per = heads * vert.shape[1] // plane
    dtype = keys.dtype
    smem = pl.BlockSpec(memory_space=pltpu.SMEM)
    vmem = pl.BlockSpec(memory_space=pltpu.VMEM)
    data = [keys, values] + ([] if other is None else [other])
    specs = [vmem] * 2
    if other is not None:
        specs.append(pl.BlockSpec((other.shape[0], heads * 2 * HD), lambda i: (0, 0)))
    outs = pl.pallas_call(
        functools.partial(prepare_kernel, (pair, local, heads, plane, per_chunk)),
        grid=(1,),
        in_specs=[smem] * 2 + specs,
        out_specs=[vmem] * (n_chunks + plane),
        out_shape=[jax.ShapeDtypeStruct((chip_rows, per_chunk * 2 * HD), dtype)] * n_chunks
        + [jax.ShapeDtypeStruct((per * BLK, 2 * HD), dtype)] * plane,
        scratch_shapes=[pltpu.VMEM((heads, chip_rows, 2 * HD), dtype)],
        compiler_params=pltpu.CompilerParams(vmem_limit_bytes=VMEM_LIMIT),
        cost_estimate=pl.CostEstimate(
            flops=0, bytes_accessed=8 * heads * chip_rows * 2 * HD, transcendentals=0
        ),
        name="prepare",
    )(info, vert, *data)
    return list(outs[:n_chunks]), list(outs[n_chunks:])


def onehot_rows(shape, at, dtype):
    row = lax.broadcasted_iota(jnp.int32, shape, 0)
    col = lax.broadcasted_iota(jnp.int32, shape, 1)
    return jnp.where(col == at(row), 1.0, 0.0).astype(dtype)


def exponentials(q, k, factor):
    return jnp.exp2(jnp.dot(q, k, preferred_element_type=jnp.float32) * factor)


def pipelined(blocks, stage):
    stage(0, 0, blocks > 1, False)

    def two_blocks(n, carry):
        stage(2 * n + 1, 1, True, True)
        stage(2 * n + 2, 0, True, True)
        return carry

    inner = max(blocks - 2, 0) // 2
    lax.fori_loop(0, inner, two_blocks, 0)
    for i in range(2 * inner + 1, blocks):
        stage(i, i % 2, i + 1 < blocks, True)
    stage(blocks, blocks % 2, False, True)


def slash_kernel(cfg, info, slash, *refs):
    first, pair, local, group, reach, n_slash = cfg
    q_refs, refs = refs[:pair], refs[pair:]
    w_refs, refs = refs[: reach + 1], refs[reach + 1 :]
    masks, acc, win, qx = refs[:4]
    kgs, vgs, ps = refs[4:6], refs[6:8], refs[8:10]
    e = first + pl.program_id(0)
    chip, core = info[0], info[1]
    dev_rows = local * BLK
    chip_blocks = pair * local
    chip_rows = chip_blocks * BLK
    width = n_slash * BLK
    factor = math.log2(math.e) / math.sqrt(HD)

    for back in range(reach + 1):
        for slot in range(pair):
            owner = core ^ slot if pair > 1 else 0
            at = pl.multiple_of((reach - back) * chip_rows + owner * dev_rows, dev_rows)
            rows = slice(slot * dev_rows, (slot + 1) * dev_rows)
            win[pl.ds(at, dev_rows), :] = w_refs[back][rows, :]
    for vg in vgs:
        vg[:, HD:] = jnp.ones((width, HD), vg.dtype)
    eye = onehot_rows((BLK, HD), lambda row: row, qx.dtype)
    for i in range(chip_blocks):
        slot, b = divmod(i, local)
        for g in range(group):
            rows = slice(g * BLK, (g + 1) * BLK)
            qx[i, rows, :HD] = q_refs[slot][b * BLK : (b + 1) * BLK, g * HD : (g + 1) * HD]
            qx[i, rows, HD:] = eye

    def within(i):
        return (core ^ i // local) * local + i % local if pair > 1 else i

    def take(i, j):
        src = (reach * chip_blocks + within(i) - slash[e, j]) * BLK
        return pl.ds(pl.multiple_of(src, BLK), BLK)

    def place_keys(i, at):
        here = chip * chip_blocks + within(i)
        for j in range(n_slash):
            off = slash[e, j]
            cols = slice(j * BLK, (j + 1) * BLK)
            kgs[at][:HD, cols] = win[take(i, j), :HD]
            kgs[at][HD:, cols] = masks[jnp.where(off > here, 2, jnp.where(off == 0, 1, 0))]

    def stage(i, at, ahead, behind):
        if ahead:
            place_keys(i + 1, 1 - at)
        if behind:
            acc[i - 1] = jnp.dot(
                ps[1 - at][...], vgs[1 - at][...], preferred_element_type=jnp.float32
            )
        if isinstance(i, int) and i == chip_blocks:
            return
        for j in range(n_slash):
            vgs[at][j * BLK : (j + 1) * BLK, :HD] = win[take(i, j), HD:]
        ps[at][...] = exponentials(qx[i], kgs[at][...], factor).astype(ps[at].dtype)

    place_keys(0, 0)
    pipelined(chip_blocks, stage)


def vertical_kernel(cfg, info, vert, slash, *refs):
    first, pair, local, group, reach, n_slash, n_vert, plane, heads = cfg
    q_refs, refs = refs[:pair], refs[pair:]
    w_refs, refs = refs[: reach + 1], refs[reach + 1 :]
    before, kv_vert, masks, refs = refs[0], refs[1], refs[2], refs[3:]
    out_refs, refs = refs[:pair], refs[pair:]
    ke, ve, qx, res, good = refs[:5]
    ps, (kg, vg, sc, pg) = refs[5:7], refs[7:]
    e = first + pl.program_id(0)
    chip, core = info[0], info[1]
    dev_rows = local * BLK
    chip_blocks = pair * local
    wide = n_vert * BLK
    step = min(2 * BLK, wide)
    factor = math.log2(math.e) / math.sqrt(HD)

    def within(i):
        return (core ^ i // local) * local + i % local if pair > 1 else i

    def hidden(i, j):
        here = chip * chip_blocks + within(i)
        found = vert[e, j] >= here
        for u in range(n_slash):
            found = found | (vert[e, j] == here - slash[e, u])
        return found

    per = heads * n_vert // plane
    row = lax.broadcasted_iota(jnp.int32, (HD, BLK), 0)
    for j in range(n_vert):
        flat = e * n_vert + j
        src = pl.multiple_of(((flat // per ^ chip % plane) * per + flat % per) * BLK, BLK)
        rows = slice(j * BLK, (j + 1) * BLK)
        ke[:HD, rows] = kv_vert[pl.ds(src, BLK), :HD]
        ve[rows, :HD] = kv_vert[pl.ds(src, BLK), HD:]
        bias = jnp.zeros((HD, BLK), jnp.float32)
        for i in range(chip_blocks):
            bias = jnp.where((row == i) & hidden(i, j), MASKED, bias)
        ke[HD:, rows] = bias.astype(ke.dtype)
    ve[:, HD:] = jnp.ones((wide, HD), ve.dtype)
    block_rows = group * BLK
    for i in range(chip_blocks):
        slot, b = divmod(i, local)
        mark = onehot_rows((BLK, HD), lambda row, i=i: i, qx.dtype)
        for g in range(group):
            rows = slice(i * block_rows + g * BLK, i * block_rows + (g + 1) * BLK)
            qx[rows, :HD] = q_refs[slot][b * BLK : (b + 1) * BLK, g * HD : (g + 1) * HD]
            qx[rows, HD:] = mark

    n_rows = ps[0].shape[0]

    def stage(t, at, behind):
        if behind:
            part = jnp.dot(ps[1 - at][...], ve[...], preferred_element_type=jnp.float32)
            for u in range(n_rows // block_rows):
                i = (t - 1) * (n_rows // block_rows) + u
                finish(i, before[i] + part[u * block_rows : (u + 1) * block_rows, :])
        if t * n_rows == qx.shape[0]:
            return
        q = qx[t * n_rows : (t + 1) * n_rows, :]
        ps[at][...] = exponentials(q, ke[...], factor).astype(ps[at].dtype)

    def finish(i, acc):
        total = acc[:, HD:]
        res[i] = (acc[:, :HD] / total).astype(res.dtype)
        fine = jnp.where((total > SMALLEST) & (total < LARGEST), 1.0, 0.0)
        good[...] = jnp.minimum(good[...], jnp.min(fine, axis=0, keepdims=True))

    good[...] = jnp.ones(good.shape, good.dtype)
    for t in range(qx.shape[0] // n_rows + 1):
        stage(t, t % 2, t > 0)

    @pl.when(jnp.logical_not(jnp.min(good[...]) > 0.5))
    def _():
        vg[: n_slash * BLK, HD:] = jnp.ones((n_slash * BLK, HD), vg.dtype)
        kg[:, n_slash * BLK :] = ke[...]
        vg[n_slash * BLK :, :] = ve[...]
        eye = onehot_rows((BLK, HD), lambda row: row, qx.dtype)

        def shifted_block(i, carry):
            here = chip * chip_blocks + within(i)
            q_rows = pl.ds(pl.multiple_of(i * block_rows, block_rows), block_rows)
            for g in range(group):
                at = pl.ds(pl.multiple_of(i * block_rows + g * BLK, BLK), BLK)
                qx[at, HD:] = eye
            for j in range(n_slash):
                off = slash[e, j]
                pos = reach * chip_blocks + within(i) - off
                back = reach - pos // chip_blocks
                src = pos % chip_blocks
                if pair > 1:
                    src = (src // local ^ core) * local + src % local
                at = pl.ds(pl.multiple_of(src * BLK, BLK), BLK)
                found = w_refs[0][at, :]
                for d in range(1, reach + 1):
                    found = jnp.where(back == d, w_refs[d][at, :], found)
                rows = slice(j * BLK, (j + 1) * BLK)
                kg[:HD, rows] = found[:, :HD]
                vg[rows, :HD] = found[:, HD:]
                kg[HD:, rows] = masks[jnp.where(off > here, 2, jnp.where(off == 0, 1, 0))]
            for j in range(n_vert):
                rows = slice((n_slash + j) * BLK, (n_slash + j + 1) * BLK)
                kg[HD:, rows] = masks[jnp.where(hidden(i, j), 2, 0)]
            top = None
            for t in range(0, kg.shape[1], step):
                s = jnp.dot(qx[q_rows, :], kg[:, t : t + step], preferred_element_type=jnp.float32)
                sc[:, t : t + step] = s
                for u in range(0, step, HD):
                    piece = s[:, u : u + HD]
                    top = piece if top is None else jnp.maximum(top, piece)
            top = jnp.max(top, axis=1, keepdims=True)
            for t in range(0, kg.shape[1], step):
                p = jnp.exp2((sc[:, t : t + step] - top) * factor)
                pg[:, t : t + step] = p.astype(pg.dtype)
            sums = jnp.dot(pg[...], vg[...], preferred_element_type=jnp.float32)
            res[i] = (sums[:, :HD] / sums[:, HD:]).astype(res.dtype)
            return carry

        lax.fori_loop(0, chip_blocks, shifted_block, 0)

    for i in range(chip_blocks):
        slot, b = divmod(i, local)
        for g in range(group):
            out_refs[slot][b * BLK : (b + 1) * BLK, g * HD : (g + 1) * HD] = res[
                i, g * BLK : (g + 1) * BLK
            ]


class Attention:
    def __init__(self, queries, q_other, info, vert, slash, masks, heads, local, plane):
        self.pair = 1 if q_other is None else 2
        self.qs = [queries] if q_other is None else [queries, q_other]
        self.info, self.vert, self.slash, self.masks = info, vert, slash, masks
        self.heads, self.local, self.plane = heads, local, plane
        self.dev_rows = queries.shape[0]
        self.wide = queries.shape[1] // (self.pair * heads)
        self.group = self.wide // HD
        self.blocks = self.pair * local
        self.dtype = queries.dtype

    def specs(self, first, windows):
        heads, shape = self.heads, (self.dev_rows, self.wide)
        specs = [pl.BlockSpec(shape, lambda i, info, *_: (0, info[1] * heads + first + i))]
        if self.pair > 1:
            at = self.qs[1].shape[1] // self.wide - heads + first
            specs.append(pl.BlockSpec(shape, lambda i, *_: (0, at + i)))
        return specs + [pl.BlockSpec((w.shape[0], 2 * HD), lambda i, *_: (0, i)) for w in windows]

    def whole(self, a):
        return pl.BlockSpec(a.shape, lambda i, *_: (0,) * a.ndim)

    def cost(self, n, width, more):
        rows = n * self.blocks * self.group * BLK
        return pl.CostEstimate(
            flops=8 * rows * width * HD,
            bytes_accessed=rows * HD * 2 + more,
            transcendentals=rows * width,
        )

    def acc_spec(self):
        shape = (self.blocks, self.group * BLK, 2 * HD)
        return pl.BlockSpec((None, *shape), lambda i, *_: (i, 0, 0, 0))

    def over_slash(self, first, n, windows):
        n_slash = self.slash.shape[1]
        width, rows = n_slash * BLK, self.group * BLK
        shape = (n, self.blocks, rows, 2 * HD)
        cfg = (first, self.pair, self.local, self.group, len(windows) - 1, n_slash)
        return pl.pallas_call(
            functools.partial(slash_kernel, cfg),
            grid_spec=pltpu.PrefetchScalarGridSpec(
                num_scalar_prefetch=2,
                grid=(n,),
                in_specs=self.specs(first, windows) + [self.whole(self.masks)],
                out_specs=self.acc_spec(),
                scratch_shapes=[
                    pltpu.VMEM((sum(w.shape[0] for w in windows), 2 * HD), self.dtype),
                    pltpu.VMEM((self.blocks, rows, 2 * HD), self.dtype),
                ]
                + [pltpu.VMEM((2 * HD, width), self.dtype)] * 2
                + [pltpu.VMEM((width, 2 * HD), self.dtype)] * 2
                + [pltpu.VMEM((rows, width), self.dtype)] * 2,
            ),
            out_shape=jax.ShapeDtypeStruct(shape, jnp.float32),
            compiler_params=pltpu.CompilerParams(vmem_limit_bytes=VMEM_LIMIT),
            cost_estimate=self.cost(n, width, 4 * math.prod(shape)),
            name="attend_slash",
        )(self.info, self.slash, *self.qs, *windows, self.masks)

    def over_vertical(self, first, n, windows, before, kv_vert):
        n_slash, n_vert = self.slash.shape[1], self.vert.shape[1]
        width, both, rows = n_vert * BLK, (n_slash + n_vert) * BLK, self.group * BLK
        cfg = (first, self.pair, self.local, self.group, len(windows) - 1, n_slash, n_vert)
        out = pl.BlockSpec((self.dev_rows, self.wide), lambda i, *_: (0, i))
        return pl.pallas_call(
            functools.partial(vertical_kernel, cfg + (self.plane, self.heads)),
            grid_spec=pltpu.PrefetchScalarGridSpec(
                num_scalar_prefetch=3,
                grid=(n,),
                in_specs=self.specs(first, windows)
                + [self.acc_spec(), self.whole(kv_vert), self.whole(self.masks)],
                out_specs=[out] * self.pair,
                scratch_shapes=[
                    pltpu.VMEM((2 * HD, width), self.dtype),
                    pltpu.VMEM((width, 2 * HD), self.dtype),
                    pltpu.VMEM((self.blocks * rows, 2 * HD), self.dtype),
                    pltpu.VMEM((self.blocks, rows, HD), self.dtype),
                    pltpu.VMEM((1, HD), jnp.float32),
                    pltpu.VMEM((self.blocks // 2 * rows, width), self.dtype),
                    pltpu.VMEM((self.blocks // 2 * rows, width), self.dtype),
                    pltpu.VMEM((2 * HD, both), self.dtype),
                    pltpu.VMEM((both, 2 * HD), self.dtype),
                    pltpu.VMEM((rows, both), jnp.float32),
                    pltpu.VMEM((rows, both), self.dtype),
                ],
            ),
            out_shape=[jax.ShapeDtypeStruct((self.dev_rows, n * self.wide), self.dtype)]
            * self.pair,
            compiler_params=pltpu.CompilerParams(vmem_limit_bytes=VMEM_LIMIT),
            cost_estimate=self.cost(n, width, 4 * math.prod(before.shape)),
            name="attend_vertical",
        )(self.info, self.vert, self.slash, *self.qs, *windows, before, kv_vert, self.masks)


def body(queries, keys, values, vertical_blocks, slash_offsets, out_weight):
    tokens_dev = queries.shape[0]
    kv_heads = keys.shape[1] // HD
    local = tokens_dev // BLK
    size = lax.axis_size("ctx")
    pair = 2 if kv_heads % 2 == 0 and size % 2 == 0 and lax.axis_size("head") == 1 else 1
    chips = size // pair
    heads = kv_heads // pair
    plane = PLANE if chips % PLANE == 0 and heads * vertical_blocks.shape[1] % PLANE == 0 else 1
    chip_blocks = pair * local
    reach = -(-MAXOFF // chip_blocks)
    index = lax.axis_index("ctx")
    chip, core = index // pair, index % pair
    info = jnp.stack([chip, core]).astype(jnp.int32)
    pos = jnp.arange(BLK)
    causal = jnp.where(pos[:, None] < pos[None, :], MASKED, 0.0)
    masks = jnp.stack([jnp.zeros_like(causal), causal, jnp.full_like(causal, MASKED)])
    masks = masks.astype(queries.dtype)

    def part(value, axis, which):
        span = value.shape[axis] // pair
        return lax.dynamic_slice_in_dim(value, which * span, span, axis)

    vert, slash = part(vertical_blocks, 0, core), part(slash_offsets, 0, core)
    kv_other = None
    if pair == 2:
        kv_other = crossed(jnp.concatenate([part(a, 1, 1 - core) for a in (keys, values)], 1), 1)
    per_chunk = 2 if heads % 2 == 0 else 1
    own, listed = prepare(info, vert, keys, values, kv_other, heads, local, plane, per_chunk)

    total = listed[0]
    for k in range(1, plane):
        total = total + crossed(listed[k], k * pair)
    q_other = None
    if pair == 2:
        q_other = crossed(after(part(queries, 1, 1 - core), own[0]), 1)
        total = after(total, q_other)
    steps = [2**n for n in reversed(range((chips // plane - 1).bit_length()))]
    two_back = [None] * len(own)
    passes_on = pair == 2 and reach == 2 and plane == 4
    if passes_on:
        upper = chip % plane >= 2
        stride = plane * pair

        def sent_on(value, half):
            pairs = [(i, i + stride) for i in range(size - stride) if i // pair % plane // 2 == half]
            return lax.ppermute(value, "ctx", pairs)

        risen = sent_on(own[0], 1)
        two_back[0] = crossed(after(jnp.where(upper, risen, own[0]), total), 2 * pair)
        first_step = total + shifted(total, steps[0] * stride) if steps else total
        met = two_back[0]
        for c in range(1, len(own)):
            met = crossed(after(own[c], met), 2 * pair)
            two_back[c] = jnp.where(upper, met, sent_on(met, 0))
    for n in steps:
        total = total + shifted(total, n * plane * pair)

    attention = Attention(queries, q_other, info, vert, slash, masks, heads, local, plane)
    chunks = heads // per_chunk
    all_windows, sums = [], []
    for c in range(chunks):
        windows = [own[c]]
        if passes_on:
            passed = jnp.where(chip % 2 == 0, own[c], two_back[c])
            if c == 0:
                passed = after(passed, first_step)
            one_back = crossed(passed, pair)
            if c == 0:
                one_back = after(one_back, met)
            windows += [one_back, two_back[c]]
        else:
            windows += [shifted(own[c], pair * d) for d in range(1, reach + 1)]
        all_windows.append(windows)
        sums.append(attention.over_slash(c * per_chunk, per_chunk, windows))
    gathered = [total] + [crossed(total, k * pair) for k in range(1, plane)]
    gathered = after(gathered, (sums[0], two_back[1:]))
    kv_vert = jnp.concatenate(gathered, 0)
    near, far = [], []
    for c in range(chunks):
        att = attention.over_vertical(c * per_chunk, per_chunk, all_windows[c], sums[c], kv_vert)
        near.append(att[0])
        if pair == 2:
            far.append(crossed(att[1], 1))
    attended = near
    if pair == 2:
        attended = [jnp.where(core == 0, a, b) for a, b in zip(near, far)]
        attended += [jnp.where(core == 0, b, a) for a, b in zip(near, far)]
    attended = lax.all_gather(jnp.concatenate(attended, 1), "head", axis=1, tiled=True)
    output = jnp.dot(attended, out_weight, preferred_element_type=jnp.float32)
    return output.astype(jnp.bfloat16)


def solution(mesh):
    placed = (
        P("ctx", "head"),
        P("ctx", "head"),
        P("ctx", "head"),
        P("head", None),
        P("head", None),
        P(None, "head"),
    )
    return jax.shard_map(
        body, mesh=mesh, in_specs=placed, out_specs=P("ctx", "head"), check_vma=False
    )
```

```python
import functools
import math

import jax
import jax.numpy as jnp
from jax import lax
from jax.experimental import pallas as pl
from jax.experimental.pallas import tpu as pltpu
from jax.sharding import PartitionSpec as P

HD = 128
BLK = 128
MAXOFF = 16
PLANE = 4
MASKED = -1e30
SMALLEST, LARGEST = 2.0**-60, 2.0**100
VMEM_LIMIT = 56 * 1024 * 1024


def shifted(value, by):
    size = lax.axis_size("ctx")
    return lax.ppermute(value, "ctx", [(i, i + by) for i in range(size - by)])


def crossed(value, bits):
    size = lax.axis_size("ctx")
    return lax.ppermute(value, "ctx", [(i, i ^ bits) for i in range(size)])


def after(value, other):
    return lax.optimization_barrier((value, other))[0]


def prepare_kernel(cfg, info, vert, *refs):
    pair, local, heads, plane, per_chunk = cfg
    chip, core = info[0], info[1]
    keys, values = refs[:2]
    refs = refs[2:]
    other = None
    if pair > 1:
        other, refs = refs[0], refs[1:]
    n_chunks = heads // per_chunk
    chip_outs, refs = refs[:n_chunks], refs[n_chunks:]
    list_outs, chip_kv = refs[:plane], refs[plane]
    n_vert = vert.shape[1]
    dev_rows = local * BLK
    chip_blocks = pair * local
    for e in range(heads):
        at = pl.multiple_of((core * heads + e) * HD, HD)
        chip_kv[e, :dev_rows, HD:] = values[:, pl.ds(at, HD)]
        if pair > 1:
            chip_kv[e, dev_rows:, HD:] = other[:, (heads + e) * HD : (heads + e + 1) * HD]
        for b in range(pair * local):
            rows = slice(b % local * BLK, (b % local + 1) * BLK)
            block = keys[rows, pl.ds(at, HD)] if b < local else other[rows, e * HD : (e + 1) * HD]
            chip_kv[e, b * BLK : (b + 1) * BLK, :HD] = block.T
        c, at = divmod(e, per_chunk)
        chip_outs[c][:, at * 2 * HD : (at + 1) * 2 * HD] = chip_kv[e]
    per = heads * n_vert // plane
    for k in range(plane):
        for i in range(per):
            flat = (chip % plane ^ k) * per + i
            e, j = flat // n_vert, flat % n_vert
            block = vert[e, j]
            within = block % chip_blocks
            if pair > 1:
                within = (within // local ^ core) * local + within % local
            rows = slice(i * BLK, (i + 1) * BLK)
            owned = block // chip_blocks == chip
            found = chip_kv[e, pl.ds(pl.multiple_of(within * BLK, BLK), BLK), :]
            list_outs[k][rows, :] = jnp.where(owned, found, jnp.zeros_like(found))


def prepare(info, vert, keys, values, other, heads, local, plane, per_chunk):
    pair = 1 if other is None else 2
    chip_rows = pair * local * BLK
    n_chunks = heads // per_chunk
    per = heads * vert.shape[1] // plane
    dtype = keys.dtype
    smem = pl.BlockSpec(memory_space=pltpu.SMEM)
    vmem = pl.BlockSpec(memory_space=pltpu.VMEM)
    data = [keys, values] + ([] if other is None else [other])
    specs = [vmem] * 2
    if other is not None:
        specs.append(pl.BlockSpec((other.shape[0], heads * 2 * HD), lambda i: (0, 0)))
    outs = pl.pallas_call(
        functools.partial(prepare_kernel, (pair, local, heads, plane, per_chunk)),
        grid=(1,),
        in_specs=[smem] * 2 + specs,
        out_specs=[vmem] * (n_chunks + plane),
        out_shape=[jax.ShapeDtypeStruct((chip_rows, per_chunk * 2 * HD), dtype)] * n_chunks
        + [jax.ShapeDtypeStruct((per * BLK, 2 * HD), dtype)] * plane,
        scratch_shapes=[pltpu.VMEM((heads, chip_rows, 2 * HD), dtype)],
        compiler_params=pltpu.CompilerParams(vmem_limit_bytes=VMEM_LIMIT),
        cost_estimate=pl.CostEstimate(
            flops=0, bytes_accessed=8 * heads * chip_rows * 2 * HD, transcendentals=0
        ),
        name="prepare",
    )(info, vert, *data)
    return list(outs[:n_chunks]), list(outs[n_chunks:])


def onehot_rows(shape, at, dtype):
    row = lax.broadcasted_iota(jnp.int32, shape, 0)
    col = lax.broadcasted_iota(jnp.int32, shape, 1)
    return jnp.where(col == at(row), 1.0, 0.0).astype(dtype)


def exponentials(q, k, factor):
    return jnp.exp2(jnp.dot(q, k, preferred_element_type=jnp.float32) * factor)


def pipelined(blocks, stage):
    stage(0, 0, blocks > 1, False)

    def two_blocks(n, carry):
        stage(2 * n + 1, 1, True, True)
        stage(2 * n + 2, 0, True, True)
        return carry

    inner = max(blocks - 2, 0) // 2
    lax.fori_loop(0, inner, two_blocks, 0)
    for i in range(2 * inner + 1, blocks):
        stage(i, i % 2, i + 1 < blocks, True)
    stage(blocks, blocks % 2, False, True)


def slash_kernel(cfg, info, slash, *refs):
    first, pair, local, group, reach, n_slash = cfg
    q_refs, refs = refs[:pair], refs[pair:]
    w_refs, refs = refs[: reach + 1], refs[reach + 1 :]
    masks, acc, sums, win, qx = refs[:5]
    kgs, vgs, ps = refs[5:7], refs[7:9], refs[9:11]
    lane = lax.broadcasted_iota(jnp.int32, sums.shape, 1)
    e = first + pl.program_id(0)
    chip, core = info[0], info[1]
    dev_rows = local * BLK
    chip_blocks = pair * local
    chip_rows = chip_blocks * BLK
    width = n_slash * BLK
    factor = math.log2(math.e) / math.sqrt(HD)

    for back in range(reach + 1):
        for slot in range(pair):
            owner = core ^ slot if pair > 1 else 0
            at = pl.multiple_of((reach - back) * chip_rows + owner * dev_rows, dev_rows)
            rows = slice(slot * dev_rows, (slot + 1) * dev_rows)
            win[pl.ds(at, dev_rows), :] = w_refs[back][rows, :]
    for vg in vgs:
        vg[:, HD:] = jnp.ones((width, HD), vg.dtype)
    eye = onehot_rows((BLK, HD), lambda row: row, qx.dtype)
    for i in range(chip_blocks):
        slot, b = divmod(i, local)
        for g in range(group):
            rows = slice(g * BLK, (g + 1) * BLK)
            qx[i, rows, :HD] = q_refs[slot][b * BLK : (b + 1) * BLK, g * HD : (g + 1) * HD]
            qx[i, rows, HD:] = eye

    def within(i):
        return (core ^ i // local) * local + i % local if pair > 1 else i

    def take(i, j):
        src = (reach * chip_blocks + within(i) - slash[e, j]) * BLK
        return pl.ds(pl.multiple_of(src, BLK), BLK)

    def place_keys(i, at):
        here = chip * chip_blocks + within(i)
        for j in range(n_slash):
            off = slash[e, j]
            cols = slice(j * BLK, (j + 1) * BLK)
            kgs[at][:HD, cols] = win[take(i, j), :HD]
            kgs[at][HD:, cols] = masks[jnp.where(off > here, 2, jnp.where(off == 0, 1, 0))]

    def stage(i, at, ahead, behind):
        if ahead:
            place_keys(i + 1, 1 - at)
        if behind:
            part = jnp.dot(ps[1 - at][...], vgs[1 - at][...], preferred_element_type=jnp.float32)
            acc[i - 1] = part[:, :HD]
            sums[...] = jnp.where(lane == i - 1, part[:, HD:], sums[...])
        if isinstance(i, int) and i == chip_blocks:
            return
        for j in range(n_slash):
            vgs[at][j * BLK : (j + 1) * BLK, :HD] = win[take(i, j), HD:]
        ps[at][...] = exponentials(qx[i], kgs[at][...], factor).astype(ps[at].dtype)

    sums[...] = jnp.zeros(sums.shape, sums.dtype)
    place_keys(0, 0)
    pipelined(chip_blocks, stage)


def vertical_kernel(cfg, info, vert, slash, *refs):
    first, pair, local, group, reach, n_slash, n_vert, plane, heads = cfg
    q_refs, refs = refs[:pair], refs[pair:]
    w_refs, refs = refs[: reach + 1], refs[reach + 1 :]
    before, sums, kv_vert, masks, refs = refs[0], refs[1], refs[2], refs[3], refs[4:]
    lane = lax.broadcasted_iota(jnp.int32, sums.shape, 1)
    out_refs, refs = refs[:pair], refs[pair:]
    ke, ve, qx, res, good = refs[:5]
    ps, (kg, vg, sc, pg) = refs[5:7], refs[7:]
    e = first + pl.program_id(0)
    chip, core = info[0], info[1]
    dev_rows = local * BLK
    chip_blocks = pair * local
    wide = n_vert * BLK
    step = min(2 * BLK, wide)
    factor = math.log2(math.e) / math.sqrt(HD)

    def within(i):
        return (core ^ i // local) * local + i % local if pair > 1 else i

    def hidden(i, j):
        here = chip * chip_blocks + within(i)
        found = vert[e, j] >= here
        for u in range(n_slash):
            found = found | (vert[e, j] == here - slash[e, u])
        return found

    per = heads * n_vert // plane
    row = lax.broadcasted_iota(jnp.int32, (HD, BLK), 0)
    for j in range(n_vert):
        flat = e * n_vert + j
        src = j * BLK
        if heads != plane:
            src = pl.multiple_of(((flat // per ^ chip % plane) * per + flat % per) * BLK, BLK)
        rows = slice(j * BLK, (j + 1) * BLK)
        ke[:HD, rows] = kv_vert[pl.ds(src, BLK), :HD]
        ve[rows, :HD] = kv_vert[pl.ds(src, BLK), HD:]
        bias = jnp.zeros((HD, BLK), jnp.float32)
        for i in range(chip_blocks):
            bias = jnp.where((row == i) & hidden(i, j), MASKED, bias)
        ke[HD:, rows] = bias.astype(ke.dtype)
    ve[:, HD:] = jnp.ones((wide, HD), ve.dtype)
    block_rows = group * BLK
    for i in range(chip_blocks):
        slot, b = divmod(i, local)
        mark = onehot_rows((BLK, HD), lambda row, i=i: i, qx.dtype)
        for g in range(group):
            rows = slice(i * block_rows + g * BLK, i * block_rows + (g + 1) * BLK)
            qx[rows, :HD] = q_refs[slot][b * BLK : (b + 1) * BLK, g * HD : (g + 1) * HD]
            qx[rows, HD:] = mark

    n_rows = ps[0].shape[0]

    def stage(t, at, behind):
        if behind:
            part = jnp.dot(ps[1 - at][...], ve[...], preferred_element_type=jnp.float32)
            for u in range(n_rows // block_rows):
                i = (t - 1) * (n_rows // block_rows) + u
                finish(i, part[u * block_rows : (u + 1) * block_rows, :])
        if t * n_rows == qx.shape[0]:
            return
        q = qx[t * n_rows : (t + 1) * n_rows, :]
        ps[at][...] = exponentials(q, ke[...], factor).astype(ps[at].dtype)

    def finish(i, acc):
        mine = jnp.sum(jnp.where(lane == i, sums[...], 0.0), axis=1, keepdims=True)
        total = acc[:, HD:] + mine
        res[i] = ((acc[:, :HD] + before[i]) / total).astype(res.dtype)
        fine = jnp.where((total > SMALLEST) & (total < LARGEST), 1.0, 0.0)
        good[...] = jnp.minimum(good[...], jnp.min(fine, axis=0, keepdims=True))

    good[...] = jnp.ones(good.shape, good.dtype)
    for t in range(qx.shape[0] // n_rows + 1):
        stage(t, t % 2, t > 0)

    @pl.when(jnp.logical_not(jnp.min(good[...]) > 0.5))
    def _():
        vg[: n_slash * BLK, HD:] = jnp.ones((n_slash * BLK, HD), vg.dtype)
        kg[:, n_slash * BLK :] = ke[...]
        vg[n_slash * BLK :, :] = ve[...]
        eye = onehot_rows((BLK, HD), lambda row: row, qx.dtype)

        def shifted_block(i, carry):
            here = chip * chip_blocks + within(i)
            q_rows = pl.ds(pl.multiple_of(i * block_rows, block_rows), block_rows)
            for g in range(group):
                at = pl.ds(pl.multiple_of(i * block_rows + g * BLK, BLK), BLK)
                qx[at, HD:] = eye
            for j in range(n_slash):
                off = slash[e, j]
                pos = reach * chip_blocks + within(i) - off
                back = reach - pos // chip_blocks
                src = pos % chip_blocks
                if pair > 1:
                    src = (src // local ^ core) * local + src % local
                at = pl.ds(pl.multiple_of(src * BLK, BLK), BLK)
                found = w_refs[0][at, :]
                for d in range(1, reach + 1):
                    found = jnp.where(back == d, w_refs[d][at, :], found)
                rows = slice(j * BLK, (j + 1) * BLK)
                kg[:HD, rows] = found[:, :HD]
                vg[rows, :HD] = found[:, HD:]
                kg[HD:, rows] = masks[jnp.where(off > here, 2, jnp.where(off == 0, 1, 0))]
            for j in range(n_vert):
                rows = slice((n_slash + j) * BLK, (n_slash + j + 1) * BLK)
                kg[HD:, rows] = masks[jnp.where(hidden(i, j), 2, 0)]
            top = None
            for t in range(0, kg.shape[1], step):
                s = jnp.dot(qx[q_rows, :], kg[:, t : t + step], preferred_element_type=jnp.float32)
                sc[:, t : t + step] = s
                for u in range(0, step, HD):
                    piece = s[:, u : u + HD]
                    top = piece if top is None else jnp.maximum(top, piece)
            top = jnp.max(top, axis=1, keepdims=True)
            for t in range(0, kg.shape[1], step):
                p = jnp.exp2((sc[:, t : t + step] - top) * factor)
                pg[:, t : t + step] = p.astype(pg.dtype)
            sums = jnp.dot(pg[...], vg[...], preferred_element_type=jnp.float32)
            res[i] = (sums[:, :HD] / sums[:, HD:]).astype(res.dtype)
            return carry

        lax.fori_loop(0, chip_blocks, shifted_block, 0)

    for i in range(chip_blocks):
        slot, b = divmod(i, local)
        for g in range(group):
            out_refs[slot][b * BLK : (b + 1) * BLK, g * HD : (g + 1) * HD] = res[
                i, g * BLK : (g + 1) * BLK
            ]


class Attention:
    def __init__(self, queries, q_other, info, vert, slash, masks, heads, local, plane):
        self.pair = 1 if q_other is None else 2
        self.qs = [queries] if q_other is None else [queries, q_other]
        self.info, self.vert, self.slash, self.masks = info, vert, slash, masks
        self.heads, self.local, self.plane = heads, local, plane
        self.dev_rows = queries.shape[0]
        self.wide = queries.shape[1] // (self.pair * heads)
        self.group = self.wide // HD
        self.blocks = self.pair * local
        self.dtype = queries.dtype

    def specs(self, first, windows):
        heads, shape = self.heads, (self.dev_rows, self.wide)
        specs = [pl.BlockSpec(shape, lambda i, info, *_: (0, info[1] * heads + first + i))]
        if self.pair > 1:
            at = self.qs[1].shape[1] // self.wide - heads + first
            specs.append(pl.BlockSpec(shape, lambda i, *_: (0, at + i)))
        return specs + [pl.BlockSpec((w.shape[0], 2 * HD), lambda i, *_: (0, i)) for w in windows]

    def whole(self, a):
        return pl.BlockSpec(a.shape, lambda i, *_: (0,) * a.ndim)

    def cost(self, n, width, more):
        rows = n * self.blocks * self.group * BLK
        return pl.CostEstimate(
            flops=8 * rows * width * HD,
            bytes_accessed=rows * HD * 2 + more,
            transcendentals=rows * width,
        )

    def acc_spec(self):
        rows = self.group * BLK
        return [
            pl.BlockSpec((None, self.blocks, rows, HD), lambda i, *_: (i, 0, 0, 0)),
            pl.BlockSpec((None, rows, HD), lambda i, *_: (i, 0, 0)),
        ]

    def over_slash(self, first, n, windows):
        n_slash = self.slash.shape[1]
        width, rows = n_slash * BLK, self.group * BLK
        shape = (n, self.blocks, rows, HD)
        cfg = (first, self.pair, self.local, self.group, len(windows) - 1, n_slash)
        return pl.pallas_call(
            functools.partial(slash_kernel, cfg),
            grid_spec=pltpu.PrefetchScalarGridSpec(
                num_scalar_prefetch=2,
                grid=(n,),
                in_specs=self.specs(first, windows) + [self.whole(self.masks)],
                out_specs=self.acc_spec(),
                scratch_shapes=[
                    pltpu.VMEM((sum(w.shape[0] for w in windows), 2 * HD), self.dtype),
                    pltpu.VMEM((self.blocks, rows, 2 * HD), self.dtype),
                ]
                + [pltpu.VMEM((2 * HD, width), self.dtype)] * 2
                + [pltpu.VMEM((width, 2 * HD), self.dtype)] * 2
                + [pltpu.VMEM((rows, width), self.dtype)] * 2,
            ),
            out_shape=[
                jax.ShapeDtypeStruct(shape, jnp.float32),
                jax.ShapeDtypeStruct((n, rows, HD), jnp.float32),
            ],
            compiler_params=pltpu.CompilerParams(vmem_limit_bytes=VMEM_LIMIT),
            cost_estimate=self.cost(n, width, 4 * math.prod(shape)),
            name="attend_slash",
        )(self.info, self.slash, *self.qs, *windows, self.masks)

    def over_vertical(self, first, n, windows, before, kv_vert):
        n_slash, n_vert = self.slash.shape[1], self.vert.shape[1]
        width, both, rows = n_vert * BLK, (n_slash + n_vert) * BLK, self.group * BLK
        cfg = (first, self.pair, self.local, self.group, len(windows) - 1, n_slash, n_vert)
        out = pl.BlockSpec((self.dev_rows, self.wide), lambda i, *_: (0, i))
        kv_spec, plane = self.whole(kv_vert), self.plane
        if self.heads == plane:
            kv_spec = pl.BlockSpec(
                (width, 2 * HD), lambda i, info, *_: ((first + i) ^ info[0] % plane, 0)
            )
        return pl.pallas_call(
            functools.partial(vertical_kernel, cfg + (self.plane, self.heads)),
            grid_spec=pltpu.PrefetchScalarGridSpec(
                num_scalar_prefetch=3,
                grid=(n,),
                in_specs=self.specs(first, windows)
                + self.acc_spec()
                + [kv_spec, self.whole(self.masks)],
                out_specs=[out] * self.pair,
                scratch_shapes=[
                    pltpu.VMEM((2 * HD, width), self.dtype),
                    pltpu.VMEM((width, 2 * HD), self.dtype),
                    pltpu.VMEM((self.blocks * rows, 2 * HD), self.dtype),
                    pltpu.VMEM((self.blocks, rows, HD), self.dtype),
                    pltpu.VMEM((1, HD), jnp.float32),
                    pltpu.VMEM((self.blocks // 2 * rows, width), self.dtype),
                    pltpu.VMEM((self.blocks // 2 * rows, width), self.dtype),
                    pltpu.VMEM((2 * HD, both), self.dtype),
                    pltpu.VMEM((both, 2 * HD), self.dtype),
                    pltpu.VMEM((rows, both), jnp.float32),
                    pltpu.VMEM((rows, both), self.dtype),
                ],
            ),
            out_shape=[jax.ShapeDtypeStruct((self.dev_rows, n * self.wide), self.dtype)]
            * self.pair,
            compiler_params=pltpu.CompilerParams(vmem_limit_bytes=VMEM_LIMIT),
            cost_estimate=self.cost(n, width, 4 * math.prod(before[0].shape)),
            name="attend_vertical",
        )(self.info, self.vert, self.slash, *self.qs, *windows, *before, kv_vert, self.masks)


def body(queries, keys, values, vertical_blocks, slash_offsets, out_weight):
    tokens_dev = queries.shape[0]
    kv_heads = keys.shape[1] // HD
    local = tokens_dev // BLK
    size = lax.axis_size("ctx")
    pair = 2 if kv_heads % 2 == 0 and size % 2 == 0 and lax.axis_size("head") == 1 else 1
    chips = size // pair
    heads = kv_heads // pair
    plane = PLANE if chips % PLANE == 0 and heads * vertical_blocks.shape[1] % PLANE == 0 else 1
    chip_blocks = pair * local
    reach = -(-MAXOFF // chip_blocks)
    index = lax.axis_index("ctx")
    chip, core = index // pair, index % pair
    info = jnp.stack([chip, core]).astype(jnp.int32)
    pos = jnp.arange(BLK)
    causal = jnp.where(pos[:, None] < pos[None, :], MASKED, 0.0)
    masks = jnp.stack([jnp.zeros_like(causal), causal, jnp.full_like(causal, MASKED)])
    masks = masks.astype(queries.dtype)

    def part(value, axis, which):
        span = value.shape[axis] // pair
        return lax.dynamic_slice_in_dim(value, which * span, span, axis)

    vert, slash = part(vertical_blocks, 0, core), part(slash_offsets, 0, core)
    kv_other = None
    if pair == 2:
        kv_other = crossed(jnp.concatenate([part(a, 1, 1 - core) for a in (keys, values)], 1), 1)
    per_chunk = 2 if heads % 2 == 0 else 1
    own, listed = prepare(info, vert, keys, values, kv_other, heads, local, plane, per_chunk)

    total = listed[0]
    for k in range(1, plane):
        total = total + crossed(listed[k], k * pair)
    q_other = None
    if pair == 2:
        q_other = crossed(after(part(queries, 1, 1 - core), own[0]), 1)
        total = after(total, q_other)
    two_back = [None] * len(own)
    passes_on = pair == 2 and reach == 2 and plane == 4
    if passes_on:
        upper = chip % plane >= 2
        stride = plane * pair

        def sent_on(value, half):
            pairs = [(i, i + stride) for i in range(size - stride) if i // pair % plane // 2 == half]
            return lax.ppermute(value, "ctx", pairs)

        risen = sent_on(own[0], 1)
        two_back[0] = crossed(after(jnp.where(upper, risen, own[0]), total), 2 * pair)
        met = (two_back[0], total + shifted(total, stride))
        for c in range(1, len(own)):
            met = crossed(after(own[c], met), 2 * pair)
            two_back[c] = jnp.where(upper, met, sent_on(met, 0))
    step = 1
    while step < chips // plane:
        total = total + shifted(total, step * plane * pair)
        step *= 2

    attention = Attention(queries, q_other, info, vert, slash, masks, heads, local, plane)
    chunks = heads // per_chunk
    all_windows, sums = [], []
    for c in range(chunks):
        windows = [own[c]]
        if passes_on:
            passed = jnp.where(chip % 2 == 0, own[c], two_back[c])
            one_back = crossed(passed, pair)
            if c == 0:
                one_back = after(one_back, met)
            windows += [one_back, two_back[c]]
        else:
            windows += [shifted(own[c], pair * d) for d in range(1, reach + 1)]
        all_windows.append(windows)
        sums.append(attention.over_slash(c * per_chunk, per_chunk, windows))
    gathered = [total] + [crossed(total, k * pair) for k in range(1, plane)]
    gathered = after(gathered, (sums[0], two_back[1:]))
    kv_vert = jnp.concatenate(gathered, 0)
    near, far = [], []
    for c in range(chunks):
        att = attention.over_vertical(c * per_chunk, per_chunk, all_windows[c], sums[c], kv_vert)
        near.append(att[0])
        if pair == 2:
            far.append(crossed(att[1], 1))
    attended = near
    if pair == 2:
        attended = [jnp.where(core == 0, a, b) for a, b in zip(near, far)]
        attended += [jnp.where(core == 0, b, a) for a, b in zip(near, far)]
    attended = lax.all_gather(jnp.concatenate(attended, 1), "head", axis=1, tiled=True)
    output = jnp.dot(attended, out_weight, preferred_element_type=jnp.float32)
    return output.astype(jnp.bfloat16)


def solution(mesh):
    placed = (
        P("ctx", "head"),
        P("ctx", "head"),
        P("ctx", "head"),
        P("head", None),
        P("head", None),
        P(None, "head"),
    )
    return jax.shard_map(
        body, mesh=mesh, in_specs=placed, out_specs=P("ctx", "head"), check_vma=False
    )
```
